256 devices in a mesh: res: 64 (over y, z, x_hi), seq: 4 (over x_lo, core).
Axes of the slice: x: 4 (x_hi: 2, x_lo: 2; x = x_hi * 2 + x_lo), y: 4, z: 8, core: 2. Of those that a mesh axis runs over, the one named last changes fastest.
Arguments:
- alignment_token_classes: int32 [256, 512], P('seq', 'res'), may hold values from 0 to 22
- deletions: int32 [256, 512], P('seq', 'res'), may hold values from 0 to 31
- alignment_mask: int32 [256, 512], P('seq', 'res'), may hold values from 0 to 1, as said below
- homolog_stack_values: bfloat16 [256, 512, 256], P('seq', 'res'), may hold values from -6 to 6
- letter_lookup_coefficients: float32 [23, 256], replicated, may hold values from -6 to 6
- gap_lookup_coefficients: float32 [2, 256], replicated, may hold values from -6 to 6
- standardize_gain: float32 [256], replicated, may hold values from 0.1 to 1.9
- standardize_offset: float32 [256], replicated, may hold values from -3 to 3
- first_factor_map: bfloat16 [256, 32], replicated, may hold values from -0.375 to 0.375
- left_bias_vector: float32 [32], replicated, may hold values from -4 to 4
- second_factor_map: bfloat16 [256, 32], replicated, may hold values from -0.375 to 0.375
- right_bias_vector: float32 [32], replicated, may hold values from -4 to 4
- output_weight_matrix: bfloat16 [1024, 128], replicated, may hold values from -1.5 to 1.5
- cotangent: bfloat16 [512, 512, 128], P('res'), may hold values from -0.08984375 to 0.08984375
Outputs:
- pair_update: bfloat16 [512, 512, 128], P('res', 'seq')
- grad_out_weight: float32 [1024, 128], replicated
- embedding_gradient: float32 [23, 256], replicated
The draws below stay inside these ranges and needn't reach their ends.
Inputs may be any that keep to these rules, and one draw needn't show every extreme that they name: Row 0 of alignment_mask is 1 at every residue; the other entries are 0 or 1.
All inputs are finite; a program needn't handle non-finite values.
Results may differ from the reference program's by a relative error of at most 0.0057.
Values may be sent and summed in bfloat16 or wider, within the bound.
A program may use at most 128 MiB of HBM per device.

```python
import math
import jax
import jax.numpy as jnp
import numpy as np
from jax import lax

ALIGNED_FEATURE = 256
FACTOR_WIDTH = 32
CZ = 128
LETTER_KINDS = 23
AMINO_TOTAL = 512
HOMOLOG_TOTAL = 256


def draw_alignment_mask(key, part):
    key = jax.random.fold_in(key, 7)
    random_bits = jax.random.randint(key, (HOMOLOG_TOTAL, AMINO_TOTAL), 0, 2, dtype=jnp.int32)
    row_number = lax.broadcasted_iota(jnp.int32, (HOMOLOG_TOTAL, AMINO_TOTAL), 0)
    return jnp.where(row_number == 0, 1, random_bits).astype(jnp.int32)


def plant(entries, own_key, smallest, largest):
    shape = entries.shape
    place = [jax.random.randint(jax.random.fold_in(own_key, axis), (), 0, shape[axis]) for axis in range(len(shape))]
    entries = entries.at[tuple(place)].set(smallest)
    longest = shape.index(max(shape))
    place[longest] = (place[longest] + 1) % shape[longest]
    return entries.at[tuple(place)].set(largest)


def steps_of(own_key, extent, cuts, smallest, largest):
    factor_of = 1.0
    for dim, parts in cuts:
        draws = jax.random.uniform(jax.random.fold_in(jax.random.fold_in(own_key, 6), dim), (parts,), jnp.float32, smallest / len(cuts), largest / len(cuts))
        factor_of = factor_of * jnp.repeat(jnp.exp(draws), extent[dim] // parts).reshape((-1,) + (1,) * (len(extent) - 1 - dim))
    return factor_of


def cumulative_ranks(count, skew):
    weights = [(1 << 20) // math.isqrt(grade ** skew) + 1 for grade in range(1, count + 1)]
    width = 1 + sum(weights) // (1 << 30)
    return np.cumsum(np.array([max(1, weight // width) for weight in weights]))


def skewed_ids(key, extent, count, skew):
    grid = cumulative_ranks(count, skew)
    lot = jax.random.randint(jax.random.fold_in(key, 1), extent, 0, int(grid[count - 1]))
    grade = jnp.searchsorted(jnp.asarray(grid, jnp.int32), lot, side="right")
    return jax.random.permutation(jax.random.fold_in(key, 2), count)[grade].astype(jnp.int32)


def noise(own_key, dims, scale, most, shards=(), held_as=jnp.bfloat16):
    drawn = jax.random.normal(own_key, dims, jnp.float32) * scale
    if len(shards) > 0:
        drawn = steps_of(own_key, dims, shards, -0.22, 0.18) * drawn
    return jnp.clip(drawn, min=-most, max=most).astype(held_as)


def setup_inputs(seed: int = 0) -> dict:
    streams_of = jax.random.split(jax.random.key(seed), 15)
    alignment_token_classes = plant(jax.random.randint(streams_of[0], (HOMOLOG_TOTAL, AMINO_TOTAL), 0, LETTER_KINDS), jax.random.fold_in(streams_of[0], 1), 0, LETTER_KINDS - 1).astype(jnp.int32)
    deletions = plant(skewed_ids(streams_of[1], (HOMOLOG_TOTAL, AMINO_TOTAL), 32, 2), jax.random.fold_in(streams_of[1], 3), 0, 31).astype(jnp.int32)
    alignment_mask = draw_alignment_mask(jax.random.fold_in(streams_of[14], 71), 0)
    homolog_stack_values = noise(streams_of[3], (HOMOLOG_TOTAL, AMINO_TOTAL, ALIGNED_FEATURE), 1.0, 6.0, ((0, 4), (1, 64)))
    letter_lookup_coefficients = noise(streams_of[4], (LETTER_KINDS, ALIGNED_FEATURE), 1.0, 6.0, (), jnp.float32)
    gap_lookup_coefficients = noise(streams_of[5], (2, ALIGNED_FEATURE), 1.0, 6.0, (), jnp.float32)
    standardize_gain = jnp.clip(1.0 + 0.18 * jax.random.normal(streams_of[6], (ALIGNED_FEATURE,), jnp.float32), 0.1, 1.9)
    standardize_offset = noise(streams_of[7], (ALIGNED_FEATURE,), 0.5, 3.0, (), jnp.float32)
    first_factor_map = noise(streams_of[8], (ALIGNED_FEATURE, FACTOR_WIDTH), ALIGNED_FEATURE ** -0.5, 0.375)
    left_bias_vector = noise(streams_of[9], (FACTOR_WIDTH,), 1.0, 4.0, (), jnp.float32)
    second_factor_map = noise(streams_of[10], (ALIGNED_FEATURE, FACTOR_WIDTH), ALIGNED_FEATURE ** -0.5, 0.375)
    right_bias_vector = noise(streams_of[11], (FACTOR_WIDTH,), 1.0, 4.0, (), jnp.float32)
    output_weight_matrix = noise(streams_of[12], (FACTOR_WIDTH * FACTOR_WIDTH, CZ), 16 ** -0.5, 1.5)
    cotangent = noise(streams_of[13], (AMINO_TOTAL, AMINO_TOTAL, CZ), 0.015625, 0.08984375, ((0, 64),))
    return {"alignment_token_classes": alignment_token_classes, "deletions": deletions, "alignment_mask": alignment_mask, "homolog_stack_values": homolog_stack_values, "letter_lookup_coefficients": letter_lookup_coefficients, "gap_lookup_coefficients": gap_lookup_coefficients, "standardize_gain": standardize_gain, "standardize_offset": standardize_offset, "first_factor_map": first_factor_map, "left_bias_vector": left_bias_vector, "second_factor_map": second_factor_map, "right_bias_vector": right_bias_vector, "output_weight_matrix": output_weight_matrix, "cotangent": cotangent}


EPSILON = 1e-05
TOP_PRECISION = lax.Precision.HIGHEST

def reference(alignment_token_classes, deletions, alignment_mask, homolog_stack_values, letter_lookup_coefficients, gap_lookup_coefficients, standardize_gain, standardize_offset, first_factor_map, left_bias_vector, second_factor_map, right_bias_vector, output_weight_matrix, cotangent):
    counted = deletions.astype(jnp.float32)
    marked_deletion = (deletions > 0).astype(jnp.float32)
    attenuated = 2.0 / math.pi * jnp.arctan(counted / 3.0)
    hidden_activations = homolog_stack_values.astype(jnp.float32) + letter_lookup_coefficients[alignment_token_classes] + marked_deletion[..., None] * gap_lookup_coefficients[0] + attenuated[..., None] * gap_lookup_coefficients[1]
    average = lax.optimization_barrier(jnp.mean(hidden_activations, axis=-1, keepdims=True))
    mean_removed = hidden_activations - average
    variance = lax.optimization_barrier(jnp.mean(mean_removed * mean_removed, axis=-1, keepdims=True))
    reciprocal_spread = lax.rsqrt(variance + EPSILON)
    standardized_values = (mean_removed * reciprocal_spread).reshape(HOMOLOG_TOTAL * AMINO_TOTAL, ALIGNED_FEATURE)
    normed = (standardized_values * standardize_gain + standardize_offset).astype(jnp.bfloat16)
    mask_decimal = alignment_mask.astype(jnp.float32)
    mask_column = mask_decimal.reshape(HOMOLOG_TOTAL * AMINO_TOTAL, 1)
    left_rows = (mask_column * (jnp.dot(normed, first_factor_map, preferred_element_type=jnp.float32) + left_bias_vector)).astype(jnp.bfloat16).reshape(HOMOLOG_TOTAL, AMINO_TOTAL * FACTOR_WIDTH)
    right_rows = (mask_column * (jnp.dot(normed, second_factor_map, preferred_element_type=jnp.float32) + right_bias_vector)).astype(jnp.bfloat16).reshape(HOMOLOG_TOTAL, AMINO_TOTAL * FACTOR_WIDTH)
    counts = jnp.dot(mask_decimal.T, mask_decimal, precision=TOP_PRECISION)
    scaled = (cotangent.astype(jnp.float32) / counts[:, :, None]).astype(jnp.bfloat16)
    wide_weight = output_weight_matrix.astype(jnp.float32)
    row_span = math.gcd(AMINO_TOTAL, 32)
    span_count = AMINO_TOTAL // row_span

    def step_rows(carried, position):
        grad_weight, grad_right = carried
        first_row = (position * row_span).astype(jnp.int32)
        left_part = lax.dynamic_slice_in_dim(left_rows, first_row * FACTOR_WIDTH, row_span * FACTOR_WIDTH, 1)
        outer = jnp.dot(left_part.T, right_rows, preferred_element_type=jnp.float32)
        folded = outer.reshape(row_span, FACTOR_WIDTH, AMINO_TOTAL, FACTOR_WIDTH).transpose(0, 2, 1, 3).reshape(row_span * AMINO_TOTAL, FACTOR_WIDTH * FACTOR_WIDTH)
        count_part = lax.dynamic_slice_in_dim(counts, first_row, row_span, 0)
        pair_part = (jnp.dot(folded, wide_weight, precision=TOP_PRECISION).reshape(row_span, AMINO_TOTAL, CZ) / count_part[:, :, None]).astype(jnp.bfloat16)
        grad_part = lax.dynamic_slice_in_dim(scaled, first_row, row_span, 0).reshape(row_span * AMINO_TOTAL, CZ)
        grad_weight = grad_weight + jnp.dot(folded.T, grad_part.astype(jnp.float32), precision=TOP_PRECISION)
        grad_outer = jnp.dot(grad_part, output_weight_matrix.T, preferred_element_type=jnp.float32).astype(jnp.bfloat16)
        grad_outer = grad_outer.reshape(row_span, AMINO_TOTAL, FACTOR_WIDTH, FACTOR_WIDTH).transpose(0, 2, 1, 3).reshape(row_span * FACTOR_WIDTH, AMINO_TOTAL * FACTOR_WIDTH)
        left_grad = jnp.dot(grad_outer, right_rows.T, preferred_element_type=jnp.float32)
        grad_right = grad_right + jnp.dot(left_part, grad_outer, preferred_element_type=jnp.float32)
        return ((grad_weight, grad_right), (pair_part, left_grad))
    initial = (jnp.zeros((FACTOR_WIDTH * FACTOR_WIDTH, CZ), jnp.float32), jnp.zeros((HOMOLOG_TOTAL, AMINO_TOTAL * FACTOR_WIDTH), jnp.float32))
    finals, stacked = lax.scan(step_rows, initial, jnp.arange(span_count, dtype=jnp.int32))
    grad_out_weight, grad_right = finals
    pair_blocks, left_grads = stacked
    pair_update = pair_blocks.reshape(AMINO_TOTAL, AMINO_TOTAL, CZ)
    mask_cube = mask_decimal[:, :, None]
    left_total = left_grads.reshape(AMINO_TOTAL * FACTOR_WIDTH, HOMOLOG_TOTAL).T.reshape(HOMOLOG_TOTAL, AMINO_TOTAL, FACTOR_WIDTH)
    grad_left = (mask_cube * left_total).astype(jnp.bfloat16).reshape(HOMOLOG_TOTAL * AMINO_TOTAL, FACTOR_WIDTH)
    grad_rhs = (mask_cube * grad_right.reshape(HOMOLOG_TOTAL, AMINO_TOTAL, FACTOR_WIDTH)).astype(jnp.bfloat16).reshape(HOMOLOG_TOTAL * AMINO_TOTAL, FACTOR_WIDTH)
    grad_normed = jnp.dot(grad_left, first_factor_map.T, preferred_element_type=jnp.float32) + jnp.dot(grad_rhs, second_factor_map.T, preferred_element_type=jnp.float32)
    gained = grad_normed * standardize_gain
    gradient_activations = reciprocal_spread.reshape(HOMOLOG_TOTAL * AMINO_TOTAL, 1) * (gained - lax.optimization_barrier(jnp.mean(gained, axis=-1, keepdims=True)) - standardized_values * lax.optimization_barrier(jnp.mean(gained * standardized_values, axis=-1, keepdims=True)))
    embedding_gradient = jax.ops.segment_sum(gradient_activations, alignment_token_classes.reshape(-1), num_segments=LETTER_KINDS)
    return (pair_update, grad_out_weight, embedding_gradient)
```

```python
import math

import jax
import jax.numpy as jnp
from jax import lax
from jax.experimental import pallas as pl
from jax.experimental.pallas import tpu as pltpu
from jax.sharding import PartitionSpec as P

EPSILON = 1e-05
TOP_PRECISION = lax.Precision.HIGHEST
MESH = pl.DeviceIdType.MESH
F32 = jnp.float32
BF16 = jnp.bfloat16

ROWS = 64
BLOCK = 80
WIDE = 256
TILES = 6


def place():
    res = lax.axis_index("res")
    q = lax.axis_index("seq")
    return lax.div(res, 16), lax.rem(lax.div(res, 2), 8), lax.rem(res, 2), q


def row_peer(spot, n):
    _, z, x, _ = spot
    return (lax.div(n, 4) * 16 + z * 2 + x, lax.rem(n, 4))


def depth_peer(spot, n):
    y, _, _, q = spot
    return (y * 16 + n, q)


def right_user(spot, n):
    y, z, _, _ = spot
    return (lax.div(z, 2) * 16 + n, y)


def right_owner(spot, n):
    y, _, _, q = spot
    return (q * 16 + y * 4 + lax.div(n, 4), lax.rem(n, 4))


def repeat(count, step):
    lax.fori_loop(0, count, lambda n, carried: (step(n), carried)[1], 0)


def signal(barrier, target):
    pl.semaphore_signal(barrier, inc=1, device_id=target, device_id_type=MESH)


def remote(src, dst, send, recv, target):
    return pltpu.make_async_remote_copy(
        src_ref=src, dst_ref=dst, send_sem=send, recv_sem=recv, device_id=target, device_id_type=MESH
    )


def lanes(shape):
    return lax.broadcasted_iota(jnp.int32, shape, len(shape) - 1)


def swap(parts, stride):
    lane = lanes(parts[0].shape)
    low = lax.rem(lax.div(lane, stride), 2) == 0
    high = lax.rem(lax.div(lane, 2 * stride), 2) == 0

    def pair(first, second, step, keep):
        return (
            jnp.where(keep, first, pltpu.roll(second, step, 1)),
            jnp.where(keep, pltpu.roll(first, 128 - step, 1), second),
        )

    a, b = pair(parts[0], parts[1], stride, low)
    c, d = pair(parts[2], parts[3], stride, low)
    a, c = pair(a, c, 2 * stride, high)
    b, d = pair(b, d, 2 * stride, high)
    return [a, b, c, d]


def dot(first, second):
    return jnp.dot(first, second, preferred_element_type=F32)


def dot_nt(first, second):
    return lax.dot_general(first, second, (((1,), (1,)), ((), ())), preferred_element_type=F32)


def gather_kernel(
    token, deletion, mask, mask_rows, stack, table, gain, offset, maps, bias, cotangent,
    left_all, right_all, cot_all, white, spread,
    left_own, right_own, left_send, left_recv, right_send, right_recv, cot_send, cot_recv,
):
    spot = place()
    y, z, x, q = spot
    mine = y * 4 + q
    self_user = jnp.logical_and(lax.div(z, 2) == y, q == y)
    slot = lax.rem(z, 2) * 2 + x
    my_res = y * 16 + z * 2 + x

    def is_me(target):
        return jnp.logical_and(target[0] == my_res, target[1] == q)

    barrier = pltpu.get_barrier_semaphore()

    def greet(n):
        @pl.when(n != mine)
        def _():
            signal(barrier, row_peer(spot, n))

        owner = right_owner(spot, n)

        @pl.when(jnp.logical_not(is_me(owner)))
        def _():
            signal(barrier, owner)

    repeat(16, greet)

    lane = lanes((ROWS, 128))
    wide_lane = lanes((ROWS, WIDE))
    left_tiles = [jnp.zeros((ROWS, 128), F32), jnp.zeros((ROWS, 128), F32)]
    right_part = jnp.zeros((ROWS, WIDE), F32)
    for i in range(8):
        hot = jnp.logical_or(lane == token[:, i : i + 1], lane == deletion[:, i : i + 1] + 32).astype(F32)
        hidden = stack[i].astype(F32) + jnp.dot(
            hot, table[...], precision=TOP_PRECISION, preferred_element_type=F32
        )
        centered = hidden - jnp.mean(hidden, axis=-1, keepdims=True)
        variance = jnp.mean(centered * centered, axis=-1, keepdims=True)
        scale = lax.rsqrt(variance + EPSILON)
        whitened = centered * scale
        white[i] = whitened
        spread[i] = jnp.broadcast_to(scale, (ROWS, 128))
        normed = (whitened * gain[...] + offset[...]).astype(BF16)
        rows = mask[:, i : i + 1] * (dot(normed, maps[...]) + bias[...])
        left_tiles[i // 4] = jnp.where(lax.div(lane, 32) == i % 4, rows[:, :128], left_tiles[i // 4])
        right_part = jnp.where(lax.rem(wide_lane, 8) == i, rows[:, 128:], right_part)
    left_own[:ROWS, :128] = left_tiles[0].astype(BF16)
    left_own[:ROWS, 128:] = left_tiles[1].astype(BF16)
    left_own[ROWS:, :] = mask_rows[...]
    right_own[:ROWS, :] = right_part.astype(BF16)
    right_own[ROWS:, :] = mask_rows[...]

    pl.semaphore_wait(barrier, jnp.where(self_user, 30, 31))

    def left_slot(at_y, at_q):
        return left_all.at[at_q, :, pl.ds(pl.multiple_of(at_y * WIDE, WIDE), WIDE)]

    def left_copy(n):
        return remote(left_own, left_slot(y, q), left_send.at[n], left_recv.at[mine], row_peer(spot, n))

    def right_copy(n):
        return remote(
            right_own, right_all.at[slot, q], right_send.at[n], right_recv.at[slot * 4 + q], right_user(spot, n)
        )

    def cot_part(n):
        return cotangent.at[:, pl.ds(pl.multiple_of(q * 128 + n * 32, 32), 32), :]

    def cot_copy(n):
        return remote(cot_part(n), cot_all.at[y], cot_send.at[n], cot_recv.at[y], row_peer(spot, n * 4 + q))

    def start_main(n):
        @pl.when(jnp.logical_not(is_me(right_user(spot, n))))
        def _():
            right_copy(n).start()

        @pl.when(n != mine)
        def _():
            left_copy(n).start()

    def start_cot(n):
        @pl.when(n != y)
        def _():
            cot_copy(n).start()

    repeat(4, start_cot)
    repeat(16, start_main)
    pltpu.make_async_copy(left_own, left_slot(y, q), left_recv.at[mine]).start()

    @pl.when(self_user)
    def _():
        pltpu.make_async_copy(right_own, right_all.at[slot, q], right_recv.at[slot * 4 + q]).start()

    pltpu.make_async_copy(cot_part(y), cot_all.at[y], cot_recv.at[y]).start()

    def finish_main(n):
        at_y, at_q = lax.div(n, 4), lax.rem(n, 4)
        pltpu.make_async_copy(left_own, left_slot(at_y, at_q), left_recv.at[n]).wait()
        pltpu.make_async_copy(right_own, right_all.at[at_y, at_q], right_recv.at[n]).wait()

        @pl.when(n != mine)
        def _():
            left_copy(n).wait_send()

        @pl.when(jnp.logical_not(is_me(right_user(spot, n))))
        def _():
            right_copy(n).wait_send()

    def finish_cot(n):
        pltpu.make_async_copy(cot_part(n), cot_all.at[n], cot_recv.at[n]).wait()

        @pl.when(n != y)
        def _():
            cot_copy(n).wait_send()

    repeat(16, finish_main)
    repeat(4, finish_cot)


def pair_kernel(
    left_all, right_all, cot_all, weight, weight_turned,
    pair, weight_grad, left_grad, right_grad,
    left_mat, right_mat, product, counts, scaled, folded, grad_outer,
):
    row_mask = [
        jnp.concatenate(
            [
                left_all[2 * h, ROWS : ROWS + 8, y * WIDE : y * WIDE + 128].astype(F32)
                + left_all[2 * h + 1, ROWS : ROWS + 8, y * WIDE : y * WIDE + 128].astype(F32)
                for h in range(2)
            ],
            axis=1,
        )
        for y in range(4)
    ]
    column_mask = jnp.concatenate(
        [
            jnp.concatenate(
                [
                    right_all[b, 2 * h, ROWS : ROWS + 8, :128].astype(F32)
                    + right_all[b, 2 * h + 1, ROWS : ROWS + 8, :128].astype(F32)
                    for h in range(2)
                ],
                axis=1,
            )
            for b in range(4)
        ],
        axis=0,
    )
    for i in range(32):
        row = row_mask[i // 8][i % 8 : i % 8 + 1, :]
        product[i * 32 : (i + 1) * 32, :] = (row * column_mask).astype(BF16)
    counts[...] = dot(product[...], jnp.ones((256, 128), BF16))
    for y in range(4):
        cot = cot_all[y].astype(F32).reshape(256, 128)
        scaled[y * 256 : (y + 1) * 256, :] = (cot / counts[y * 256 : (y + 1) * 256, :]).astype(BF16)

    for q in range(4):
        rows = slice(q * ROWS, (q + 1) * ROWS)
        left_mat[rows, :] = left_all[q, :ROWS, :]
        for t in range(2):
            parts = [right_all[b, q, :ROWS, t * 128 : (t + 1) * 128].astype(F32) for b in range(4)]
            for b, part in enumerate(swap(parts, 8)):
                right_mat[rows, (t * 4 + b) * 128 : (t * 4 + b + 1) * 128] = part.astype(BF16)

    def forward(g):
        span = pl.ds(pl.multiple_of(g * 128, 128), 128)
        turned = left_mat[:, span].astype(F32).T.astype(BF16)
        for t in range(8):
            outer = dot(turned, right_mat[:, t * 128 : (t + 1) * 128])
            parts = swap([outer[i * 32 : (i + 1) * 32, :] for i in range(4)], 32)
            for a, part in enumerate(parts):
                folded[(t * 4 + a) * 32 : (t * 4 + a + 1) * 32, span] = part.astype(BF16)

    def backward(g):
        span = pl.ds(pl.multiple_of(g * 128, 128), 128)
        scaled_part = scaled[span, :]
        for t in range(8):
            grad = dot_nt(weight[t * 128 : (t + 1) * 128, :], scaled_part)
            parts = swap([grad[a * 32 : (a + 1) * 32, :] for a in range(4)], 32)
            for i, part in enumerate(parts):
                at = pl.ds(pl.multiple_of(g * 128 + i * 32, 32), 32)
                grad_outer[at, t * 128 : (t + 1) * 128] = part.astype(BF16)

    def project(g):
        span = pl.ds(pl.multiple_of(g * 128, 128), 128)
        turned = dot(weight_turned[...], folded[:, span])
        update = (turned.T / counts[span, :]).astype(BF16)
        pair[pl.ds(pl.multiple_of(g * 4, 4), 4)] = update.reshape(4, 32, 128)

    def weigh(g):
        span = pl.ds(pl.multiple_of(g * 128, 128), 128)
        weight_grad[span, :] = dot(folded[span, :], scaled[...]).astype(BF16)

    def left_part(g):
        span = pl.ds(pl.multiple_of(g * 128, 128), 128)
        part = dot_nt(right_mat[...], grad_outer[span, :]).astype(BF16)
        for q in range(4):
            left_grad[q, :, span] = part[q * ROWS : (q + 1) * ROWS, :]

    repeat(8, backward)
    repeat(8, left_part)
    for t in range(2):
        for q in range(4):
            part = [
                dot(left_mat[q * ROWS : (q + 1) * ROWS, :], grad_outer[:, (t * 4 + b) * 128 : (t * 4 + b + 1) * 128])
                for b in range(4)
            ]
            for b, block in enumerate(swap(part, 8)):
                right_grad[b, q, :, t * 128 : (t + 1) * 128] = block.astype(BF16)
    repeat(8, forward)
    repeat(8, weigh)
    repeat(8, project)


def scatter_kernel(
    left_grad, right_grad, weight_grad, pair, token_turned, mask, white, spread, gain, maps,
    pair_out, weight_out, table_out,
    left_in, right_in, weight_in, weight_sum, weight_far, weight_total,
    table_part, table_in, table_sum, table_far, table_total,
    left_send, left_recv, right_send, right_recv, pair_send, pair_recv,
    wa_send, wa_recv, wb_send, wb_recv, wc_send, wc_recv,
    ta_send, ta_recv, tb_send, tb_recv, tc_send, tc_recv,
):
    spot = place()
    y, z, x, q = spot
    mine = y * 4 + q
    deep = z * 2 + x
    my_res = y * 16 + deep
    self_user = jnp.logical_and(lax.div(z, 2) == y, q == y)

    def is_me(target):
        return jnp.logical_and(target[0] == my_res, target[1] == q)

    barrier = pltpu.get_barrier_semaphore()

    def greet(n):
        @pl.when(n != mine)
        def _():
            signal(barrier, row_peer(spot, n))

        @pl.when(n != deep)
        def _():
            signal(barrier, depth_peer(spot, n))

        user = right_user(spot, n)

        @pl.when(jnp.logical_not(is_me(user)))
        def _():
            signal(barrier, user)

    repeat(16, greet)
    pl.semaphore_wait(barrier, jnp.where(self_user, 45, 46))

    def left_piece(n):
        return left_grad.at[lax.rem(n, 4), :, pl.ds(pl.multiple_of(lax.div(n, 4) * WIDE, WIDE), WIDE)]

    def left_copy(n):
        return remote(left_piece(n), left_in.at[mine], left_send.at[n], left_recv.at[mine], row_peer(spot, n))

    def right_piece(n):
        return right_grad.at[lax.div(n, 4), lax.rem(n, 4)]

    def right_copy(n):
        return remote(right_piece(n), right_in.at[deep], right_send.at[n], right_recv.at[deep], right_owner(spot, n))

    def pair_piece(n):
        return pair.at[pl.ds(pl.multiple_of(n * 8, 8), 8)]

    def pair_slot(n):
        return pair_out.at[:, pl.ds(pl.multiple_of(n * 32, 32), 32), :]

    def pair_copy(n):
        return remote(pair_piece(n), pair_slot(y), pair_send.at[n], pair_recv.at[y], row_peer(spot, n * 4 + q))

    def weight_piece(n):
        return weight_grad.at[pl.ds(pl.multiple_of(n * 64, 64), 64), :]

    def wa_copy(n):
        return remote(weight_piece(n), weight_in.at[mine], wa_send.at[n], wa_recv.at[mine], row_peer(spot, n))

    def wb_copy(n):
        return remote(weight_sum, weight_far.at[deep], wb_send.at[n], wb_recv.at[deep], depth_peer(spot, n))

    def wc_slot(n):
        return weight_out.at[pl.ds(pl.multiple_of(n * 64, 64), 64), :]

    def wc_copy(n):
        return remote(weight_total, wc_slot(mine), wc_send.at[n], wc_recv.at[mine], row_peer(spot, n))

    def ta_copy(n):
        return remote(table_part.at[n], table_in.at[mine], ta_send.at[n], ta_recv.at[mine], row_peer(spot, n))

    def tb_copy(n):
        return remote(table_sum, table_far.at[deep], tb_send.at[n], tb_recv.at[deep], depth_peer(spot, n))

    def tc_copy(n):
        return remote(table_total, table_out.at[mine], tc_send.at[n], tc_recv.at[mine], row_peer(spot, n))

    def wait(src, dst, sem):
        pltpu.make_async_copy(src, dst, sem).wait()

    def start_main(n):
        @pl.when(jnp.logical_not(is_me(right_owner(spot, n))))
        def _():
            right_copy(n).start()

        @pl.when(n != mine)
        def _():
            left_copy(n).start()

    def start_rest(n):
        @pl.when(n != mine)
        def _():
            wa_copy(n).start()

    def start_pair(n):
        @pl.when(n != y)
        def _():
            pair_copy(n).start()

    repeat(16, start_main)
    pltpu.make_async_copy(left_piece(mine), left_in.at[mine], left_recv.at[mine]).start()

    @pl.when(self_user)
    def _():
        n = (lax.rem(z, 2) * 2 + x) * 4 + q
        pltpu.make_async_copy(right_piece(n), right_in.at[deep], right_recv.at[deep]).start()

    repeat(16, start_rest)
    pltpu.make_async_copy(weight_piece(mine), weight_in.at[mine], wa_recv.at[mine]).start()
    repeat(4, start_pair)
    pltpu.make_async_copy(pair_piece(y), pair_slot(y), pair_recv.at[y]).start()

    def arrive_main(n):
        wait(left_piece(n), left_in.at[n], left_recv.at[n])
        wait(right_piece(n), right_in.at[n], right_recv.at[n])

    repeat(16, arrive_main)

    repeat(16, lambda n: wait(weight_piece(n), weight_in.at[n], wa_recv.at[n]))
    total = weight_in[0].astype(F32)
    for n in range(1, 16):
        total = total + weight_in[n].astype(F32)
    weight_sum[...] = total.astype(BF16)

    def start_wb(n):
        @pl.when(n != deep)
        def _():
            wb_copy(n).start()

    repeat(16, start_wb)
    pltpu.make_async_copy(weight_sum, weight_far.at[deep], wb_recv.at[deep]).start()

    left_total = left_in[0].astype(F32)
    right_total = right_in[0].astype(F32)
    for n in range(1, 16):
        left_total = left_total + left_in[n].astype(F32)
        right_total = right_total + right_in[n].astype(F32)
    left_total = left_total.astype(BF16).astype(F32)
    right_total = right_total.astype(BF16).astype(F32)
    lane = lanes((ROWS, 128))
    wide_lane = lanes((ROWS, WIDE))
    kind = lax.broadcasted_iota(jnp.int32, (32, ROWS), 0)
    table = jnp.zeros((32, WIDE), F32)
    for i in range(8):
        tile = left_total[:, (i // 4) * 128 : (i // 4 + 1) * 128]
        picked = jnp.concatenate(
            [
                jnp.where(lax.div(lane, 32) == i % 4, tile, 0.0),
                jnp.where(lax.rem(wide_lane, 8) == i, right_total, 0.0),
            ],
            axis=1,
        ).astype(BF16)
        gained = mask[:, i : i + 1] * dot_nt(picked, maps[...]) * gain[...]
        whitened = white[i]
        stream_grad = spread[i][:, :1] * (
            gained
            - jnp.mean(gained, axis=-1, keepdims=True)
            - whitened * jnp.mean(gained * whitened, axis=-1, keepdims=True)
        )
        hot = (kind == token_turned[i : i + 1, :]).astype(F32)
        table = table + jnp.dot(hot, stream_grad, precision=TOP_PRECISION, preferred_element_type=F32)
    for n in range(TILES):
        table_part[n] = table[(n // 2) * 8 : (n // 2 + 1) * 8, (n % 2) * 128 : (n % 2 + 1) * 128]

    def start_ta(n):
        @pl.when(n != mine)
        def _():
            ta_copy(n).start()

        @pl.when(n == mine)
        def _():
            pltpu.make_async_copy(table_part.at[n], table_in.at[mine], ta_recv.at[mine]).start()

    repeat(TILES, start_ta)
    holder = mine < TILES

    @pl.when(holder)
    def _():
        repeat(16, lambda n: wait(table_sum, table_in.at[n], ta_recv.at[n]))
        partial = table_in[0]
        for n in range(1, 16):
            partial = partial + table_in[n]
        table_sum[...] = partial

        def start_tb(n):
            @pl.when(n != deep)
            def _():
                tb_copy(n).start()

        repeat(16, start_tb)
        pltpu.make_async_copy(table_sum, table_far.at[deep], tb_recv.at[deep]).start()

    repeat(16, lambda n: wait(weight_sum, weight_far.at[n], wb_recv.at[n]))
    total = weight_far[0].astype(F32)
    for n in range(1, 16):
        total = total + weight_far[n].astype(F32)
    weight_total[...] = total.astype(BF16)

    def start_wc(n):
        @pl.when(n != mine)
        def _():
            wc_copy(n).start()

    repeat(16, start_wc)
    pltpu.make_async_copy(weight_total, wc_slot(mine), wc_recv.at[mine]).start()

    @pl.when(holder)
    def _():
        repeat(16, lambda n: wait(table_sum, table_far.at[n], tb_recv.at[n]))
        partial = table_far[0]
        for n in range(1, 16):
            partial = partial + table_far[n]
        table_total[...] = partial

        def start_tc(n):
            @pl.when(n != mine)
            def _():
                tc_copy(n).start()

        repeat(16, start_tc)
        pltpu.make_async_copy(table_total, table_out.at[mine], tc_recv.at[mine]).start()

    repeat(4, lambda n: wait(pair_piece(n), pair_slot(n), pair_recv.at[n]))
    repeat(16, lambda n: wait(weight_total, wc_slot(n), wc_recv.at[n]))
    repeat(TILES, lambda n: wait(table_total, table_out.at[n], tc_recv.at[n]))

    def sent(n):
        @pl.when(n != mine)
        def _():
            left_copy(n).wait_send()
            wa_copy(n).wait_send()
            wc_copy(n).wait_send()

        @pl.when(jnp.logical_not(is_me(right_owner(spot, n))))
        def _():
            right_copy(n).wait_send()

        @pl.when(n != deep)
        def _():
            wb_copy(n).wait_send()

        @pl.when(jnp.logical_and(holder, n != deep))
        def _():
            tb_copy(n).wait_send()

        @pl.when(jnp.logical_and(holder, n != mine))
        def _():
            tc_copy(n).wait_send()

    def sent_table(n):
        @pl.when(n != mine)
        def _():
            ta_copy(n).wait_send()

    def sent_pair(n):
        @pl.when(n != y)
        def _():
            pair_copy(n).wait_send()

    repeat(16, sent)
    repeat(TILES, sent_table)
    repeat(4, sent_pair)


def vmem(count):
    return [pl.BlockSpec(memory_space=pltpu.VMEM)] * count


def sems(*sizes):
    return [pltpu.SemaphoreType.DMA((size,)) for size in sizes]


def shape(dims, dtype=BF16):
    return jax.ShapeDtypeStruct(dims, dtype)


def body(
    alignment_token_classes, deletions, alignment_mask, homolog_stack_values,
    letter_lookup_coefficients, gap_lookup_coefficients, standardize_gain, standardize_offset,
    first_factor_map, left_bias_vector, second_factor_map, right_bias_vector,
    output_weight_matrix, cotangent,
):
    q = lax.axis_index("seq")
    stack = homolog_stack_values.transpose(1, 0, 2)
    mask = alignment_mask.astype(F32)
    mask_turned = jnp.pad(mask.T, ((0, 8), (0, 0)))
    empty = jnp.zeros_like(mask_turned)
    odd = (q % 2) == 1
    mask_rows = jnp.concatenate(
        [jnp.where(odd, empty, mask_turned), jnp.where(odd, mask_turned, empty), empty, empty], axis=1
    ).astype(BF16)
    steps = jnp.arange(32, dtype=jnp.int32).astype(F32)[:, None]
    gaps = (steps > 0).astype(F32) * gap_lookup_coefficients[0] + (
        2.0 / math.pi * jnp.arctan(steps / 3.0)
    ) * gap_lookup_coefficients[1]
    letters = jnp.pad(letter_lookup_coefficients, ((0, 32 - letter_lookup_coefficients.shape[0]), (0, 0)))
    table = jnp.concatenate([letters, gaps, jnp.zeros((64, 256), F32)], axis=0)
    gain = standardize_gain[None, :]
    offset = standardize_offset[None, :]
    maps = jnp.concatenate([jnp.tile(first_factor_map, (1, 4)), jnp.repeat(second_factor_map, 8, axis=1)], axis=1)
    bias = jnp.concatenate([jnp.tile(left_bias_vector, 4), jnp.repeat(right_bias_vector, 8)])[None, :]
    weight = output_weight_matrix.reshape(32, 2, 4, 4, 128).transpose(1, 3, 2, 0, 4).reshape(1024, 128)

    left_all, right_all, cot_all, white, spread = pl.pallas_call(
        gather_kernel,
        out_shape=[
            shape((4, BLOCK, 1024)),
            shape((4, 4, BLOCK, WIDE)),
            shape((4, 8, 32, 128)),
            shape((8, ROWS, 256), F32),
            shape((8, ROWS, 128), F32),
        ],
        in_specs=vmem(10) + [pl.BlockSpec(memory_space=pl.ANY)],
        out_specs=vmem(5),
        scratch_shapes=[pltpu.VMEM((BLOCK, WIDE), BF16), pltpu.VMEM((BLOCK, WIDE), BF16)]
        + sems(16, 16, 16, 16, 4, 4),
        compiler_params=pltpu.CompilerParams(
            collective_id=0, has_side_effects=True, vmem_limit_bytes=32 * 1024 * 1024
        ),
        name="gather",
    )(
        alignment_token_classes, deletions, mask, mask_rows, stack, table, gain, offset, maps, bias, cotangent
    )

    pair, weight_grad, left_grad, right_grad = pl.pallas_call(
        pair_kernel,
        out_shape=[
            shape((32, 32, 128)),
            shape((1024, 128)),
            shape((4, ROWS, 1024)),
            shape((4, 4, ROWS, WIDE)),
        ],
        in_specs=vmem(5),
        out_specs=vmem(4),
        scratch_shapes=[
            pltpu.VMEM((256, 1024), BF16),
            pltpu.VMEM((256, 1024), BF16),
            pltpu.VMEM((1024, 256), BF16),
            pltpu.VMEM((1024, 128), F32),
            pltpu.VMEM((1024, 128), BF16),
            pltpu.VMEM((1024, 1024), BF16),
            pltpu.VMEM((1024, 1024), BF16),
        ],
        compiler_params=pltpu.CompilerParams(vmem_limit_bytes=40 * 1024 * 1024),
        name="pairs",
    )(left_all, right_all, cot_all, weight, weight.T)

    tile = pltpu.VMEM((8, 128), F32)
    pair_update, weight_out, table_out = pl.pallas_call(
        scatter_kernel,
        out_shape=[shape((8, 128, 128)), shape((1024, 128)), shape((TILES, 8, 128), F32)],
        in_specs=vmem(10),
        out_specs=vmem(3),
        scratch_shapes=[
            pltpu.VMEM((16, ROWS, WIDE), BF16),
            pltpu.VMEM((16, ROWS, WIDE), BF16),
            pltpu.VMEM((16, 64, 128), BF16),
            pltpu.VMEM((64, 128), BF16),
            pltpu.VMEM((16, 64, 128), BF16),
            pltpu.VMEM((64, 128), BF16),
            pltpu.VMEM((TILES, 8, 128), F32),
            pltpu.VMEM((16, 8, 128), F32),
            tile,
            pltpu.VMEM((16, 8, 128), F32),
            tile,
        ]
        + sems(16, 16, 16, 16, 4, 4, 16, 16, 16, 16, 16, 16, 16, 16, 16, 16, 16, 16),
        compiler_params=pltpu.CompilerParams(
            collective_id=1, has_side_effects=True, vmem_limit_bytes=32 * 1024 * 1024
        ),
        name="scatter",
    )(
        left_grad, right_grad, weight_grad, pair, alignment_token_classes.T, mask, white, spread, gain, maps
    )
    grad_weight = (
        weight_out.astype(F32).reshape(2, 4, 4, 32, 128).transpose(3, 0, 2, 1, 4).reshape(1024, 128)
    )
    grad_table = (
        table_out.reshape(TILES // 2, 2, 8, 128).transpose(0, 2, 1, 3).reshape(TILES * 4, 256)
    )[: letter_lookup_coefficients.shape[0]]
    return (pair_update, grad_weight, grad_table)


def solution(mesh):
    in_specs = (
        P("seq", "res"), P("seq", "res"), P("seq", "res"), P("seq", "res", None),
        P(), P(), P(), P(), P(), P(), P(), P(), P(),
        P("res", None, None),
    )
    out_specs = (P("res", "seq", None), P(), P())
    return jax.shard_map(body, mesh=mesh, in_specs=in_specs, out_specs=out_specs, check_vma=False)
```

```python
import math

import jax
import jax.numpy as jnp
from jax import lax
from jax.experimental import pallas as pl
from jax.experimental.pallas import tpu as pltpu
from jax.sharding import PartitionSpec as P

EPSILON = 1e-05
MESH = pl.DeviceIdType.MESH
F32 = jnp.float32
BF16 = jnp.bfloat16

ROWS = 64
WIDE = 256
TILES = 6


def device(y, z, xh, xl, c):
    return (y * 16 + z * 2 + xh, xl * 2 + c)


def repeat(count, step):
    lax.fori_loop(0, count, lambda n, carried: (step(n), carried)[1], 0)


def remote(src, dst, send, recv, target):
    return pltpu.make_async_remote_copy(
        src_ref=src, dst_ref=dst, send_sem=send, recv_sem=recv, device_id=target, device_id_type=MESH
    )


def start_all(count, copy, own):
    def step(n):
        @pl.when(n != own)
        def _():
            copy(n).start()

    repeat(count, step)


def sent_all(count, copy, own):
    def step(n):
        @pl.when(n != own)
        def _():
            copy(n).wait_send()

    repeat(count, step)


def local(src, dst, sem):
    return pltpu.make_async_copy(src, dst, sem)


def lanes(dims):
    return lax.broadcasted_iota(jnp.int32, dims, len(dims) - 1)


def block(n, size):
    return pl.ds(pl.multiple_of(n * size, size), size)


def swap(parts, stride):
    lane = lanes(parts[0].shape)
    low = lax.rem(lax.div(lane, stride), 2) == 0
    high = lax.rem(lax.div(lane, 2 * stride), 2) == 0

    def pair(first, second, step, keep):
        return (
            jnp.where(keep, first, pltpu.roll(second, step, 1)),
            jnp.where(keep, pltpu.roll(first, 128 - step, 1), second),
        )

    a, b = pair(parts[0], parts[1], stride, low)
    c, d = pair(parts[2], parts[3], stride, low)
    a, c = pair(a, c, 2 * stride, high)
    b, d = pair(b, d, 2 * stride, high)
    return [a, b, c, d]


def dot(first, second):
    return jnp.dot(first, second, preferred_element_type=F32)


def dot_nt(first, second):
    return lax.dot_general(first, second, (((1,), (1,)), ((), ())), preferred_element_type=F32)


def split(value, count):
    pieces = []
    for _ in range(count):
        piece = value.astype(BF16)
        pieces.append(piece)
        value = value - piece.astype(F32)
    return pieces


def total(ref, count):
    value = ref[0].astype(F32)
    for n in range(1, count):
        value = value + ref[n].astype(F32)
    return value


def kernel(
    token_h, deletion_h, mask_h, mask_rows_h, token_row_h, stack_h, table_h, gain_h, offset_h, maps_h, bias_h,
    weight_h, turned_h, cotangent,
    pair_out, weight_out, table_out,
    token, deletion, mask, mask_rows, token_row, stack, table, gain, offset, maps, bias, weight, weight_turned,
    white, spread, left_own, right_own, row_masks, column_masks, cot_all, left_all, right_all,
    right_mat, product, counts, scaled, folded, grad_outer, pair,
    left_grad, left_core, left_sum, left_in, left_last, left_send, right_grad, right_part, right_in,
    weight_grad, weight_in, weight_sum, weight_far, weight_total, weight_all,
    table_part, table_core, table_x, table_y, table_z, table_half, table_all,
    in_sem, rm_send, rm_recv, cm_send, cm_recv, cot_send, cot_recv,
    l1_send, l1_recv, l2_send, l2_recv, l3_send, l3_recv, r_send, r_recv,
    gx_send, gx_recv, gz_send, gz_recv, gl_send, gl_recv, gr_send, gr_recv, pair_send, pair_recv,
    wa_send, wa_recv, wb_send, wb_recv, wc_send, wc_recv,
    t_send, t_recv, tx_send, tx_recv, ty_send, ty_recv, tz_send, tz_recv,
):
    res = lax.axis_index("res")
    q = lax.axis_index("seq")
    y, z, xh = lax.div(res, 16), lax.rem(lax.div(res, 2), 8), lax.rem(res, 2)
    xl, c = lax.div(q, 2), lax.rem(q, 2)
    zi, parity = lax.div(z, 2), lax.rem(z, 2)
    active = parity == xl
    other_q = (1 - xl) * 2 + c
    plane = y * 4 + xh * 2 + xl
    deep = z * 2 + c
    column = lax.rem(y, 2) * 2 + xh
    own_row = jnp.where(active, deep, -1)
    own_column = jnp.where(lax.div(y, 2) == c, plane, -1)
    other_core = device(y, z, xh, xl, 1 - c)
    partner = device(y, z, xh, 1 - xl, c)

    def wait(src, dst, sem):
        local(src, dst, sem).wait()

    loads = [
        local(src, dst, in_sem.at[n])
        for n, (src, dst) in enumerate(
            [
                (token_h, token), (deletion_h, deletion), (mask_h, mask), (mask_rows_h, mask_rows),
                (token_row_h, token_row), (stack_h, stack), (table_h, table), (gain_h, gain), (offset_h, offset),
                (maps_h, maps), (bias_h, bias), (weight_h, weight), (turned_h, weight_turned),
            ]
        )
    ]
    for load in loads:
        load.start()

    barrier = pltpu.get_barrier_semaphore()

    def signal(target):
        pl.semaphore_signal(barrier, inc=1, device_id=target, device_id_type=MESH)

    def greet(n):
        @pl.when(n != z * 4 + q)
        def _():
            signal((y * 16 + lax.div(n, 4) * 2 + xh, lax.rem(n, 4)))

        @pl.when(n != (y * 2 + xh) * 4 + q)
        def _():
            signal((lax.div(n, 8) * 16 + z * 2 + lax.rem(lax.div(n, 4), 2), lax.rem(n, 4)))

    repeat(32, greet)

    def line_user(n):
        return device(y, lax.div(n, 2), xh, parity, lax.rem(n, 2))

    def plane_user(n):
        return device(lax.div(n, 4), z, lax.div(lax.rem(n, 4), 2), lax.rem(n, 2), lax.div(y, 2))

    def rm_copy(n):
        return remote(mask_rows, row_masks.at[zi, q], rm_send.at[n], rm_recv.at[zi * 4 + q], line_user(n))

    def cm_copy(n):
        return remote(mask_rows, column_masks.at[column, q], cm_send.at[n], cm_recv.at[column * 4 + q], plane_user(n))

    def cot_part(n):
        return cotangent.at[:, pl.ds(c * 2, 2), block(n, 16), :]

    def cot_copy(n):
        return remote(cot_part(n), cot_all.at[zi], cot_send.at[n], cot_recv.at[zi], device(y, n, xh, xl, c))

    def left_slot(at_q, at_z):
        return left_all.at[at_q, :, block(at_z, WIDE)]

    def l1_copy():
        return remote(left_own, left_slot(q, zi), l1_send.at[0], l1_recv.at[0], partner)

    def l2_copy(n):
        return remote(
            left_own, left_slot(q, zi), l2_send.at[n], l2_recv.at[zi * 2 + xl], device(y, n, xh, xl, c)
        )

    def l2_forward(n):
        return remote(
            left_slot(other_q, zi), left_slot(other_q, zi), l2_send.at[8 + n], l2_recv.at[zi * 2 + 1 - xl],
            device(y, n, xh, xl, c),
        )

    def l3_copy(n):
        at_q = n * 2 + c
        return remote(left_all.at[at_q], left_all.at[at_q], l3_send.at[n], l3_recv.at[n], other_core)

    def r_copy(n):
        return remote(right_own, right_all.at[column, q], r_send.at[n], r_recv.at[column * 4 + q], plane_user(n))

    for load in loads[:11]:
        load.wait()
    lane = lanes((ROWS, 128))
    wide_lane = lanes((ROWS, WIDE))
    pieces = split(table[...], 3)
    right_value = jnp.zeros((ROWS, WIDE), F32)
    for h in range(2):
        hot = jnp.concatenate(
            [
                jnp.logical_or(lane == token[:, i : i + 1], lane == deletion[:, i : i + 1] + 32).astype(F32)
                for i in range(h * 4, h * 4 + 4)
            ],
            axis=0,
        ).astype(BF16)
        hidden = stack[h * 4 : h * 4 + 4].reshape(256, 256).astype(F32) + (
            dot(hot, pieces[0]) + dot(hot, pieces[1]) + dot(hot, pieces[2])
        )
        centered = hidden - jnp.mean(hidden, axis=-1, keepdims=True)
        variance = jnp.mean(centered * centered, axis=-1, keepdims=True)
        scale = lax.rsqrt(variance + EPSILON)
        whitened = centered * scale
        white[h * 256 : (h + 1) * 256, :] = whitened
        spread[h * 256 : (h + 1) * 256, :] = jnp.broadcast_to(scale, (256, 128))
        normed = (whitened * gain[...] + offset[...]).astype(BF16)
        rows = dot(normed, maps[...]) + bias[...]
        left_value = jnp.zeros((ROWS, 128), F32)
        for i in range(4):
            part = mask[:, h * 4 + i : h * 4 + i + 1].astype(F32) * rows[i * ROWS : (i + 1) * ROWS, :]
            left_value = jnp.where(lax.div(lane, 32) == i, part[:, :128], left_value)
            right_value = jnp.where(lax.rem(wide_lane, 8) == h * 4 + i, part[:, 128:], right_value)
        left_own[:, h * 128 : (h + 1) * 128] = left_value.astype(BF16)
        if h == 0:
            pl.semaphore_wait(barrier, 62)
            start_all(16, rm_copy, own_row)
            start_all(16, cm_copy, own_column)

            @pl.when(active)
            def _():
                local(mask_rows, row_masks.at[zi, q], rm_recv.at[zi * 4 + q]).start()
                start_all(8, cot_copy, z)
                local(cot_part(z), cot_all.at[zi], cot_recv.at[zi]).start()

            @pl.when(lax.div(y, 2) == c)
            def _():
                local(mask_rows, column_masks.at[column, q], cm_recv.at[column * 4 + q]).start()

    right_own[...] = right_value.astype(BF16)

    @pl.when(jnp.logical_not(active))
    def _():
        l1_copy().start()

    @pl.when(active)
    def _():
        start_all(8, l2_copy, z)
        local(left_own, left_slot(q, zi), l2_recv.at[zi * 2 + xl]).start()

    start_all(16, r_copy, own_column)

    @pl.when(lax.div(y, 2) == c)
    def _():
        local(right_own, right_all.at[column, q], r_recv.at[column * 4 + q]).start()

    @pl.when(active)
    def _():
        wait(left_own, left_slot(other_q, zi), l1_recv.at[0])
        start_all(8, l2_forward, z)

    def arrive_masks(n):
        wait(mask_rows, row_masks.at[lax.div(n, 4), lax.rem(n, 4)], rm_recv.at[n])
        wait(mask_rows, column_masks.at[lax.div(n, 4), lax.rem(n, 4)], cm_recv.at[n])

    repeat(16, arrive_masks)
    column_mask = jnp.concatenate(
        [
            jnp.concatenate([column_masks[b, 2 * h] + column_masks[b, 2 * h + 1] for h in range(2)], axis=1)
            for b in range(4)
        ],
        axis=0,
    )
    for i in range(32):
        row = jnp.concatenate(
            [
                row_masks[i // 8, 2 * h, i % 8 : i % 8 + 1, :] + row_masks[i // 8, 2 * h + 1, i % 8 : i % 8 + 1, :]
                for h in range(2)
            ],
            axis=1,
        )
        product[i * 32 : (i + 1) * 32, :] = (row * column_mask).astype(BF16)
    counts[...] = dot(product[...], jnp.ones((256, 128), BF16))
    for load in loads[11:]:
        load.wait()
    repeat(4, lambda n: wait(cot_part(n), cot_all.at[n], cot_recv.at[n]))
    for n in range(4):
        cot = cot_all[n].astype(F32).reshape(256, 128)
        scaled[n * 256 : (n + 1) * 256, :] = (cot / counts[n * 256 : (n + 1) * 256, :]).astype(BF16)

    def backward(g):
        span = block(g, 256)
        scaled_part = scaled[span, :]
        for t in range(8):
            grad = dot_nt(weight[t * 128 : (t + 1) * 128, :], scaled_part)
            for half in range(2):
                lane_part = grad[:, half * 128 : (half + 1) * 128]
                parts = swap([lane_part[a * 32 : (a + 1) * 32, :] for a in range(4)], 32)
                for i, part in enumerate(parts):
                    at = pl.ds(pl.multiple_of(g * 256 + half * 128 + i * 32, 32), 32)
                    grad_outer[at, t * 128 : (t + 1) * 128] = part.astype(BF16)

    repeat(4, backward)

    forwarded = jnp.where(active, zi * 2 + 1 - xl, -1)

    def arrive_left(n):
        @pl.when(n != forwarded)
        def _():
            wait(left_own, left_slot(lax.rem(n, 2) * 2 + c, lax.div(n, 2)), l2_recv.at[n])

    repeat(8, arrive_left)
    start_all(2, l3_copy, -1)
    repeat(16, lambda n: wait(right_own, right_all.at[lax.div(n, 4), lax.rem(n, 4)], r_recv.at[n]))
    for at_q in range(4):
        rows = slice(at_q * ROWS, (at_q + 1) * ROWS)
        for t in range(2):
            parts = [right_all[b, at_q, :, t * 128 : (t + 1) * 128].astype(F32) for b in range(4)]
            for b, part in enumerate(swap(parts, 8)):
                right_mat[rows, (t * 4 + b) * 128 : (t * 4 + b + 1) * 128] = part.astype(BF16)

    def left_step(g):
        span = block(g, 256)
        part = dot_nt(right_mat[...], grad_outer[span, :]).astype(BF16)
        for at_q in range(4):
            left_grad[at_q, :, span] = part[at_q * ROWS : (at_q + 1) * ROWS, :]

    repeat(4, left_step)

    def gx_copy(n):
        return remote(left_grad.at[n * 2 + 1 - c], left_core.at[n], gx_send.at[n], gx_recv.at[n], other_core)

    start_all(2, gx_copy, -1)
    repeat(2, lambda n: wait(left_all.at[n * 2 + 1 - c], left_all.at[n * 2 + 1 - c], l3_recv.at[n]))

    def right_step(t):
        for b in range(2):
            right_part[:, b * 256 : (b + 1) * 256] = dot(
                left_all[...].reshape(256, 1024), grad_outer[:, t * 512 + b * 256 : t * 512 + (b + 1) * 256]
            )
        for at_q in range(4):
            rows = slice(at_q * ROWS, (at_q + 1) * ROWS)
            parts = swap([right_part[rows, b * 128 : (b + 1) * 128] for b in range(4)], 8)
            for b, part in enumerate(parts):
                right_grad[b, at_q, :, t * 128 : (t + 1) * 128] = part.astype(BF16)

    right_step(0)

    def gz_part(n):
        return left_sum.at[:, :, block(n, WIDE)]

    def gz_copy(n):
        return remote(
            gz_part(n), left_in.at[z], gz_send.at[n], gz_recv.at[z], device(y, n * 2 + xl, xh, xl, c)
        )

    own_gz = jnp.where(active, zi, -1)
    for n in range(2):
        wait(left_core.at[n], left_core.at[n], gx_recv.at[n])
        left_sum[n] = (left_grad[n * 2 + c].astype(F32) + left_core[n].astype(F32)).astype(BF16)
    start_all(4, gz_copy, own_gz)

    @pl.when(active)
    def _():
        local(gz_part(zi), left_in.at[z], gz_recv.at[z]).start()

    right_step(1)

    def gr_part(n):
        return right_grad.at[lax.div(n, 4), lax.rem(n, 4)]

    def gr_copy(n):
        target = device(c * 2 + lax.div(n, 8), z, lax.rem(lax.div(n, 4), 2), lax.div(lax.rem(n, 4), 2), lax.rem(n, 2))
        return remote(gr_part(n), right_in.at[plane], gr_send.at[n], gr_recv.at[plane], target)

    own_gr = jnp.where(lax.div(y, 2) == c, column * 4 + q, -1)
    start_all(16, gr_copy, own_gr)

    @pl.when(lax.div(y, 2) == c)
    def _():
        local(gr_part(column * 4 + q), right_in.at[plane], gr_recv.at[plane]).start()

    def forward(g):
        span = block(g, 128)
        turned = left_all[:, :, span].reshape(256, 128).astype(F32).T.astype(BF16)
        for t in range(8):
            outer = dot(turned, right_mat[:, t * 128 : (t + 1) * 128])
            parts = swap([outer[i * 32 : (i + 1) * 32, :] for i in range(4)], 32)
            for a, part in enumerate(parts):
                folded[(t * 4 + a) * 32 : (t * 4 + a + 1) * 32, span] = part.astype(BF16)

    def weigh(g):
        span = block(g, 128)
        weight_grad[span, :] = dot(folded[span, :], scaled[...]).astype(BF16)

    def project(g):
        span = block(g, 128)
        value = dot(weight_turned[...], folded[:, span])
        update = (value.T / counts[span, :]).astype(BF16)
        pair[block(g, 4)] = update.reshape(4, 32, 128)

    repeat(8, forward)
    repeat(8, weigh)

    def plane_peer(n):
        return device(lax.div(n, 4), z, lax.div(lax.rem(n, 4), 2), lax.rem(n, 2), c)

    def deep_peer(n):
        return device(y, lax.div(n, 2), xh, xl, lax.rem(n, 2))

    def wa_part(n):
        return weight_grad.at[block(n, 64), :]

    def wa_copy(n):
        return remote(wa_part(n), weight_in.at[plane], wa_send.at[n], wa_recv.at[plane], plane_peer(n))

    def wb_copy(n):
        return remote(weight_sum, weight_far.at[deep], wb_send.at[n], wb_recv.at[deep], deep_peer(n))

    def wc_slot(n):
        return weight_all.at[block(n, 64), :]

    def wc_copy(n):
        return remote(weight_total, wc_slot(plane), wc_send.at[n], wc_recv.at[plane], plane_peer(n))

    start_all(16, wa_copy, plane)
    local(wa_part(plane), weight_in.at[plane], wa_recv.at[plane]).start()
    repeat(8, project)

    def pair_part(n):
        return pair.at[block(lax.div(n, 2), 8), block(lax.rem(n, 2), 16), :]

    def pair_slot(n):
        return pair_out.at[:, block(n, 16), :]

    def pair_copy(n):
        target = device(y, lax.div(n, 2) * 2 + xl, xh, c, lax.rem(n, 2))
        return remote(pair_part(n), pair_slot(z), pair_send.at[n], pair_recv.at[z], target)

    keeps_pair = jnp.logical_and(active, xl == c)
    own_pair = jnp.where(keeps_pair, zi * 2 + c, -1)
    start_all(8, pair_copy, own_pair)

    @pl.when(keeps_pair)
    def _():
        local(pair_part(zi * 2 + c), pair_slot(z), pair_recv.at[z]).start()

    def gl_copy():
        return remote(left_send, left_last, gl_send.at[0], gl_recv.at[0], partner)

    @pl.when(active)
    def _():
        repeat(8, lambda n: wait(gz_part(0), left_in.at[n], gz_recv.at[n]))
        away = left_in[0, 1 - xl].astype(F32)
        for n in range(1, 8):
            away = away + left_in[n, 1 - xl].astype(F32)
        left_send[...] = away.astype(BF16)
        gl_copy().start()
        here = left_in[0, xl].astype(F32)
        for n in range(1, 8):
            here = here + left_in[n, xl].astype(F32)
        left_last[...] = here.astype(BF16)

    repeat(16, lambda n: wait(right_in.at[n], right_in.at[n], gr_recv.at[n]))
    right_total = total(right_in, 16).astype(BF16).astype(F32)

    @pl.when(jnp.logical_not(active))
    def _():
        wait(left_last, left_last, gl_recv.at[0])

    left_total = left_last[...].astype(F32)

    sums = jnp.zeros((32, WIDE), F32)
    for h in range(2):
        picked = []
        for i in range(4):
            keep = mask[:, h * 4 + i : h * 4 + i + 1].astype(F32)
            tile = left_total[:, h * 128 : (h + 1) * 128]
            picked.append(
                jnp.concatenate(
                    [
                        jnp.where(lax.div(lane, 32) == i, tile, 0.0) * keep,
                        jnp.where(lax.rem(wide_lane, 8) == h * 4 + i, right_total, 0.0) * keep,
                    ],
                    axis=1,
                )
            )
        picked = jnp.concatenate(picked, axis=0).astype(BF16)
        gained = dot_nt(picked, maps[...]) * gain[...]
        whitened = white[h * 256 : (h + 1) * 256, :]
        stream_grad = spread[h * 256 : (h + 1) * 256, :1] * (
            gained
            - jnp.mean(gained, axis=-1, keepdims=True)
            - whitened * jnp.mean(gained * whitened, axis=-1, keepdims=True)
        )
        kind = lax.broadcasted_iota(jnp.int32, (32, 256), 0)
        hot = (kind == token_row[:, h * 256 : (h + 1) * 256]).astype(F32).astype(BF16)
        for piece in split(stream_grad, 2):
            sums = sums + dot(hot, piece)
    for n in range(TILES):
        table_part[n] = sums[(n // 2) * 8 : (n // 2 + 1) * 8, (n % 2) * 128 : (n % 2 + 1) * 128]

    def t_copy():
        return remote(table_part.at[pl.ds((1 - c) * 3, 3)], table_core, t_send.at[0], t_recv.at[0], other_core)

    at_x = xh * 2 + xl

    def tx_copy(n):
        return remote(
            table_x.at[at_x], table_x.at[at_x], tx_send.at[n], tx_recv.at[at_x],
            device(y, z, lax.div(n, 2), lax.rem(n, 2), c),
        )

    def ty_copy(n):
        return remote(table_y.at[y], table_y.at[y], ty_send.at[n], ty_recv.at[y], device(n, z, xh, xl, c))

    def tz_copy(n):
        return remote(table_z.at[z], table_z.at[z], tz_send.at[n], tz_recv.at[z], device(y, n, xh, xl, c))

    def half(at_c):
        return table_all.at[pl.ds(at_c * 3, 3)]

    def t_last():
        return remote(table_half, half(c), t_send.at[1], t_recv.at[1], other_core)

    def arrive(count, ref, sem, own):
        def step(n):
            @pl.when(n != own)
            def _():
                wait(ref.at[n], ref.at[n], sem.at[n])

        repeat(count, step)

    t_copy().start()
    wait(table_core, table_core, t_recv.at[0])
    table_x[at_x] = table_part[pl.ds(c * 3, 3)] + table_core[...]
    start_all(4, tx_copy, at_x)

    repeat(16, lambda n: wait(weight_in.at[n], weight_in.at[n], wa_recv.at[n]))
    weight_sum[...] = total(weight_in, 16).astype(BF16)
    start_all(16, wb_copy, deep)
    local(weight_sum, weight_far.at[deep], wb_recv.at[deep]).start()

    arrive(4, table_x, tx_recv, at_x)
    table_y[y] = total(table_x, 4)
    start_all(4, ty_copy, y)
    arrive(4, table_y, ty_recv, y)
    table_z[z] = total(table_y, 4)
    start_all(8, tz_copy, z)

    repeat(16, lambda n: wait(weight_far.at[n], weight_far.at[n], wb_recv.at[n]))
    weight_total[...] = total(weight_far, 16).astype(BF16)
    start_all(16, wc_copy, plane)
    local(weight_total, wc_slot(plane), wc_recv.at[plane]).start()

    arrive(8, table_z, tz_recv, z)
    summed = total(table_z, 8)
    table_half[...] = summed
    t_last().start()
    table_all[pl.ds(c * 3, 3)] = summed
    repeat(8, lambda n: wait(pair_slot(n), pair_slot(n), pair_recv.at[n]))
    wait(table_half, half(1 - c), t_recv.at[1])
    for n in range(TILES):
        high = min(8, table_out.shape[0] - (n // 2) * 8)
        table_out[(n // 2) * 8 : (n // 2) * 8 + high, (n % 2) * 128 : (n % 2 + 1) * 128] = table_all[n][:high]
    repeat(16, lambda n: wait(weight_total, wc_slot(n), wc_recv.at[n]))
    for t in range(2):
        for b in range(4):
            for a in range(4):
                at = ((t * 4 + b) * 4 + a) * 32
                weight_out[pl.ds(t * 16 + a * 4 + b, 32, stride=32), :] = weight_all[at : at + 32, :].astype(F32)

    sent_all(16, rm_copy, own_row)
    sent_all(16, cm_copy, own_column)
    sent_all(16, r_copy, own_column)
    sent_all(16, gr_copy, own_gr)
    sent_all(2, l3_copy, -1)
    sent_all(2, gx_copy, -1)
    sent_all(4, gz_copy, own_gz)
    sent_all(16, wa_copy, plane)
    sent_all(16, wb_copy, deep)
    sent_all(16, wc_copy, plane)
    sent_all(8, pair_copy, own_pair)
    sent_all(4, tx_copy, at_x)
    sent_all(4, ty_copy, y)
    sent_all(8, tz_copy, z)
    t_copy().wait_send()
    t_last().wait_send()

    @pl.when(active)
    def _():
        sent_all(8, cot_copy, z)
        sent_all(8, l2_copy, z)
        sent_all(8, l2_forward, z)
        gl_copy().wait_send()

    @pl.when(jnp.logical_not(active))
    def _():
        l1_copy().wait_send()


def shape(dims, dtype=BF16):
    return jax.ShapeDtypeStruct(dims, dtype)


def body(
    alignment_token_classes, deletions, alignment_mask, homolog_stack_values,
    letter_lookup_coefficients, gap_lookup_coefficients, standardize_gain, standardize_offset,
    first_factor_map, left_bias_vector, second_factor_map, right_bias_vector,
    output_weight_matrix, cotangent,
):
    core = lax.rem(lax.axis_index("seq"), 2)
    mask_turned = alignment_mask.astype(F32).T
    empty = jnp.zeros_like(mask_turned)
    mask_rows = jnp.concatenate(
        [jnp.where(core == 0, mask_turned, empty), jnp.where(core == 1, mask_turned, empty)], axis=1
    )
    steps = jnp.arange(32, dtype=jnp.int32).astype(F32)[:, None]
    gaps = (steps > 0).astype(F32) * gap_lookup_coefficients[0] + (
        2.0 / math.pi * jnp.arctan(steps / 3.0)
    ) * gap_lookup_coefficients[1]
    kinds = letter_lookup_coefficients.shape[0]
    letters = jnp.pad(letter_lookup_coefficients, ((0, 32 - kinds), (0, 0)))
    table = jnp.concatenate([letters, gaps, jnp.zeros((64, 256), F32)], axis=0)
    maps = jnp.concatenate([jnp.tile(first_factor_map, (1, 4)), jnp.repeat(second_factor_map, 8, axis=1)], axis=1)
    bias = jnp.concatenate([jnp.tile(left_bias_vector, 4), jnp.repeat(right_bias_vector, 8)])[None, :]
    weight = output_weight_matrix.reshape(32, 2, 4, 4, 128).transpose(1, 3, 2, 0, 4).reshape(1024, 128)
    inputs = [
        alignment_token_classes, deletions, alignment_mask, mask_rows, alignment_token_classes.T.reshape(1, 512),
        homolog_stack_values.transpose(1, 0, 2), table, standardize_gain[None, :], standardize_offset[None, :],
        maps, bias, weight, weight.T,
    ]
    vmem = pltpu.VMEM
    scratch = [vmem(value.shape, value.dtype) for value in inputs] + [
        vmem((512, 256), F32), vmem((512, 128), F32),
        vmem((ROWS, WIDE), BF16), vmem((ROWS, WIDE), BF16),
        vmem((4, 4, 8, 128), F32), vmem((4, 4, 8, 128), F32),
        vmem((4, 8, 2, 16, 128), BF16),
        vmem((4, ROWS, 1024), BF16), vmem((4, 4, ROWS, WIDE), BF16),
        vmem((256, 1024), BF16), vmem((1024, 256), BF16),
        vmem((1024, 128), F32), vmem((1024, 128), BF16),
        vmem((1024, 1024), BF16), vmem((1024, 1024), BF16),
        vmem((32, 32, 128), BF16),
        vmem((4, ROWS, 1024), BF16), vmem((2, ROWS, 1024), BF16), vmem((2, ROWS, 1024), BF16),
        vmem((8, 2, ROWS, WIDE), BF16), vmem((ROWS, WIDE), BF16), vmem((ROWS, WIDE), BF16),
        vmem((4, 4, ROWS, WIDE), BF16), vmem((256, 512), F32), vmem((16, ROWS, WIDE), BF16),
        vmem((1024, 128), BF16), vmem((16, 64, 128), BF16), vmem((64, 128), BF16),
        vmem((16, 64, 128), BF16), vmem((64, 128), BF16), vmem((1024, 128), BF16),
        vmem((TILES, 8, 128), F32), vmem((3, 8, 128), F32),
        vmem((4, 3, 8, 128), F32), vmem((4, 3, 8, 128), F32), vmem((8, 3, 8, 128), F32),
        vmem((3, 8, 128), F32), vmem((TILES, 8, 128), F32),
    ]
    sizes = [len(inputs), 16, 16, 16, 16, 8, 4, 1, 1, 16, 8, 2, 2, 16, 16]
    sizes += [2, 2, 4, 8, 1, 1, 16, 16, 8, 8, 16, 16, 16, 16, 16, 16, 2, 2, 4, 4, 4, 4, 8, 8]
    return pl.pallas_call(
        kernel,
        out_shape=[shape((8, 128, 128)), shape((1024, 128), F32), shape((kinds, 256), F32)],
        in_specs=[pl.BlockSpec(memory_space=pl.ANY)] * (len(inputs) + 1),
        out_specs=[pl.BlockSpec(memory_space=pltpu.VMEM)] * 3,
        scratch_shapes=scratch + [pltpu.SemaphoreType.DMA((size,)) for size in sizes],
        compiler_params=pltpu.CompilerParams(
            collective_id=0, has_side_effects=True, vmem_limit_bytes=48 * 1024 * 1024
        ),
        name="outer_product_mean",
    )(*inputs, cotangent.reshape(8, 4, 128, 128))


def solution(mesh):
    in_specs = (
        P("seq", "res"), P("seq", "res"), P("seq", "res"), P("seq", "res", None),
        P(), P(), P(), P(), P(), P(), P(), P(), P(),
        P("res", None, None),
    )
    out_specs = (P("res", "seq", None), P(), P())
    return jax.shard_map(body, mesh=mesh, in_specs=in_specs, out_specs=out_specs, check_vma=False)
```

```python
import math

import jax
import jax.numpy as jnp
import numpy as np
from jax import lax
from jax.experimental import pallas as pl
from jax.experimental.pallas import tpu as pltpu
from jax.sharding import PartitionSpec as P

EPSILON = 1e-05
MESH = pl.DeviceIdType.MESH
F32 = jnp.float32
BF16 = jnp.bfloat16

ROWS = 64
WIDE = 256
TILES = 6


def device(y, z, xh, xl, c):
    return (y * 16 + z * 2 + xh, xl * 2 + c)


def repeat(count, step):
    lax.fori_loop(0, count, lambda n, carried: (step(n), carried)[1], 0)


def remote(src, dst, send, recv, target):
    return pltpu.make_async_remote_copy(
        src_ref=src, dst_ref=dst, send_sem=send, recv_sem=recv, device_id=target, device_id_type=MESH
    )


def start_all(count, copy, own):
    def step(n):
        @pl.when(n != own)
        def _():
            copy(n).start()

    repeat(count, step)


def sent_all(count, copy, own):
    def step(n):
        @pl.when(n != own)
        def _():
            copy(n).wait_send()

    repeat(count, step)


def local(src, dst, sem):
    return pltpu.make_async_copy(src, dst, sem)


def lanes(dims):
    return lax.broadcasted_iota(jnp.int32, dims, len(dims) - 1)


def block(n, size):
    return pl.ds(pl.multiple_of(n * size, size), size)


def swap(parts, stride):
    lane = lanes(parts[0].shape)
    low = lax.rem(lax.div(lane, stride), 2) == 0
    high = lax.rem(lax.div(lane, 2 * stride), 2) == 0

    def pair(first, second, step, keep):
        return (
            jnp.where(keep, first, pltpu.roll(second, step, 1)),
            jnp.where(keep, pltpu.roll(first, 128 - step, 1), second),
        )

    a, b = pair(parts[0], parts[1], stride, low)
    c, d = pair(parts[2], parts[3], stride, low)
    a, c = pair(a, c, 2 * stride, high)
    b, d = pair(b, d, 2 * stride, high)
    return [a, b, c, d]


def dot(first, second):
    return jnp.dot(first, second, preferred_element_type=F32)


def dot_nt(first, second):
    return lax.dot_general(first, second, (((1,), (1,)), ((), ())), preferred_element_type=F32)


def split(value, count):
    pieces = []
    for _ in range(count):
        piece = value.astype(BF16)
        pieces.append(piece)
        value = value - piece.astype(F32)
    return pieces


def total(ref, count):
    value = ref[0].astype(F32)
    for n in range(1, count):
        value = value + ref[n].astype(F32)
    return value


def kernel(
    token_h, deletion_h, mask_h, stack_h, letters_h, gaps_h, steps_h, gain_h, offset_h,
    left_map_h, left_bias_h, right_map_h, right_bias_h, weight_h, cotangent,
    pair_out, weight_out, table_out,
    token, deletion, mask, stack_raw, letters, gaps, steps, gain, offset,
    left_map, left_bias, right_map, right_bias, weight_raw,
    square, turned, mask_rows, stack, table, maps, bias, weight_wide, weight, weight_turned, hot_turned,
    white, spread, left_own, right_own, row_masks, column_masks, cot_all, left_all, right_all,
    right_mat, product, counts, scaled, folded, grad_outer, pair,
    left_grad, left_core, left_sum, left_in, left_last, left_send, right_grad, right_part, right_in,
    weight_grad, weight_core, weight_half, weight_in, weight_sum, weight_far, weight_total, weight_all,
    table_part, table_core, table_x, table_y, table_z, table_half, table_all,
    in_sem, rm_send, rm_recv, cm_send, cm_recv, cot_send, cot_recv,
    l1_send, l1_recv, l2_send, l2_recv, l3_send, l3_recv, r_send, r_recv,
    gx_send, gx_recv, gz_send, gz_recv, gl_send, gl_recv, gr_send, gr_recv, pair_send, pair_recv,
    wh_send, wh_recv, wa_send, wa_recv, wb_send, wb_recv, wc_send, wc_recv,
    t_send, t_recv, tx_send, tx_recv, ty_send, ty_recv, tz_send, tz_recv,
):
    res = lax.axis_index("res")
    q = lax.axis_index("seq")
    y, z, xh = lax.div(res, 16), lax.rem(lax.div(res, 2), 8), lax.rem(res, 2)
    xl, c = lax.div(q, 2), lax.rem(q, 2)
    zi, parity = lax.div(z, 2), lax.rem(z, 2)
    active = parity == xl
    other_q = (1 - xl) * 2 + c
    plane = y * 4 + xh * 2 + xl
    deep = z * 2 + c
    column = lax.rem(y, 2) * 2 + xh
    own_row = jnp.where(active, deep, -1)
    own_column = jnp.where(lax.div(y, 2) == c, plane, -1)
    other_core = device(y, z, xh, xl, 1 - c)
    partner = device(y, z, xh, 1 - xl, c)

    def wait(src, dst, sem):
        local(src, dst, sem).wait()

    loads = [
        local(src, dst, in_sem.at[n])
        for n, (src, dst) in enumerate(
            [
                (token_h, token), (deletion_h, deletion), (mask_h, mask), (stack_h, stack_raw),
                (letters_h, letters), (gaps_h, gaps), (steps_h, steps), (gain_h, gain), (offset_h, offset),
                (left_map_h, left_map), (left_bias_h, left_bias), (right_map_h, right_map),
                (right_bias_h, right_bias), (weight_h, weight_raw),
            ]
        )
    ]
    for load in loads:
        load.start()

    barrier = pltpu.get_barrier_semaphore()

    def signal(target):
        pl.semaphore_signal(barrier, inc=1, device_id=target, device_id_type=MESH)

    def greet(n):
        @pl.when(n != z * 4 + q)
        def _():
            signal((y * 16 + lax.div(n, 4) * 2 + xh, lax.rem(n, 4)))

        @pl.when(n != (y * 2 + xh) * 4 + q)
        def _():
            signal((lax.div(n, 8) * 16 + z * 2 + lax.rem(lax.div(n, 4), 2), lax.rem(n, 4)))

    repeat(32, greet)

    def line_user(n):
        return device(y, lax.div(n, 2), xh, parity, lax.rem(n, 2))

    def plane_user(n):
        return device(lax.div(n, 4), z, lax.div(lax.rem(n, 4), 2), lax.rem(n, 2), lax.div(y, 2))

    def rm_copy(n):
        return remote(mask_rows, row_masks.at[zi, q], rm_send.at[n], rm_recv.at[zi * 4 + q], line_user(n))

    def cm_copy(n):
        return remote(mask_rows, column_masks.at[column, q], cm_send.at[n], cm_recv.at[column * 4 + q], plane_user(n))

    def cot_part(n):
        return cotangent.at[:, pl.ds(c * 2, 2), block(n, 16), :]

    def cot_copy(n):
        return remote(cot_part(n), cot_all.at[zi], cot_send.at[n], cot_recv.at[zi], device(y, n, xh, xl, c))

    def left_slot(at_q, at_z):
        return left_all.at[at_q, :, block(at_z, WIDE)]

    def l1_copy():
        return remote(left_own, left_slot(q, zi), l1_send.at[0], l1_recv.at[0], partner)

    def l2_copy(n):
        return remote(
            left_own, left_slot(q, zi), l2_send.at[n], l2_recv.at[zi * 2 + xl], device(y, n, xh, xl, c)
        )

    def l2_forward(n):
        return remote(
            left_slot(other_q, zi), left_slot(other_q, zi), l2_send.at[8 + n], l2_recv.at[zi * 2 + 1 - xl],
            device(y, n, xh, xl, c),
        )

    def l3_copy(n):
        at_q = n * 2 + c
        return remote(left_all.at[at_q], left_all.at[at_q], l3_send.at[n], l3_recv.at[n], other_core)

    def r_copy(n):
        return remote(right_own, right_all.at[column, q], r_send.at[n], r_recv.at[column * 4 + q], plane_user(n))

    for load in loads[:13]:
        load.wait()
    mask_value = mask[...].astype(F32)
    empty = jnp.zeros((8, ROWS), F32)
    mask_rows[...] = jnp.where(
        c == 0, jnp.concatenate([mask_value, empty], axis=1), jnp.concatenate([empty, mask_value], axis=1)
    )
    square[...] = jnp.zeros((128, 128), F32)
    square[0:8, 0:ROWS] = token[...].astype(F32)
    square[8:16, 0:ROWS] = deletion[...].astype(F32)
    square[16:24, 0:ROWS] = mask_value
    turned[...] = square[...].T[:ROWS]
    for n in range(2):
        stack[n] = stack_raw[:, :, n * 128 : (n + 1) * 128].astype(F32).reshape(512, 128)
    table[...] = jnp.zeros((128, WIDE), F32)
    table[: letters.shape[0], :] = letters[...]
    table[32:64, :] = steps[:, 0:1] * gaps[0:1, :] + steps[:, 1:2] * gaps[1:2, :]
    spread_left = (
        lax.rem(lax.broadcasted_iota(jnp.int32, (128, 32), 0), 32) == lanes((128, 32))
    ).astype(F32).astype(BF16)
    spread_right = (
        lax.div(lax.broadcasted_iota(jnp.int32, (WIDE, 32), 0), 8) == lanes((WIDE, 32))
    ).astype(F32).astype(BF16)
    maps[:128, :] = dot(spread_left, left_map[...]).astype(BF16)
    maps[128:, :] = dot(spread_right, right_map[...]).astype(BF16)
    bias[...] = jnp.concatenate(
        [
            sum(dot_nt(piece, spread_left) for piece in split(jnp.broadcast_to(left_bias[...], (8, 32)), 3)),
            sum(dot_nt(piece, spread_right) for piece in split(jnp.broadcast_to(right_bias[...], (8, 32)), 3)),
        ],
        axis=1,
    )
    lane = lanes((ROWS, 128))
    fine = lane.astype(F32)
    wide_lane = lanes((ROWS, WIDE))
    pieces = split(table[...], 3)
    right_value = jnp.zeros((ROWS, WIDE), F32)
    for h in range(2):
        hot = jnp.concatenate(
            [
                jnp.logical_or(fine == turned[:, i : i + 1], fine == turned[:, 8 + i : 9 + i] + 32.0).astype(F32)
                for i in range(h * 4, h * 4 + 4)
            ],
            axis=0,
        )
        hot_turned[h] = hot.T[:32].astype(BF16)
        hot = hot.astype(BF16)
        hidden = jnp.concatenate(
            [
                jnp.concatenate([stack[n, pl.ds(i, ROWS, stride=8), :] for i in range(h * 4, h * 4 + 4)], axis=0)
                for n in range(2)
            ],
            axis=1,
        ) + (dot(hot, pieces[0]) + dot(hot, pieces[1]) + dot(hot, pieces[2]))
        centered = hidden - jnp.mean(hidden, axis=-1, keepdims=True)
        variance = jnp.mean(centered * centered, axis=-1, keepdims=True)
        scale = lax.rsqrt(variance + EPSILON)
        whitened = centered * scale
        white[h * 256 : (h + 1) * 256, :] = whitened
        spread[h * 256 : (h + 1) * 256, :] = jnp.broadcast_to(scale, (256, 128))
        normed = (whitened * gain[...] + offset[...]).astype(BF16)
        rows = dot_nt(normed, maps[...]) + bias[:1, :]
        left_value = jnp.zeros((ROWS, 128), F32)
        for i in range(4):
            part = turned[:, 16 + h * 4 + i : 17 + h * 4 + i] * rows[i * ROWS : (i + 1) * ROWS, :]
            left_value = jnp.where(lax.div(lane, 32) == i, part[:, :128], left_value)
            right_value = jnp.where(lax.rem(wide_lane, 8) == h * 4 + i, part[:, 128:], right_value)
        left_own[:, h * 128 : (h + 1) * 128] = left_value.astype(BF16)
        if h == 0:
            pl.semaphore_wait(barrier, 62)
            start_all(16, rm_copy, own_row)
            start_all(16, cm_copy, own_column)

            @pl.when(active)
            def _():
                local(mask_rows, row_masks.at[zi, q], rm_recv.at[zi * 4 + q]).start()
                start_all(8, cot_copy, z)
                local(cot_part(z), cot_all.at[zi], cot_recv.at[zi]).start()

            @pl.when(lax.div(y, 2) == c)
            def _():
                local(mask_rows, column_masks.at[column, q], cm_recv.at[column * 4 + q]).start()

    right_own[...] = right_value.astype(BF16)

    @pl.when(jnp.logical_not(active))
    def _():
        l1_copy().start()

    @pl.when(active)
    def _():
        start_all(8, l2_copy, z)
        local(left_own, left_slot(q, zi), l2_recv.at[zi * 2 + xl]).start()

    start_all(16, r_copy, own_column)

    @pl.when(lax.div(y, 2) == c)
    def _():
        local(right_own, right_all.at[column, q], r_recv.at[column * 4 + q]).start()

    @pl.when(active)
    def _():
        wait(left_own, left_slot(other_q, zi), l1_recv.at[0])
        start_all(8, l2_forward, z)

    loads[13].wait()
    weight_wide[...] = weight_raw[...].astype(F32)
    for t in range(2):
        for b in range(4):
            for a in range(4):
                at = ((t * 4 + b) * 4 + a) * 32
                weight[at : at + 32, :] = weight_wide[pl.ds(t * 16 + a * 4 + b, 32, stride=32), :].astype(BF16)
    for t in range(8):
        weight_turned[:, t * 128 : (t + 1) * 128] = weight[t * 128 : (t + 1) * 128, :].astype(F32).T.astype(BF16)

    def arrive_masks(n):
        wait(mask_rows, row_masks.at[lax.div(n, 4), lax.rem(n, 4)], rm_recv.at[n])
        wait(mask_rows, column_masks.at[lax.div(n, 4), lax.rem(n, 4)], cm_recv.at[n])

    repeat(16, arrive_masks)
    column_mask = jnp.concatenate(
        [
            jnp.concatenate([column_masks[b, 2 * h] + column_masks[b, 2 * h + 1] for h in range(2)], axis=1)
            for b in range(4)
        ],
        axis=0,
    )
    for i in range(32):
        row = jnp.concatenate(
            [
                row_masks[i // 8, 2 * h, i % 8 : i % 8 + 1, :] + row_masks[i // 8, 2 * h + 1, i % 8 : i % 8 + 1, :]
                for h in range(2)
            ],
            axis=1,
        )
        product[i * 32 : (i + 1) * 32, :] = (row * column_mask).astype(BF16)
    counts[...] = dot(product[...], jnp.ones((256, 128), BF16))
    repeat(4, lambda n: wait(cot_part(n), cot_all.at[n], cot_recv.at[n]))
    for n in range(4):
        cot = cot_all[n].astype(F32).reshape(256, 128)
        scaled[n * 256 : (n + 1) * 256, :] = (cot / counts[n * 256 : (n + 1) * 256, :]).astype(BF16)

    def backward(g):
        span = block(g, 256)
        scaled_part = scaled[span, :]
        for t in range(8):
            grad = dot_nt(weight[t * 128 : (t + 1) * 128, :], scaled_part)
            for half in range(2):
                lane_part = grad[:, half * 128 : (half + 1) * 128]
                parts = swap([lane_part[a * 32 : (a + 1) * 32, :] for a in range(4)], 32)
                for i, part in enumerate(parts):
                    at = pl.ds(pl.multiple_of(g * 256 + half * 128 + i * 32, 32), 32)
                    grad_outer[at, t * 128 : (t + 1) * 128] = part.astype(BF16)

    repeat(4, backward)

    forwarded = jnp.where(active, zi * 2 + 1 - xl, -1)

    def arrive_left(n):
        @pl.when(n != forwarded)
        def _():
            wait(left_own, left_slot(lax.rem(n, 2) * 2 + c, lax.div(n, 2)), l2_recv.at[n])

    repeat(8, arrive_left)
    start_all(2, l3_copy, -1)
    repeat(16, lambda n: wait(right_own, right_all.at[lax.div(n, 4), lax.rem(n, 4)], r_recv.at[n]))
    for at_q in range(4):
        rows = slice(at_q * ROWS, (at_q + 1) * ROWS)
        for t in range(2):
            parts = [right_all[b, at_q, :, t * 128 : (t + 1) * 128].astype(F32) for b in range(4)]
            for b, part in enumerate(swap(parts, 8)):
                right_mat[rows, (t * 4 + b) * 128 : (t * 4 + b + 1) * 128] = part.astype(BF16)

    def left_step(g):
        span = block(g, 256)
        part = dot_nt(right_mat[...], grad_outer[span, :]).astype(BF16)
        for at_q in range(4):
            left_grad[at_q, :, span] = part[at_q * ROWS : (at_q + 1) * ROWS, :]

    repeat(4, left_step)

    def gx_copy(n):
        return remote(left_grad.at[n * 2 + 1 - c], left_core.at[n], gx_send.at[n], gx_recv.at[n], other_core)

    start_all(2, gx_copy, -1)
    repeat(2, lambda n: wait(left_all.at[n * 2 + 1 - c], left_all.at[n * 2 + 1 - c], l3_recv.at[n]))

    def right_step(t):
        for b in range(2):
            right_part[:, b * 256 : (b + 1) * 256] = dot(
                left_all[...].reshape(256, 1024), grad_outer[:, t * 512 + b * 256 : t * 512 + (b + 1) * 256]
            )
        for at_q in range(4):
            rows = slice(at_q * ROWS, (at_q + 1) * ROWS)
            parts = swap([right_part[rows, b * 128 : (b + 1) * 128] for b in range(4)], 8)
            for b, part in enumerate(parts):
                right_grad[b, at_q, :, t * 128 : (t + 1) * 128] = part.astype(BF16)

    right_step(0)

    def gz_part(n):
        return left_sum.at[:, :, block(n, WIDE)]

    def gz_copy(n):
        return remote(
            gz_part(n), left_in.at[z], gz_send.at[n], gz_recv.at[z], device(y, n * 2 + xl, xh, xl, c)
        )

    own_gz = jnp.where(active, zi, -1)
    for n in range(2):
        wait(left_core.at[n], left_core.at[n], gx_recv.at[n])
        left_sum[n] = (left_grad[n * 2 + c].astype(F32) + left_core[n].astype(F32)).astype(BF16)
    start_all(4, gz_copy, own_gz)

    @pl.when(active)
    def _():
        local(gz_part(zi), left_in.at[z], gz_recv.at[z]).start()

    right_step(1)

    def gr_part(n):
        return right_grad.at[lax.div(n, 4), lax.rem(n, 4)]

    def gr_copy(n):
        target = device(c * 2 + lax.div(n, 8), z, lax.rem(lax.div(n, 4), 2), lax.div(lax.rem(n, 4), 2), lax.rem(n, 2))
        return remote(gr_part(n), right_in.at[plane], gr_send.at[n], gr_recv.at[plane], target)

    own_gr = jnp.where(lax.div(y, 2) == c, column * 4 + q, -1)
    start_all(16, gr_copy, own_gr)

    @pl.when(lax.div(y, 2) == c)
    def _():
        local(gr_part(column * 4 + q), right_in.at[plane], gr_recv.at[plane]).start()

    def forward(g):
        span = block(g, 128)
        lead = left_all[:, :, span].reshape(256, 128).astype(F32).T.astype(BF16)
        for t in range(8):
            outer = dot(lead, right_mat[:, t * 128 : (t + 1) * 128])
            parts = swap([outer[i * 32 : (i + 1) * 32, :] for i in range(4)], 32)
            for a, part in enumerate(parts):
                folded[(t * 4 + a) * 32 : (t * 4 + a + 1) * 32, span] = part.astype(BF16)

    def weigh(g):
        span = block(g, 128)
        weight_grad[span, :] = dot(folded[span, :], scaled[...])

    def project(g):
        span = block(g, 128)
        value = dot(weight_turned[...], folded[:, span])
        update = (value.T / counts[span, :]).astype(BF16)
        pair[block(g, 4)] = update.reshape(4, 32, 128)

    repeat(8, forward)
    repeat(8, weigh)

    def plane_peer(n):
        return device(lax.div(n, 4), z, lax.div(lax.rem(n, 4), 2), lax.rem(n, 2), c)

    def line_peer(n):
        return device(y, n, xh, xl, c)

    def wh_copy():
        return remote(weight_grad.at[block(1 - c, 512), :], weight_core, wh_send.at[0], wh_recv.at[0], other_core)

    def wa_part(n):
        return weight_half.at[block(n, 32), :]

    def wa_copy(n):
        return remote(wa_part(n), weight_in.at[plane], wa_send.at[n], wa_recv.at[plane], plane_peer(n))

    def wb_copy(n):
        return remote(weight_sum, weight_far.at[z], wb_send.at[n], wb_recv.at[z], line_peer(n))

    def wc_slot(n):
        return weight_all.at[c, block(n, 32), :]

    def wc_copy(n):
        return remote(weight_total, wc_slot(plane), wc_send.at[n], wc_recv.at[plane], plane_peer(n))

    def wd_copy():
        return remote(weight_all.at[c], weight_all.at[c], wh_send.at[1], wh_recv.at[1], other_core)

    wh_copy().start()
    repeat(8, project)
    wait(weight_core, weight_core, wh_recv.at[0])
    weight_half[...] = (weight_grad[block(c, 512), :] + weight_core[...]).astype(BF16)
    start_all(16, wa_copy, plane)
    local(wa_part(plane), weight_in.at[plane], wa_recv.at[plane]).start()

    def pair_part(n):
        return pair.at[block(lax.div(n, 2), 8), block(lax.rem(n, 2), 16), :]

    def pair_slot(n):
        return pair_out.at[:, block(n, 16), :]

    def pair_copy(n):
        target = device(y, lax.div(n, 2) * 2 + xl, xh, c, lax.rem(n, 2))
        return remote(pair_part(n), pair_slot(z), pair_send.at[n], pair_recv.at[z], target)

    keeps_pair = jnp.logical_and(active, xl == c)
    own_pair = jnp.where(keeps_pair, zi * 2 + c, -1)
    start_all(8, pair_copy, own_pair)

    @pl.when(keeps_pair)
    def _():
        local(pair_part(zi * 2 + c), pair_slot(z), pair_recv.at[z]).start()

    def gl_copy():
        return remote(left_send, left_last, gl_send.at[0], gl_recv.at[0], partner)

    @pl.when(active)
    def _():
        repeat(8, lambda n: wait(gz_part(0), left_in.at[n], gz_recv.at[n]))
        away = left_in[0, 1 - xl].astype(F32)
        for n in range(1, 8):
            away = away + left_in[n, 1 - xl].astype(F32)
        left_send[...] = away.astype(BF16)
        gl_copy().start()
        here = left_in[0, xl].astype(F32)
        for n in range(1, 8):
            here = here + left_in[n, xl].astype(F32)
        left_last[...] = here.astype(BF16)

    repeat(16, lambda n: wait(right_in.at[n], right_in.at[n], gr_recv.at[n]))
    right_total = total(right_in, 16).astype(BF16).astype(F32)

    @pl.when(jnp.logical_not(active))
    def _():
        wait(left_last, left_last, gl_recv.at[0])

    left_total = left_last[...].astype(F32)

    repeat(16, lambda n: wait(weight_in.at[n], weight_in.at[n], wa_recv.at[n]))
    weight_sum[...] = total(weight_in, 16).astype(BF16)
    start_all(8, wb_copy, z)
    local(weight_sum, weight_far.at[z], wb_recv.at[z]).start()

    sums = jnp.zeros((32, WIDE), F32)
    for h in range(2):
        picked = []
        for i in range(4):
            keep = turned[:, 16 + h * 4 + i : 17 + h * 4 + i]
            tile = left_total[:, h * 128 : (h + 1) * 128]
            picked.append(
                jnp.concatenate(
                    [
                        jnp.where(lax.div(lane, 32) == i, tile, 0.0) * keep,
                        jnp.where(lax.rem(wide_lane, 8) == h * 4 + i, right_total, 0.0) * keep,
                    ],
                    axis=1,
                )
            )
        picked = jnp.concatenate(picked, axis=0).astype(BF16)
        gained = dot(picked, maps[...]) * gain[...]
        whitened = white[h * 256 : (h + 1) * 256, :]
        stream_grad = spread[h * 256 : (h + 1) * 256, :1] * (
            gained
            - jnp.mean(gained, axis=-1, keepdims=True)
            - whitened * jnp.mean(gained * whitened, axis=-1, keepdims=True)
        )
        for piece in split(stream_grad, 2):
            sums = sums + dot(hot_turned[h], piece)
    for n in range(TILES):
        table_part[n] = sums[(n // 2) * 8 : (n // 2 + 1) * 8, (n % 2) * 128 : (n % 2 + 1) * 128]

    def t_copy():
        return remote(table_part.at[pl.ds((1 - c) * 3, 3)], table_core, t_send.at[0], t_recv.at[0], other_core)

    at_x = xh * 2 + xl

    def tx_copy(n):
        return remote(
            table_x.at[at_x], table_x.at[at_x], tx_send.at[n], tx_recv.at[at_x],
            device(y, z, lax.div(n, 2), lax.rem(n, 2), c),
        )

    def ty_copy(n):
        return remote(table_y.at[y], table_y.at[y], ty_send.at[n], ty_recv.at[y], device(n, z, xh, xl, c))

    def tz_copy(n):
        return remote(table_z.at[z], table_z.at[z], tz_send.at[n], tz_recv.at[z], device(y, n, xh, xl, c))

    def half(at_c):
        return table_all.at[pl.ds(at_c * 3, 3)]

    def t_last():
        return remote(table_half, half(c), t_send.at[1], t_recv.at[1], other_core)

    def arrive(count, ref, sem, own):
        def step(n):
            @pl.when(n != own)
            def _():
                wait(ref.at[n], ref.at[n], sem.at[n])

        repeat(count, step)

    t_copy().start()
    wait(table_core, table_core, t_recv.at[0])
    table_x[at_x] = table_part[pl.ds(c * 3, 3)] + table_core[...]
    start_all(4, tx_copy, at_x)

    repeat(8, lambda n: wait(weight_far.at[n], weight_far.at[n], wb_recv.at[n]))
    weight_total[...] = total(weight_far, 8).astype(BF16)
    start_all(16, wc_copy, plane)
    local(weight_total, wc_slot(plane), wc_recv.at[plane]).start()

    arrive(4, table_x, tx_recv, at_x)
    table_y[y] = total(table_x, 4)
    start_all(4, ty_copy, y)
    arrive(4, table_y, ty_recv, y)
    table_z[z] = total(table_y, 4)
    start_all(8, tz_copy, z)

    repeat(16, lambda n: wait(weight_total, wc_slot(n), wc_recv.at[n]))
    wd_copy().start()

    arrive(8, table_z, tz_recv, z)
    summed = total(table_z, 8)
    table_half[...] = summed
    t_last().start()
    table_all[pl.ds(c * 3, 3)] = summed
    repeat(8, lambda n: wait(pair_slot(n), pair_slot(n), pair_recv.at[n]))
    wait(table_half, half(1 - c), t_recv.at[1])
    for n in range(TILES):
        high = min(8, table_out.shape[0] - (n // 2) * 8)
        table_out[(n // 2) * 8 : (n // 2) * 8 + high, (n % 2) * 128 : (n % 2 + 1) * 128] = table_all[n][:high]
    wait(weight_all.at[1 - c], weight_all.at[1 - c], wh_recv.at[1])
    for t in range(2):
        for b in range(4):
            for a in range(4):
                at = ((t * 4 + b) * 4 + a) * 32
                weight_out[pl.ds(t * 16 + a * 4 + b, 32, stride=32), :] = weight_all[at // 512, at % 512 : at % 512 + 32, :].astype(F32)

    sent_all(16, rm_copy, own_row)
    sent_all(16, cm_copy, own_column)
    sent_all(16, r_copy, own_column)
    sent_all(16, gr_copy, own_gr)
    sent_all(2, l3_copy, -1)
    sent_all(2, gx_copy, -1)
    sent_all(4, gz_copy, own_gz)
    sent_all(16, wa_copy, plane)
    sent_all(8, wb_copy, z)
    wh_copy().wait_send()
    wd_copy().wait_send()
    sent_all(16, wc_copy, plane)
    sent_all(8, pair_copy, own_pair)
    sent_all(4, tx_copy, at_x)
    sent_all(4, ty_copy, y)
    sent_all(8, tz_copy, z)
    t_copy().wait_send()
    t_last().wait_send()

    @pl.when(active)
    def _():
        sent_all(8, cot_copy, z)
        sent_all(8, l2_copy, z)
        sent_all(8, l2_forward, z)
        gl_copy().wait_send()

    @pl.when(jnp.logical_not(active))
    def _():
        l1_copy().wait_send()


def shape(dims, dtype=BF16):
    return jax.ShapeDtypeStruct(dims, dtype)


def body(
    alignment_token_classes, deletions, alignment_mask, homolog_stack_values,
    letter_lookup_coefficients, gap_lookup_coefficients, standardize_gain, standardize_offset,
    first_factor_map, left_bias_vector, second_factor_map, right_bias_vector,
    output_weight_matrix, cotangent,
):
    kinds = letter_lookup_coefficients.shape[0]
    grades = np.arange(32, dtype=np.float32)
    steps = jnp.asarray(
        np.stack([(grades > 0).astype(np.float32), (2.0 / math.pi * np.arctan(grades / 3.0)).astype(np.float32)], 1)
    )
    inputs = [
        alignment_token_classes.T, deletions.T, alignment_mask.T, homolog_stack_values,
        letter_lookup_coefficients, gap_lookup_coefficients, steps,
        standardize_gain.reshape(1, 256), standardize_offset.reshape(1, 256),
        first_factor_map.T, left_bias_vector.reshape(1, 32), second_factor_map.T, right_bias_vector.reshape(1, 32),
        output_weight_matrix,
    ]
    vmem = pltpu.VMEM
    scratch = [vmem(value.shape, value.dtype) for value in inputs] + [
        vmem((128, 128), F32), vmem((ROWS, 128), F32), vmem((8, 128), F32),
        vmem((2, 512, 128), F32),
        vmem((128, WIDE), F32), vmem((384, 256), BF16), vmem((8, 384), F32),
        vmem((1024, 128), F32), vmem((1024, 128), BF16), vmem((128, 1024), BF16),
        vmem((2, 32, 256), BF16),
        vmem((512, 256), F32), vmem((512, 128), F32),
        vmem((ROWS, WIDE), BF16), vmem((ROWS, WIDE), BF16),
        vmem((4, 4, 8, 128), F32), vmem((4, 4, 8, 128), F32),
        vmem((4, 8, 2, 16, 128), BF16),
        vmem((4, ROWS, 1024), BF16), vmem((4, 4, ROWS, WIDE), BF16),
        vmem((256, 1024), BF16), vmem((1024, 256), BF16),
        vmem((1024, 128), F32), vmem((1024, 128), BF16),
        vmem((1024, 1024), BF16), vmem((1024, 1024), BF16),
        vmem((32, 32, 128), BF16),
        vmem((4, ROWS, 1024), BF16), vmem((2, ROWS, 1024), BF16), vmem((2, ROWS, 1024), BF16),
        vmem((8, 2, ROWS, WIDE), BF16), vmem((ROWS, WIDE), BF16), vmem((ROWS, WIDE), BF16),
        vmem((4, 4, ROWS, WIDE), BF16), vmem((256, 512), F32), vmem((16, ROWS, WIDE), BF16),
        vmem((1024, 128), F32), vmem((512, 128), F32), vmem((512, 128), BF16),
        vmem((16, 32, 128), BF16), vmem((32, 128), BF16),
        vmem((8, 32, 128), BF16), vmem((32, 128), BF16), vmem((2, 512, 128), BF16),
        vmem((TILES, 8, 128), F32), vmem((3, 8, 128), F32),
        vmem((4, 3, 8, 128), F32), vmem((4, 3, 8, 128), F32), vmem((8, 3, 8, 128), F32),
        vmem((3, 8, 128), F32), vmem((TILES, 8, 128), F32),
    ]
    sizes = [len(inputs), 16, 16, 16, 16, 8, 4, 1, 1, 16, 8, 2, 2, 16, 16]
    sizes += [2, 2, 4, 8, 1, 1, 16, 16, 8, 8, 2, 2, 16, 16, 8, 8, 16, 16, 2, 2, 4, 4, 4, 4, 8, 8]
    results = pl.pallas_call(
        kernel,
        out_shape=[shape((8, 128, 128)), shape((1024, 128), F32), shape((kinds, 256), F32)],
        in_specs=[pl.BlockSpec(memory_space=pl.ANY)] * (len(inputs) + 1),
        out_specs=[pl.BlockSpec(memory_space=pltpu.VMEM)] * 3,
        scratch_shapes=scratch + [pltpu.SemaphoreType.DMA((size,)) for size in sizes],
        compiler_params=pltpu.CompilerParams(
            collective_id=0, has_side_effects=True, vmem_limit_bytes=60 * 1024 * 1024
        ),
        name="outer_product_mean",
    )(*inputs, cotangent.reshape(8, 4, 128, 128))
    return pl.pallas_call(
        hand_over,
        out_shape=[shape(value.shape, value.dtype) for value in results],
        in_specs=[pl.BlockSpec(memory_space=pl.ANY)] * 3,
        out_specs=[pl.BlockSpec(memory_space=pl.ANY)] * 3,
        scratch_shapes=[vmem(value.shape, value.dtype) for value in results] + [pltpu.SemaphoreType.DMA((3,))],
        name="hand_over",
    )(*results)


def hand_over(pair, weight, table, pair_out, weight_out, table_out, pair_here, weight_here, table_here, sem):
    here = [pair_here, weight_here, table_here]
    arrive = [local(src, dst, sem.at[n]) for n, (src, dst) in enumerate(zip([pair, weight, table], here))]
    leave = [local(src, dst, sem.at[n]) for n, (src, dst) in enumerate(zip(here, [pair_out, weight_out, table_out]))]
    for copy in arrive:
        copy.start()
    for first, second in zip(arrive, leave):
        first.wait()
        second.start()
    for copy in leave:
        copy.wait()


def solution(mesh):
    in_specs = (
        P("seq", "res"), P("seq", "res"), P("seq", "res"), P("seq", "res", None),
        P(), P(), P(), P(), P(), P(), P(), P(), P(),
        P("res", None, None),
    )
    out_specs = (P("res", "seq", None), P(), P())
    return jax.shard_map(body, mesh=mesh, in_specs=in_specs, out_specs=out_specs, check_vma=False)
```

```python
import math

import jax
import jax.numpy as jnp
import numpy as np
from jax import lax
from jax.experimental import pallas as pl
from jax.experimental.pallas import tpu as pltpu
from jax.sharding import PartitionSpec as P

EPSILON = 1e-05
MESH = pl.DeviceIdType.MESH
F32 = jnp.float32
BF16 = jnp.bfloat16

ROWS = 64
WIDE = 256
TILES = 6


def device(y, z, xh, xl, c):
    return (y * 16 + z * 2 + xh, xl * 2 + c)


def repeat(count, step):
    lax.fori_loop(0, count, lambda n, carried: (step(n), carried)[1], 0)


def remote(src, dst, send, recv, target):
    return pltpu.make_async_remote_copy(
        src_ref=src, dst_ref=dst, send_sem=send, recv_sem=recv, device_id=target, device_id_type=MESH
    )


def start_all(count, copy, own):
    def step(n):
        @pl.when(n != own)
        def _():
            copy(n).start()

    repeat(count, step)


def sent_all(count, copy, own):
    def step(n):
        @pl.when(n != own)
        def _():
            copy(n).wait_send()

    repeat(count, step)


def local(src, dst, sem):
    return pltpu.make_async_copy(src, dst, sem)


def lanes(dims):
    return lax.broadcasted_iota(jnp.int32, dims, len(dims) - 1)


def block(n, size):
    return pl.ds(pl.multiple_of(n * size, size), size)


def swap(parts, stride):
    lane = lanes(parts[0].shape)
    low = lax.rem(lax.div(lane, stride), 2) == 0
    high = lax.rem(lax.div(lane, 2 * stride), 2) == 0

    def pair(first, second, step, keep):
        return (
            jnp.where(keep, first, pltpu.roll(second, step, 1)),
            jnp.where(keep, pltpu.roll(first, 128 - step, 1), second),
        )

    a, b = pair(parts[0], parts[1], stride, low)
    c, d = pair(parts[2], parts[3], stride, low)
    a, c = pair(a, c, 2 * stride, high)
    b, d = pair(b, d, 2 * stride, high)
    return [a, b, c, d]


def dot(first, second):
    return jnp.dot(first, second, preferred_element_type=F32)


def dot_nt(first, second):
    return lax.dot_general(first, second, (((1,), (1,)), ((), ())), preferred_element_type=F32)


def split(value, count):
    pieces = []
    for _ in range(count):
        piece = value.astype(BF16)
        pieces.append(piece)
        value = value - piece.astype(F32)
    return pieces


def total(ref, count):
    value = ref[0].astype(F32)
    for n in range(1, count):
        value = value + ref[n].astype(F32)
    return value


def kernel(
    token_h, deletion_h, mask_h, stack_h, letters_h, gaps_h, steps_h, gain_h, offset_h,
    left_map_h, left_bias_h, right_map_h, right_bias_h, weight_h, cotangent,
    pair_out, weight_out, table_out,
    token, deletion, mask, stack_raw, letters, gaps, steps, gain, offset,
    left_map, left_bias, right_map, right_bias, weight_raw, cot_raw, cot_stage,
    square, turned, mask_rows, stack, table, maps, bias, weight_wide, weight, weight_turned, hot_turned,
    white, spread, left_own, right_own, row_masks, column_masks, cot_all, left_all, right_all,
    right_mat, product, counts, scaled, folded, grad_outer, pair, pair_in,
    right_grad, right_part, right_core, right_sum, right_in, right_last, right_send, left_grad, left_in,
    weight_grad, weight_core, weight_half, weight_in, weight_sum, weight_far, weight_total, weight_all,
    table_part, table_core, table_p, table_z, table_half, table_all,
    in_sem, rm_send, rm_recv, cm_send, cm_recv, cot_send, cot_recv,
    r1_send, r1_recv, r2_send, r2_recv, r3_send, r3_recv, l_send, l_recv,
    gx_send, gx_recv, gz_send, gz_recv, gf_send, gf_recv, gl_send, gl_recv, pair_send, pair_recv,
    wh_send, wh_recv, wa_send, wa_recv, wb_send, wb_recv, wc_send, wc_recv,
    t_send, t_recv, tp_send, tp_recv, tz_send, tz_recv,
):
    res = lax.axis_index("res")
    q = lax.axis_index("seq")
    y, z, xh = lax.div(res, 16), lax.rem(lax.div(res, 2), 8), lax.rem(res, 2)
    xl, c = lax.div(q, 2), lax.rem(q, 2)
    zi, parity = lax.div(z, 2), lax.rem(z, 2)
    active = parity == xl
    inside = lax.div(y, 2) == c
    other_q = (1 - xl) * 2 + c
    plane = y * 4 + xh * 2 + xl
    band = lax.rem(y, 2) * 2 + xh
    own_column = jnp.where(active, z * 2 + c, -1)
    own_row = jnp.where(inside, plane, -1)
    other_core = device(y, z, xh, xl, 1 - c)
    partner = device(y, z, xh, 1 - xl, c)

    def wait(src, dst, sem):
        local(src, dst, sem).wait()

    loads = [
        local(src, dst, in_sem.at[n])
        for n, (src, dst) in enumerate(
            [
                (token_h, token), (deletion_h, deletion), (mask_h, mask), (stack_h, stack_raw),
                (letters_h, letters), (gaps_h, gaps), (steps_h, steps), (gain_h, gain), (offset_h, offset),
                (left_map_h, left_map), (left_bias_h, left_bias), (right_map_h, right_map),
                (right_bias_h, right_bias), (weight_h, weight_raw), (cotangent.at[:, :, xl], cot_raw),
            ]
        )
    ]
    for load in loads:
        load.start()

    barrier = pltpu.get_barrier_semaphore()

    def signal(target):
        pl.semaphore_signal(barrier, inc=1, device_id=target, device_id_type=MESH)

    def greet(n):
        @pl.when(n != z * 4 + q)
        def _():
            signal((y * 16 + lax.div(n, 4) * 2 + xh, lax.rem(n, 4)))

        @pl.when(n != (y * 2 + xh) * 4 + q)
        def _():
            signal((lax.div(n, 8) * 16 + z * 2 + lax.rem(lax.div(n, 4), 2), lax.rem(n, 4)))

    repeat(32, greet)

    def line_user(n):
        return device(y, lax.div(n, 2), xh, parity, lax.rem(n, 2))

    def plane_user(n):
        return device(lax.div(n, 4), z, lax.div(lax.rem(n, 4), 2), lax.rem(n, 2), lax.div(y, 2))

    def rm_copy(n):
        return remote(mask_rows, row_masks.at[band, q], rm_send.at[n], rm_recv.at[band * 4 + q], plane_user(n))

    def cm_copy(n):
        return remote(mask_rows, column_masks.at[zi, q], cm_send.at[n], cm_recv.at[zi * 4 + q], line_user(n))

    def cot_copy(n):
        return remote(cot_stage.at[n], cot_all.at[band], cot_send.at[n], cot_recv.at[band], device(n, z, c, xl, lax.div(y, 2)))

    own_cot = jnp.where(jnp.logical_and(inside, xh == c), y, -1)

    def left_slot(at_band, at_q):
        return left_all.at[at_q, :, block(at_band, WIDE)]

    def l_copy(n):
        return remote(left_own, left_slot(band, q), l_send.at[n], l_recv.at[band * 4 + q], plane_user(n))

    def r1_copy():
        return remote(right_own, right_all.at[zi, q], r1_send.at[0], r1_recv.at[0], partner)

    def r2_copy(n):
        return remote(
            right_own, right_all.at[zi, q], r2_send.at[n], r2_recv.at[zi * 2 + xl], device(y, n, xh, xl, c)
        )

    def r2_forward(n):
        return remote(
            right_all.at[zi, other_q], right_all.at[zi, other_q], r2_send.at[8 + n], r2_recv.at[zi * 2 + 1 - xl],
            device(y, n, xh, xl, c),
        )

    def r3_copy(n):
        at_q = n * 2 + c
        return remote(right_all.at[:, at_q], right_all.at[:, at_q], r3_send.at[n], r3_recv.at[n], other_core)

    for load in loads[:13]:
        load.wait()
    mask_value = mask[...].astype(F32)
    empty = jnp.zeros((8, ROWS), F32)
    mask_rows[...] = jnp.where(
        c == 0, jnp.concatenate([mask_value, empty], axis=1), jnp.concatenate([empty, mask_value], axis=1)
    )
    square[...] = jnp.zeros((128, 128), F32)
    square[0:8, 0:ROWS] = token[...].astype(F32)
    square[8:16, 0:ROWS] = deletion[...].astype(F32)
    square[16:24, 0:ROWS] = mask_value
    turned[...] = square[...].T[:ROWS]
    for n in range(2):
        stack[n] = stack_raw[:, :, n * 128 : (n + 1) * 128].astype(F32).reshape(512, 128)
    table[...] = jnp.zeros((128, WIDE), F32)
    table[: letters.shape[0], :] = letters[...]
    table[32:64, :] = steps[:, 0:1] * gaps[0:1, :] + steps[:, 1:2] * gaps[1:2, :]
    spread_left = (
        lax.rem(lax.broadcasted_iota(jnp.int32, (128, 32), 0), 32) == lanes((128, 32))
    ).astype(F32).astype(BF16)
    spread_right = (
        lax.div(lax.broadcasted_iota(jnp.int32, (WIDE, 32), 0), 8) == lanes((WIDE, 32))
    ).astype(F32).astype(BF16)
    maps[:128, :] = dot(spread_left, left_map[...]).astype(BF16)
    maps[128:, :] = dot(spread_right, right_map[...]).astype(BF16)
    bias[...] = jnp.concatenate(
        [
            sum(dot_nt(piece, spread_left) for piece in split(jnp.broadcast_to(left_bias[...], (8, 32)), 3)),
            sum(dot_nt(piece, spread_right) for piece in split(jnp.broadcast_to(right_bias[...], (8, 32)), 3)),
        ],
        axis=1,
    )
    loads[14].wait()
    for n in range(4):
        strip = cot_raw[:, n * 4 : n * 4 + 4].astype(F32)
        strip = jnp.where(c == 0, strip[:, :, :8, :], strip[:, :, 8:, :])
        cot_stage[n] = strip.reshape(8, 32, 128).astype(BF16)
    lane = lanes((ROWS, 128))
    fine = lane.astype(F32)
    wide_lane = lanes((ROWS, WIDE))
    pieces = split(table[...], 3)
    right_value = jnp.zeros((ROWS, WIDE), F32)
    for h in range(2):
        hot = jnp.concatenate(
            [
                jnp.logical_or(fine == turned[:, i : i + 1], fine == turned[:, 8 + i : 9 + i] + 32.0).astype(F32)
                for i in range(h * 4, h * 4 + 4)
            ],
            axis=0,
        )
        hot_turned[h] = hot.T[:32].astype(BF16)
        hot = hot.astype(BF16)
        hidden = jnp.concatenate(
            [
                jnp.concatenate([stack[n, pl.ds(i, ROWS, stride=8), :] for i in range(h * 4, h * 4 + 4)], axis=0)
                for n in range(2)
            ],
            axis=1,
        ) + (dot(hot, pieces[0]) + dot(hot, pieces[1]) + dot(hot, pieces[2]))
        centered = hidden - jnp.mean(hidden, axis=-1, keepdims=True)
        variance = jnp.mean(centered * centered, axis=-1, keepdims=True)
        scale = lax.rsqrt(variance + EPSILON)
        whitened = centered * scale
        white[h * 256 : (h + 1) * 256, :] = whitened
        spread[h * 256 : (h + 1) * 256, :] = jnp.broadcast_to(scale, (256, 128))
        normed = (whitened * gain[...] + offset[...]).astype(BF16)
        rows = dot_nt(normed, maps[...]) + bias[:1, :]
        left_value = jnp.zeros((ROWS, 128), F32)
        for i in range(4):
            part = turned[:, 16 + h * 4 + i : 17 + h * 4 + i] * rows[i * ROWS : (i + 1) * ROWS, :]
            left_value = jnp.where(lax.div(lane, 32) == i, part[:, :128], left_value)
            right_value = jnp.where(lax.rem(wide_lane, 8) == h * 4 + i, part[:, 128:], right_value)
        left_own[:, h * 128 : (h + 1) * 128] = left_value.astype(BF16)
        if h == 0:
            pl.semaphore_wait(barrier, 62)
            start_all(4, cot_copy, own_cot)
            start_all(16, rm_copy, own_row)
            start_all(16, cm_copy, own_column)

            @pl.when(inside)
            def _():
                local(mask_rows, row_masks.at[band, q], rm_recv.at[band * 4 + q]).start()

            @pl.when(jnp.logical_and(inside, xh == c))
            def _():
                local(cot_stage.at[y], cot_all.at[band], cot_recv.at[band]).start()

            @pl.when(active)
            def _():
                local(mask_rows, column_masks.at[zi, q], cm_recv.at[zi * 4 + q]).start()

    right_own[...] = right_value.astype(BF16)

    @pl.when(jnp.logical_not(active))
    def _():
        r1_copy().start()

    @pl.when(active)
    def _():
        start_all(8, r2_copy, z)
        local(right_own, right_all.at[zi, q], r2_recv.at[zi * 2 + xl]).start()

    start_all(16, l_copy, own_row)

    @pl.when(inside)
    def _():
        local(left_own, left_slot(band, q), l_recv.at[band * 4 + q]).start()

    @pl.when(active)
    def _():
        wait(right_own, right_all.at[zi, other_q], r1_recv.at[0])
        start_all(8, r2_forward, z)

    loads[13].wait()
    weight_wide[...] = weight_raw[...].astype(F32)
    for t in range(2):
        for b in range(4):
            for a in range(4):
                at = ((t * 4 + b) * 4 + a) * 32
                weight[at : at + 32, :] = weight_wide[pl.ds(t * 16 + a * 4 + b, 32, stride=32), :].astype(BF16)
    for t in range(8):
        weight_turned[:, t * 128 : (t + 1) * 128] = weight[t * 128 : (t + 1) * 128, :].astype(F32).T.astype(BF16)

    def arrive_masks(n):
        wait(mask_rows, row_masks.at[lax.div(n, 4), lax.rem(n, 4)], rm_recv.at[n])
        wait(mask_rows, column_masks.at[lax.div(n, 4), lax.rem(n, 4)], cm_recv.at[n])

    repeat(16, arrive_masks)
    column_mask = jnp.concatenate(
        [
            jnp.concatenate([column_masks[b, 2 * h] + column_masks[b, 2 * h + 1] for h in range(2)], axis=1)
            for b in range(4)
        ],
        axis=0,
    )
    for i in range(32):
        row = jnp.concatenate(
            [
                row_masks[i // 8, 2 * h, i % 8 : i % 8 + 1, :] + row_masks[i // 8, 2 * h + 1, i % 8 : i % 8 + 1, :]
                for h in range(2)
            ],
            axis=1,
        )
        product[i * 32 : (i + 1) * 32, :] = (row * column_mask).astype(BF16)
    counts[...] = dot(product[...], jnp.ones((256, 128), BF16))
    repeat(4, lambda n: wait(cot_stage.at[n], cot_all.at[n], cot_recv.at[n]))
    for n in range(4):
        cot = cot_all[n].astype(F32).reshape(256, 128)
        scaled[n * 256 : (n + 1) * 256, :] = (cot / counts[n * 256 : (n + 1) * 256, :]).astype(BF16)

    def backward(g):
        span = block(g, 256)
        scaled_part = scaled[span, :]
        for t in range(8):
            grad = dot_nt(weight[t * 128 : (t + 1) * 128, :], scaled_part)
            for half in range(2):
                lane_part = grad[:, half * 128 : (half + 1) * 128]
                parts = swap([lane_part[a * 32 : (a + 1) * 32, :] for a in range(4)], 32)
                for i, part in enumerate(parts):
                    at = pl.ds(pl.multiple_of(g * 256 + half * 128 + i * 32, 32), 32)
                    grad_outer[at, t * 128 : (t + 1) * 128] = part.astype(BF16)

    repeat(4, backward)

    forwarded = jnp.where(active, zi * 2 + 1 - xl, -1)

    def arrive_right(n):
        @pl.when(n != forwarded)
        def _():
            wait(right_own, right_all.at[lax.div(n, 2), lax.rem(n, 2) * 2 + c], r2_recv.at[n])

    repeat(8, arrive_right)
    start_all(2, r3_copy, -1)
    repeat(16, lambda n: wait(left_own, left_slot(lax.div(n, 4), lax.rem(n, 4)), l_recv.at[n]))
    repeat(2, lambda n: wait(right_all.at[:, n * 2 + 1 - c], right_all.at[:, n * 2 + 1 - c], r3_recv.at[n]))
    for at_q in range(4):
        rows = slice(at_q * ROWS, (at_q + 1) * ROWS)
        for t in range(2):
            parts = [right_all[b, at_q, :, t * 128 : (t + 1) * 128].astype(F32) for b in range(4)]
            for b, part in enumerate(swap(parts, 8)):
                right_mat[rows, (t * 4 + b) * 128 : (t * 4 + b + 1) * 128] = part.astype(BF16)

    def right_step(t):
        for b in range(2):
            right_part[:, b * 256 : (b + 1) * 256] = dot(
                left_all[...].reshape(256, 1024), grad_outer[:, t * 512 + b * 256 : t * 512 + (b + 1) * 256]
            )
        for at_q in range(4):
            rows = slice(at_q * ROWS, (at_q + 1) * ROWS)
            parts = swap([right_part[rows, b * 128 : (b + 1) * 128] for b in range(4)], 8)
            for b, part in enumerate(parts):
                right_grad[b, at_q, :, t * 128 : (t + 1) * 128] = part.astype(BF16)

    def gx_copy(n):
        return remote(right_grad.at[:, n * 2 + 1 - c], right_core.at[n], gx_send.at[n], gx_recv.at[n], other_core)

    right_step(0)
    right_step(1)
    start_all(2, gx_copy, -1)

    def gl_part(n):
        return left_grad.at[lax.rem(n, 4), :, block(lax.div(n, 4), WIDE)]

    def gl_copy(n):
        target = device(c * 2 + lax.div(n, 8), z, lax.rem(lax.div(n, 4), 2), lax.div(lax.rem(n, 4), 2), lax.rem(n, 2))
        return remote(gl_part(n), left_in.at[plane], gl_send.at[n], gl_recv.at[plane], target)

    own_gl = jnp.where(inside, band * 4 + q, -1)

    def left_step(g):
        span = block(g, 256)
        part = dot_nt(right_mat[...], grad_outer[span, :]).astype(BF16)
        for at_q in range(4):
            left_grad[at_q, :, span] = part[at_q * ROWS : (at_q + 1) * ROWS, :]

    left_step(0)

    def gz_copy(n):
        return remote(
            right_sum.at[n], right_in.at[z], gz_send.at[n], gz_recv.at[z], device(y, n * 2 + xl, xh, xl, c)
        )

    own_gz = jnp.where(active, zi, -1)
    for n in range(2):
        wait(right_core.at[n], right_core.at[n], gx_recv.at[n])
        for b in range(4):
            right_sum[b, n] = (right_grad[b, n * 2 + c].astype(F32) + right_core[n, b].astype(F32)).astype(BF16)
    start_all(4, gz_copy, own_gz)

    @pl.when(active)
    def _():
        local(right_sum.at[zi], right_in.at[z], gz_recv.at[z]).start()

    for g in range(4):
        if g > 0:
            left_step(g)

        def start_left(n):
            @pl.when(n + g * 4 != own_gl)
            def _():
                gl_copy(n + g * 4).start()

        repeat(4, start_left)

    @pl.when(inside)
    def _():
        local(gl_part(band * 4 + q), left_in.at[plane], gl_recv.at[plane]).start()

    def forward(g):
        span = block(g, 128)
        lead = left_all[:, :, span].reshape(256, 128).astype(F32).T.astype(BF16)
        for t in range(8):
            outer = dot(lead, right_mat[:, t * 128 : (t + 1) * 128])
            parts = swap([outer[i * 32 : (i + 1) * 32, :] for i in range(4)], 32)
            for a, part in enumerate(parts):
                folded[(t * 4 + a) * 32 : (t * 4 + a + 1) * 32, span] = part.astype(BF16)

    def weigh(g):
        span = block(g, 128)
        weight_grad[span, :] = dot(folded[span, :], scaled[...])

    def project(g):
        span = block(g, 128)
        value = dot(weight_turned[...], folded[:, span])
        update = (value.T / counts[span, :]).astype(BF16)
        pair[block(g, 4)] = update.reshape(4, 32, 128)

    repeat(8, forward)
    repeat(8, weigh)

    def plane_peer(n):
        return device(lax.div(n, 4), z, lax.div(lax.rem(n, 4), 2), lax.rem(n, 2), c)

    def line_peer(n):
        return device(y, n, xh, xl, c)

    def wh_copy():
        return remote(weight_grad.at[block(1 - c, 512), :], weight_core, wh_send.at[0], wh_recv.at[0], other_core)

    def wa_part(n):
        return weight_half.at[block(n, 32), :]

    def wa_copy(n):
        return remote(wa_part(n), weight_in.at[plane], wa_send.at[n], wa_recv.at[plane], plane_peer(n))

    def wb_copy(n):
        return remote(weight_sum, weight_far.at[z], wb_send.at[n], wb_recv.at[z], line_peer(n))

    def wc_slot(n):
        return weight_all.at[c, block(n, 32), :]

    def wc_copy(n):
        return remote(weight_total, wc_slot(plane), wc_send.at[n], wc_recv.at[plane], plane_peer(n))

    def wd_copy():
        return remote(weight_all.at[c], weight_all.at[c], wh_send.at[1], wh_recv.at[1], other_core)

    wh_copy().start()
    repeat(8, project)
    wait(weight_core, weight_core, wh_recv.at[0])
    weight_half[...] = (weight_grad[block(c, 512), :] + weight_core[...]).astype(BF16)
    start_all(16, wa_copy, plane)
    local(wa_part(plane), weight_in.at[plane], wa_recv.at[plane]).start()

    def pair_part(n):
        return pair.at[block(n, 8)]

    def pair_copy(n):
        target = device(c * 2 + lax.div(n, 2), z, lax.rem(n, 2), lax.div(y, 2), lax.rem(y, 2))
        return remote(pair_part(n), pair_in.at[xh * 2 + xl], pair_send.at[n], pair_recv.at[xh * 2 + xl], target)

    keeps_pair = jnp.logical_and(inside, q == y)
    own_pair = jnp.where(keeps_pair, band, -1)
    start_all(4, pair_copy, own_pair)

    @pl.when(keeps_pair)
    def _():
        local(pair_part(band), pair_in.at[xh * 2 + xl], pair_recv.at[xh * 2 + xl]).start()

    def gf_copy():
        return remote(right_send, right_last, gf_send.at[0], gf_recv.at[0], partner)

    @pl.when(active)
    def _():
        repeat(8, lambda n: wait(right_in.at[n], right_in.at[n], gz_recv.at[n]))
        away = right_in[0, 1 - xl].astype(F32)
        for n in range(1, 8):
            away = away + right_in[n, 1 - xl].astype(F32)
        right_send[...] = away.astype(BF16)
        gf_copy().start()
        here = right_in[0, xl].astype(F32)
        for n in range(1, 8):
            here = here + right_in[n, xl].astype(F32)
        right_last[...] = here.astype(BF16)

    repeat(16, lambda n: wait(left_in.at[n], left_in.at[n], gl_recv.at[n]))
    left_total = total(left_in, 16).astype(BF16).astype(F32)

    @pl.when(jnp.logical_not(active))
    def _():
        wait(right_last, right_last, gf_recv.at[0])

    right_total = right_last[...].astype(F32)

    repeat(16, lambda n: wait(weight_in.at[n], weight_in.at[n], wa_recv.at[n]))
    weight_sum[...] = total(weight_in, 16).astype(BF16)
    start_all(8, wb_copy, z)
    local(weight_sum, weight_far.at[z], wb_recv.at[z]).start()

    sums = jnp.zeros((32, WIDE), F32)
    for h in range(2):
        picked = []
        for i in range(4):
            keep = turned[:, 16 + h * 4 + i : 17 + h * 4 + i]
            tile = left_total[:, h * 128 : (h + 1) * 128]
            picked.append(
                jnp.concatenate(
                    [
                        jnp.where(lax.div(lane, 32) == i, tile, 0.0) * keep,
                        jnp.where(lax.rem(wide_lane, 8) == h * 4 + i, right_total, 0.0) * keep,
                    ],
                    axis=1,
                )
            )
        picked = jnp.concatenate(picked, axis=0).astype(BF16)
        gained = dot(picked, maps[...]) * gain[...]
        whitened = white[h * 256 : (h + 1) * 256, :]
        stream_grad = spread[h * 256 : (h + 1) * 256, :1] * (
            gained
            - jnp.mean(gained, axis=-1, keepdims=True)
            - whitened * jnp.mean(gained * whitened, axis=-1, keepdims=True)
        )
        for piece in split(stream_grad, 2):
            sums = sums + dot(hot_turned[h], piece)
    for n in range(TILES):
        table_part[n] = sums[(n // 2) * 8 : (n // 2 + 1) * 8, (n % 2) * 128 : (n % 2 + 1) * 128]

    def t_copy():
        return remote(table_part.at[pl.ds((1 - c) * 3, 3)], table_core, t_send.at[0], t_recv.at[0], other_core)

    def tp_copy(n):
        return remote(table_p.at[plane], table_p.at[plane], tp_send.at[n], tp_recv.at[plane], plane_peer(n))

    def tz_copy(n):
        return remote(table_z.at[z], table_z.at[z], tz_send.at[n], tz_recv.at[z], device(y, n, xh, xl, c))

    def half(at_c):
        return table_all.at[pl.ds(at_c * 3, 3)]

    def t_last():
        return remote(table_half, half(c), t_send.at[1], t_recv.at[1], other_core)

    def arrive(count, ref, sem, own):
        def step(n):
            @pl.when(n != own)
            def _():
                wait(ref.at[n], ref.at[n], sem.at[n])

        repeat(count, step)

    t_copy().start()
    wait(table_core, table_core, t_recv.at[0])
    table_p[plane] = table_part[pl.ds(c * 3, 3)] + table_core[...]
    start_all(16, tp_copy, plane)

    repeat(8, lambda n: wait(weight_far.at[n], weight_far.at[n], wb_recv.at[n]))
    weight_total[...] = total(weight_far, 8).astype(BF16)
    start_all(16, wc_copy, plane)
    local(weight_total, wc_slot(plane), wc_recv.at[plane]).start()

    repeat(4, lambda n: wait(pair_part(n), pair_in.at[n], pair_recv.at[n]))
    for at_z in range(8):
        run = [
            pair_in[at_x * 2 + at_z % 2, :, (at_z // 2) * 8 : (at_z // 2 + 1) * 8, :].astype(F32) for at_x in range(2)
        ]
        pair_out[:, at_z * 16 : (at_z + 1) * 16, :] = jnp.concatenate(run, axis=1).astype(BF16)

    arrive(16, table_p, tp_recv, plane)
    table_z[z] = total(table_p, 16)
    start_all(8, tz_copy, z)

    repeat(16, lambda n: wait(weight_total, wc_slot(n), wc_recv.at[n]))
    wd_copy().start()

    arrive(8, table_z, tz_recv, z)
    summed = total(table_z, 8)
    table_half[...] = summed
    t_last().start()
    table_all[pl.ds(c * 3, 3)] = summed
    wait(table_half, half(1 - c), t_recv.at[1])
    for n in range(TILES):
        high = min(8, table_out.shape[0] - (n // 2) * 8)
        table_out[(n // 2) * 8 : (n // 2) * 8 + high, (n % 2) * 128 : (n % 2 + 1) * 128] = table_all[n][:high]
    wait(weight_all.at[1 - c], weight_all.at[1 - c], wh_recv.at[1])
    for t in range(2):
        for b in range(4):
            for a in range(4):
                at = ((t * 4 + b) * 4 + a) * 32
                weight_out[pl.ds(t * 16 + a * 4 + b, 32, stride=32), :] = weight_all[at // 512, at % 512 : at % 512 + 32, :].astype(F32)

    sent_all(16, rm_copy, own_row)
    sent_all(16, cm_copy, own_column)
    sent_all(4, cot_copy, own_cot)
    sent_all(16, l_copy, own_row)
    sent_all(2, r3_copy, -1)
    sent_all(2, gx_copy, -1)
    sent_all(4, gz_copy, own_gz)
    sent_all(16, gl_copy, own_gl)
    sent_all(16, wa_copy, plane)
    sent_all(8, wb_copy, z)
    sent_all(16, wc_copy, plane)
    wh_copy().wait_send()
    wd_copy().wait_send()
    sent_all(4, pair_copy, own_pair)
    sent_all(16, tp_copy, plane)
    sent_all(8, tz_copy, z)
    t_copy().wait_send()
    t_last().wait_send()

    @pl.when(active)
    def _():
        sent_all(8, r2_copy, z)
        sent_all(8, r2_forward, z)
        gf_copy().wait_send()

    @pl.when(jnp.logical_not(active))
    def _():
        r1_copy().wait_send()


def shape(dims, dtype=BF16):
    return jax.ShapeDtypeStruct(dims, dtype)


def body(
    alignment_token_classes, deletions, alignment_mask, homolog_stack_values,
    letter_lookup_coefficients, gap_lookup_coefficients, standardize_gain, standardize_offset,
    first_factor_map, left_bias_vector, second_factor_map, right_bias_vector,
    output_weight_matrix, cotangent,
):
    kinds = letter_lookup_coefficients.shape[0]
    grades = np.arange(32, dtype=np.float32)
    steps = jnp.asarray(
        np.stack([(grades > 0).astype(np.float32), (2.0 / math.pi * np.arctan(grades / 3.0)).astype(np.float32)], 1)
    )
    inputs = [
        alignment_token_classes.T, deletions.T, alignment_mask.T, homolog_stack_values,
        letter_lookup_coefficients, gap_lookup_coefficients, steps,
        standardize_gain.reshape(1, 256), standardize_offset.reshape(1, 256),
        first_factor_map.T, left_bias_vector.reshape(1, 32), second_factor_map.T, right_bias_vector.reshape(1, 32),
        output_weight_matrix,
    ]
    vmem = pltpu.VMEM
    scratch = [vmem(value.shape, value.dtype) for value in inputs] + [
        vmem((8, 16, 16, 128), BF16), vmem((4, 8, 32, 128), BF16),
        vmem((128, 128), F32), vmem((ROWS, 128), F32), vmem((8, 128), F32),
        vmem((2, 512, 128), F32),
        vmem((128, WIDE), F32), vmem((384, 256), BF16), vmem((8, 384), F32),
        vmem((1024, 128), F32), vmem((1024, 128), BF16), vmem((128, 1024), BF16),
        vmem((2, 32, 256), BF16),
        vmem((512, 256), F32), vmem((512, 128), F32),
        vmem((ROWS, WIDE), BF16), vmem((ROWS, WIDE), BF16),
        vmem((4, 4, 8, 128), F32), vmem((4, 4, 8, 128), F32),
        vmem((4, 8, 32, 128), BF16),
        vmem((4, ROWS, 1024), BF16), vmem((4, 4, ROWS, WIDE), BF16),
        vmem((256, 1024), BF16), vmem((1024, 256), BF16),
        vmem((1024, 128), F32), vmem((1024, 128), BF16),
        vmem((1024, 1024), BF16), vmem((1024, 1024), BF16),
        vmem((32, 32, 128), BF16), vmem((4, 8, 32, 128), BF16),
        vmem((4, 4, ROWS, WIDE), BF16), vmem((256, 512), F32), vmem((2, 4, ROWS, WIDE), BF16),
        vmem((4, 2, ROWS, WIDE), BF16), vmem((8, 2, ROWS, WIDE), BF16),
        vmem((ROWS, WIDE), BF16), vmem((ROWS, WIDE), BF16),
        vmem((4, ROWS, 1024), BF16), vmem((16, ROWS, WIDE), BF16),
        vmem((1024, 128), F32), vmem((512, 128), F32), vmem((512, 128), BF16),
        vmem((16, 32, 128), BF16), vmem((32, 128), BF16),
        vmem((8, 32, 128), BF16), vmem((32, 128), BF16), vmem((2, 512, 128), BF16),
        vmem((TILES, 8, 128), F32), vmem((3, 8, 128), F32),
        vmem((16, 3, 8, 128), F32), vmem((8, 3, 8, 128), F32),
        vmem((3, 8, 128), F32), vmem((TILES, 8, 128), F32),
    ]
    sizes = [len(inputs) + 1, 16, 16, 16, 16, 4, 4, 1, 1, 16, 8, 2, 2, 16, 16]
    sizes += [2, 2, 4, 8, 1, 1, 16, 16, 4, 4, 2, 2, 16, 16, 8, 8, 16, 16, 2, 2, 16, 16, 8, 8]
    results = pl.pallas_call(
        kernel,
        out_shape=[shape((8, 128, 128)), shape((1024, 128), F32), shape((kinds, 256), F32)],
        in_specs=[pl.BlockSpec(memory_space=pl.ANY)] * (len(inputs) + 1),
        out_specs=[pl.BlockSpec(memory_space=pltpu.VMEM)] * 3,
        scratch_shapes=scratch + [pltpu.SemaphoreType.DMA((size,)) for size in sizes],
        compiler_params=pltpu.CompilerParams(
            collective_id=0, has_side_effects=True, vmem_limit_bytes=60 * 1024 * 1024
        ),
        name="outer_product_mean",
    )(*inputs, cotangent.reshape(8, 16, 2, 16, 128))
    return pl.pallas_call(
        hand_over,
        out_shape=[shape(value.shape, value.dtype) for value in results],
        in_specs=[pl.BlockSpec(memory_space=pl.ANY)] * 3,
        out_specs=[pl.BlockSpec(memory_space=pl.ANY)] * 3,
        scratch_shapes=[vmem(value.shape, value.dtype) for value in results] + [pltpu.SemaphoreType.DMA((3,))],
        name="hand_over",
    )(*results)


def hand_over(pair, weight, table, pair_out, weight_out, table_out, pair_here, weight_here, table_here, sem):
    here = [pair_here, weight_here, table_here]
    arrive = [local(src, dst, sem.at[n]) for n, (src, dst) in enumerate(zip([pair, weight, table], here))]
    leave = [local(src, dst, sem.at[n]) for n, (src, dst) in enumerate(zip(here, [pair_out, weight_out, table_out]))]
    for copy in arrive:
        copy.start()
    for first, second in zip(arrive, leave):
        first.wait()
        second.start()
    for copy in leave:
        copy.wait()


def solution(mesh):
    in_specs = (
        P("seq", "res"), P("seq", "res"), P("seq", "res"), P("seq", "res", None),
        P(), P(), P(), P(), P(), P(), P(), P(), P(),
        P("res", None, None),
    )
    out_specs = (P("res", "seq", None), P(), P())
    return jax.shard_map(body, mesh=mesh, in_specs=in_specs, out_specs=out_specs, check_vma=False)
```

```python
import math

import jax
import jax.numpy as jnp
import numpy as np
from jax import lax
from jax.experimental import pallas as pl
from jax.experimental.pallas import tpu as pltpu
from jax.sharding import PartitionSpec as P

EPSILON = 1e-05
MESH = pl.DeviceIdType.MESH
F32 = jnp.float32
BF16 = jnp.bfloat16

ROWS = 64
WIDE = 256
TILES = 6


def device(y, z, xh, xl, c):
    return (y * 16 + z * 2 + xh, xl * 2 + c)


def repeat(count, step):
    lax.fori_loop(0, count, lambda n, carried: (step(n), carried)[1], 0)


def remote(src, dst, send, recv, target):
    return pltpu.make_async_remote_copy(
        src_ref=src, dst_ref=dst, send_sem=send, recv_sem=recv, device_id=target, device_id_type=MESH
    )


def start_all(count, copy, own):
    def step(n):
        @pl.when(n != own)
        def _():
            copy(n).start()

    repeat(count, step)


def sent_all(count, copy, own):
    def step(n):
        @pl.when(n != own)
        def _():
            copy(n).wait_send()

    repeat(count, step)


def local(src, dst, sem):
    return pltpu.make_async_copy(src, dst, sem)


def lanes(dims):
    return lax.broadcasted_iota(jnp.int32, dims, len(dims) - 1)


def block(n, size):
    return pl.ds(pl.multiple_of(n * size, size), size)


def swap(parts, stride):
    lane = lanes(parts[0].shape)
    low = lax.rem(lax.div(lane, stride), 2) == 0
    high = lax.rem(lax.div(lane, 2 * stride), 2) == 0

    def pair(first, second, step, keep):
        return (
            jnp.where(keep, first, pltpu.roll(second, step, 1)),
            jnp.where(keep, pltpu.roll(first, 128 - step, 1), second),
        )

    a, b = pair(parts[0], parts[1], stride, low)
    c, d = pair(parts[2], parts[3], stride, low)
    a, c = pair(a, c, 2 * stride, high)
    b, d = pair(b, d, 2 * stride, high)
    return [a, b, c, d]


def dot(first, second):
    return jnp.dot(first, second, preferred_element_type=F32)


def dot_nt(first, second):
    return lax.dot_general(first, second, (((1,), (1,)), ((), ())), preferred_element_type=F32)


def split(value, count):
    pieces = []
    for _ in range(count):
        piece = value.astype(BF16)
        pieces.append(piece)
        value = value - piece.astype(F32)
    return pieces


def total(ref, count):
    value = ref[0].astype(F32)
    for n in range(1, count):
        value = value + ref[n].astype(F32)
    return value


def kernel(
    token_h, deletion_h, mask_h, stack_h, letters_h, gaps_h, steps_h, gain_h, offset_h,
    left_map_h, left_bias_h, right_map_h, right_bias_h, weight_h, cotangent,
    pair_h, weight_grad_h, table_out,
    token, deletion, mask, stack_raw, letters, gaps, steps, gain, offset,
    left_map, left_bias, right_map, right_bias, weight_raw, cot_raw, cot_stage,
    square, turned, mask_rows, stack, table, maps, bias, weight_wide, weight, weight_turned, hot_turned,
    white, spread, left_own, right_own, row_masks, column_masks, cot_all, left_all, right_all,
    right_mat, wide_grad, wide_outer, product, counts, scaled, folded, grad_outer, pair, pair_in,
    right_grad, right_part, right_core, right_sum, right_in, right_last, right_send, left_grad, left_in,
    weight_grad, weight_core, weight_half, weight_in, weight_sum, weight_far, weight_total, weight_all,
    table_part, table_core, table_p, table_z, table_half, table_all, pair_out, weight_out,
    in_sem, out_sem, rm_send, rm_recv, cm_send, cm_recv, cot_send, cot_recv,
    r1_send, r1_recv, r2_send, r2_recv, r3_send, r3_recv, l_send, l_recv,
    gx_send, gx_recv, gz_send, gz_recv, gf_send, gf_recv, gl_send, gl_recv, pair_send, pair_recv,
    wh_send, wh_recv, wa_send, wa_recv, wb_send, wb_recv, wc_send, wc_recv,
    t_send, t_recv, tp_send, tp_recv, tz_send, tz_recv,
):
    res = lax.axis_index("res")
    q = lax.axis_index("seq")
    y, z, xh = lax.div(res, 16), lax.rem(lax.div(res, 2), 8), lax.rem(res, 2)
    xl, c = lax.div(q, 2), lax.rem(q, 2)
    zi, parity = lax.div(z, 2), lax.rem(z, 2)
    active = parity == xl
    inside = lax.div(y, 2) == c
    other_q = (1 - xl) * 2 + c
    plane = y * 4 + xh * 2 + xl
    band = lax.rem(y, 2) * 2 + xh
    own_column = jnp.where(active, z * 2 + c, -1)
    own_row = jnp.where(inside, plane, -1)
    other_core = device(y, z, xh, xl, 1 - c)
    partner = device(y, z, xh, 1 - xl, c)

    def wait(src, dst, sem):
        local(src, dst, sem).wait()

    loads = [
        local(src, dst, in_sem.at[n])
        for n, (src, dst) in enumerate(
            [
                (token_h, token), (deletion_h, deletion), (mask_h, mask), (stack_h, stack_raw),
                (letters_h, letters), (gaps_h, gaps), (steps_h, steps), (gain_h, gain), (offset_h, offset),
                (left_map_h, left_map), (left_bias_h, left_bias), (right_map_h, right_map),
                (right_bias_h, right_bias), (weight_h, weight_raw), (cotangent.at[:, :, xl], cot_raw),
            ]
        )
    ]
    for load in loads:
        load.start()

    barrier = pltpu.get_barrier_semaphore()

    def signal(target):
        pl.semaphore_signal(barrier, inc=1, device_id=target, device_id_type=MESH)

    def greet(n):
        @pl.when(n != z * 4 + q)
        def _():
            signal((y * 16 + lax.div(n, 4) * 2 + xh, lax.rem(n, 4)))

        @pl.when(n != (y * 2 + xh) * 4 + q)
        def _():
            signal((lax.div(n, 8) * 16 + z * 2 + lax.rem(lax.div(n, 4), 2), lax.rem(n, 4)))

    repeat(32, greet)

    def line_user(n):
        return device(y, lax.div(n, 2), xh, parity, lax.rem(n, 2))

    def plane_user(n):
        return device(lax.div(n, 4), z, lax.div(lax.rem(n, 4), 2), lax.rem(n, 2), lax.div(y, 2))

    def rm_copy(n):
        return remote(mask_rows, row_masks.at[band, q], rm_send.at[n], rm_recv.at[band * 4 + q], plane_user(n))

    def cm_copy(n):
        return remote(mask_rows, column_masks.at[zi, q], cm_send.at[n], cm_recv.at[zi * 4 + q], line_user(n))

    def cot_copy(n):
        return remote(cot_stage.at[n], cot_all.at[band], cot_send.at[n], cot_recv.at[band], device(n, z, c, xl, lax.div(y, 2)))

    own_cot = jnp.where(jnp.logical_and(inside, xh == c), y, -1)

    def left_slot(at_band, at_q):
        return left_all.at[at_q, :, block(at_band, WIDE)]

    def l_copy(n):
        return remote(left_own, left_slot(band, q), l_send.at[n], l_recv.at[band * 4 + q], plane_user(n))

    def r1_copy():
        return remote(right_own, right_all.at[zi, q], r1_send.at[0], r1_recv.at[0], partner)

    def r2_copy(n):
        return remote(
            right_own, right_all.at[zi, q], r2_send.at[n], r2_recv.at[zi * 2 + xl], device(y, n, xh, xl, c)
        )

    def r2_forward(n):
        return remote(
            right_all.at[zi, other_q], right_all.at[zi, other_q], r2_send.at[8 + n], r2_recv.at[zi * 2 + 1 - xl],
            device(y, n, xh, xl, c),
        )

    def r3_copy(n):
        at_q = n * 2 + c
        return remote(right_all.at[:, at_q], right_all.at[:, at_q], r3_send.at[n], r3_recv.at[n], other_core)

    for load in loads[:13]:
        load.wait()
    mask_value = mask[...].astype(F32)
    empty = jnp.zeros((8, ROWS), F32)
    mask_rows[...] = jnp.where(
        c == 0, jnp.concatenate([mask_value, empty], axis=1), jnp.concatenate([empty, mask_value], axis=1)
    )
    square[...] = jnp.zeros((128, 128), F32)
    square[0:8, 0:ROWS] = token[...].astype(F32)
    square[8:16, 0:ROWS] = deletion[...].astype(F32)
    square[16:24, 0:ROWS] = mask_value
    turned[...] = square[...].T[:ROWS]
    for n in range(2):
        stack[n] = stack_raw[:, :, n * 128 : (n + 1) * 128].astype(F32).reshape(512, 128)
    table[...] = jnp.zeros((128, WIDE), F32)
    table[: letters.shape[0], :] = letters[...]
    table[32:64, :] = steps[:, 0:1] * gaps[0:1, :] + steps[:, 1:2] * gaps[1:2, :]
    spread_left = (
        lax.rem(lax.broadcasted_iota(jnp.int32, (128, 32), 0), 32) == lanes((128, 32))
    ).astype(F32).astype(BF16)
    spread_right = (
        lax.div(lax.broadcasted_iota(jnp.int32, (WIDE, 32), 0), 8) == lanes((WIDE, 32))
    ).astype(F32).astype(BF16)
    maps[:128, :] = dot(spread_left, left_map[...]).astype(BF16)
    maps[128:, :] = dot(spread_right, right_map[...]).astype(BF16)
    bias[...] = jnp.concatenate(
        [
            sum(dot_nt(piece, spread_left) for piece in split(jnp.broadcast_to(left_bias[...], (8, 32)), 3)),
            sum(dot_nt(piece, spread_right) for piece in split(jnp.broadcast_to(right_bias[...], (8, 32)), 3)),
        ],
        axis=1,
    )
    loads[14].wait()
    for n in range(4):
        strip = cot_raw[:, n * 4 : n * 4 + 4].astype(F32)
        strip = jnp.where(c == 0, strip[:, :, :8, :], strip[:, :, 8:, :])
        cot_stage[n] = strip.reshape(8, 32, 128).astype(BF16)
    lane = lanes((ROWS, 128))
    fine = lane.astype(F32)
    wide_lane = lanes((ROWS, WIDE))
    pieces = split(table[...], 3)
    right_value = jnp.zeros((ROWS, WIDE), F32)
    for h in range(2):
        hot = jnp.concatenate(
            [
                jnp.logical_or(fine == turned[:, i : i + 1], fine == turned[:, 8 + i : 9 + i] + 32.0).astype(F32)
                for i in range(h * 4, h * 4 + 4)
            ],
            axis=0,
        )
        hot_turned[h] = hot.T[:32].astype(BF16)
        hot = hot.astype(BF16)
        hidden = jnp.concatenate(
            [
                jnp.concatenate([stack[n, pl.ds(i, ROWS, stride=8), :] for i in range(h * 4, h * 4 + 4)], axis=0)
                for n in range(2)
            ],
            axis=1,
        ) + (dot(hot, pieces[0]) + dot(hot, pieces[1]) + dot(hot, pieces[2]))
        centered = hidden - jnp.mean(hidden, axis=-1, keepdims=True)
        variance = jnp.mean(centered * centered, axis=-1, keepdims=True)
        scale = lax.rsqrt(variance + EPSILON)
        whitened = centered * scale
        white[h * 256 : (h + 1) * 256, :] = whitened
        spread[h * 256 : (h + 1) * 256, :] = jnp.broadcast_to(scale, (256, 128))
        normed = (whitened * gain[...] + offset[...]).astype(BF16)
        rows = dot_nt(normed, maps[...]) + bias[:1, :]
        left_value = jnp.zeros((ROWS, 128), F32)
        for i in range(4):
            part = turned[:, 16 + h * 4 + i : 17 + h * 4 + i] * rows[i * ROWS : (i + 1) * ROWS, :]
            left_value = jnp.where(lax.div(lane, 32) == i, part[:, :128], left_value)
            right_value = jnp.where(lax.rem(wide_lane, 8) == h * 4 + i, part[:, 128:], right_value)
        left_own[:, h * 128 : (h + 1) * 128] = left_value.astype(BF16)
        if h == 0:
            pl.semaphore_wait(barrier, 62)
            start_all(4, cot_copy, own_cot)
            start_all(16, rm_copy, own_row)
            start_all(16, cm_copy, own_column)

            @pl.when(inside)
            def _():
                local(mask_rows, row_masks.at[band, q], rm_recv.at[band * 4 + q]).start()

            @pl.when(jnp.logical_and(inside, xh == c))
            def _():
                local(cot_stage.at[y], cot_all.at[band], cot_recv.at[band]).start()

            @pl.when(active)
            def _():
                local(mask_rows, column_masks.at[zi, q], cm_recv.at[zi * 4 + q]).start()

    right_own[...] = right_value.astype(BF16)

    @pl.when(jnp.logical_not(active))
    def _():
        r1_copy().start()

    @pl.when(active)
    def _():
        start_all(8, r2_copy, z)
        local(right_own, right_all.at[zi, q], r2_recv.at[zi * 2 + xl]).start()

    start_all(16, l_copy, own_row)

    @pl.when(inside)
    def _():
        local(left_own, left_slot(band, q), l_recv.at[band * 4 + q]).start()

    @pl.when(active)
    def _():
        wait(right_own, right_all.at[zi, other_q], r1_recv.at[0])
        start_all(8, r2_forward, z)

    loads[13].wait()
    weight_wide[...] = weight_raw[...].astype(F32)
    for t in range(2):
        for b in range(4):
            for a in range(4):
                at = ((t * 4 + b) * 4 + a) * 32
                weight[at : at + 32, :] = weight_wide[pl.ds(t * 16 + a * 4 + b, 32, stride=32), :].astype(BF16)
    for t in range(8):
        weight_turned[:, t * 128 : (t + 1) * 128] = weight[t * 128 : (t + 1) * 128, :].astype(F32).T.astype(BF16)

    def arrive_masks(n):
        wait(mask_rows, row_masks.at[lax.div(n, 4), lax.rem(n, 4)], rm_recv.at[n])
        wait(mask_rows, column_masks.at[lax.div(n, 4), lax.rem(n, 4)], cm_recv.at[n])

    repeat(16, arrive_masks)
    column_mask = jnp.concatenate(
        [
            jnp.concatenate([column_masks[b, 2 * h] + column_masks[b, 2 * h + 1] for h in range(2)], axis=1)
            for b in range(4)
        ],
        axis=0,
    )
    for i in range(32):
        row = jnp.concatenate(
            [
                row_masks[i // 8, 2 * h, i % 8 : i % 8 + 1, :] + row_masks[i // 8, 2 * h + 1, i % 8 : i % 8 + 1, :]
                for h in range(2)
            ],
            axis=1,
        )
        product[i * 32 : (i + 1) * 32, :] = (row * column_mask).astype(BF16)
    counts[...] = dot(product[...], jnp.ones((256, 128), BF16))
    repeat(4, lambda n: wait(cot_stage.at[n], cot_all.at[n], cot_recv.at[n]))
    for n in range(4):
        cot = cot_all[n].astype(F32).reshape(256, 128)
        scaled[n * 256 : (n + 1) * 256, :] = (cot / counts[n * 256 : (n + 1) * 256, :]).astype(BF16)

    def backward(g):
        span = block(g, 256)
        wide_grad[...] = dot_nt(weight[...], scaled[span, :])
        for t in range(8):
            for half in range(2):
                lane_part = wide_grad[t * 128 : (t + 1) * 128, half * 128 : (half + 1) * 128]
                parts = swap([lane_part[a * 32 : (a + 1) * 32, :] for a in range(4)], 32)
                for i, part in enumerate(parts):
                    at = pl.ds(pl.multiple_of(g * 256 + half * 128 + i * 32, 32), 32)
                    grad_outer[at, t * 128 : (t + 1) * 128] = part.astype(BF16)

    repeat(4, backward)

    def right_step(t):
        for b in range(2):
            right_part[:, b * 256 : (b + 1) * 256] = dot(
                left_all[...].reshape(256, 1024), grad_outer[:, t * 512 + b * 256 : t * 512 + (b + 1) * 256]
            )
        for at_q in range(4):
            rows = slice(at_q * ROWS, (at_q + 1) * ROWS)
            parts = swap([right_part[rows, b * 128 : (b + 1) * 128] for b in range(4)], 8)
            for b, part in enumerate(parts):
                right_grad[b, at_q, :, t * 128 : (t + 1) * 128] = part.astype(BF16)

    def gx_copy(n):
        return remote(right_grad.at[:, n * 2 + 1 - c], right_core.at[n], gx_send.at[n], gx_recv.at[n], other_core)

    repeat(16, lambda n: wait(left_own, left_slot(lax.div(n, 4), lax.rem(n, 4)), l_recv.at[n]))
    right_step(0)
    right_step(1)
    start_all(2, gx_copy, -1)

    forwarded = jnp.where(active, zi * 2 + 1 - xl, -1)

    def arrive_right(n):
        @pl.when(n != forwarded)
        def _():
            wait(right_own, right_all.at[lax.div(n, 2), lax.rem(n, 2) * 2 + c], r2_recv.at[n])

    repeat(8, arrive_right)
    start_all(2, r3_copy, -1)
    def gz_copy(n):
        return remote(
            right_sum.at[n], right_in.at[z], gz_send.at[n], gz_recv.at[z], device(y, n * 2 + xl, xh, xl, c)
        )

    own_gz = jnp.where(active, zi, -1)
    for n in range(2):
        wait(right_core.at[n], right_core.at[n], gx_recv.at[n])
        for b in range(4):
            right_sum[b, n] = (right_grad[b, n * 2 + c].astype(F32) + right_core[n, b].astype(F32)).astype(BF16)
    start_all(4, gz_copy, own_gz)

    @pl.when(active)
    def _():
        local(right_sum.at[zi], right_in.at[z], gz_recv.at[z]).start()

    repeat(2, lambda n: wait(right_all.at[:, n * 2 + 1 - c], right_all.at[:, n * 2 + 1 - c], r3_recv.at[n]))
    for at_q in range(4):
        rows = slice(at_q * ROWS, (at_q + 1) * ROWS)
        for t in range(2):
            parts = [right_all[b, at_q, :, t * 128 : (t + 1) * 128].astype(F32) for b in range(4)]
            for b, part in enumerate(swap(parts, 8)):
                right_mat[rows, (t * 4 + b) * 128 : (t * 4 + b + 1) * 128] = part.astype(BF16)


    def gl_part(n):
        return left_grad.at[lax.rem(n, 4), :, block(lax.div(n, 4), WIDE)]

    def gl_copy(n):
        target = device(c * 2 + lax.div(n, 8), z, lax.rem(lax.div(n, 4), 2), lax.div(lax.rem(n, 4), 2), lax.rem(n, 2))
        return remote(gl_part(n), left_in.at[plane], gl_send.at[n], gl_recv.at[plane], target)

    own_gl = jnp.where(inside, band * 4 + q, -1)

    def left_step(g):
        span = block(g, 256)
        part = dot_nt(right_mat[...], grad_outer[span, :]).astype(BF16)
        for at_q in range(4):
            left_grad[at_q, :, span] = part[at_q * ROWS : (at_q + 1) * ROWS, :]

    for g in range(4):
        left_step(g)

        def start_left(n):
            @pl.when(n + g * 4 != own_gl)
            def _():
                gl_copy(n + g * 4).start()

        repeat(4, start_left)

    @pl.when(inside)
    def _():
        local(gl_part(band * 4 + q), left_in.at[plane], gl_recv.at[plane]).start()

    def forward(g):
        lead = left_all[:, :, block(g, 256)].reshape(256, 256).astype(F32).T.astype(BF16)
        wide_outer[...] = dot(lead, right_mat[...])
        for half in range(2):
            span = pl.ds(pl.multiple_of(g * 256 + half * 128, 128), 128)
            for t in range(8):
                tile = wide_outer[half * 128 : (half + 1) * 128, t * 128 : (t + 1) * 128]
                parts = swap([tile[i * 32 : (i + 1) * 32, :] for i in range(4)], 32)
                for a, part in enumerate(parts):
                    folded[(t * 4 + a) * 32 : (t * 4 + a + 1) * 32, span] = part.astype(BF16)

    def project(g):
        span = block(g, 256)
        value = dot(weight_turned[...], folded[:, span])
        update = (value.T / counts[span, :]).astype(BF16)
        pair[block(g, 8)] = update.reshape(8, 32, 128)

    repeat(4, forward)
    weight_grad[...] = dot(folded[...], scaled[...])

    def plane_peer(n):
        return device(lax.div(n, 4), z, lax.div(lax.rem(n, 4), 2), lax.rem(n, 2), c)

    def line_peer(n):
        return device(y, n, xh, xl, c)

    def wh_copy():
        return remote(weight_grad.at[block(1 - c, 512), :], weight_core, wh_send.at[0], wh_recv.at[0], other_core)

    def wa_part(n):
        return weight_half.at[block(n, 32), :]

    def wa_copy(n):
        return remote(wa_part(n), weight_in.at[plane], wa_send.at[n], wa_recv.at[plane], plane_peer(n))

    def wb_copy(n):
        return remote(weight_sum, weight_far.at[z], wb_send.at[n], wb_recv.at[z], line_peer(n))

    def wc_slot(n):
        return weight_all.at[c, block(n, 32), :]

    def wc_copy(n):
        return remote(weight_total, wc_slot(plane), wc_send.at[n], wc_recv.at[plane], plane_peer(n))

    def wd_copy():
        return remote(weight_all.at[c], weight_all.at[c], wh_send.at[1], wh_recv.at[1], other_core)

    wh_copy().start()
    repeat(4, project)
    wait(weight_core, weight_core, wh_recv.at[0])
    weight_half[...] = (weight_grad[block(c, 512), :] + weight_core[...]).astype(BF16)
    start_all(16, wa_copy, plane)
    local(wa_part(plane), weight_in.at[plane], wa_recv.at[plane]).start()

    def pair_part(n):
        return pair.at[block(n, 8)]

    def pair_copy(n):
        target = device(c * 2 + lax.div(n, 2), z, lax.rem(n, 2), lax.div(y, 2), lax.rem(y, 2))
        return remote(pair_part(n), pair_in.at[xh * 2 + xl], pair_send.at[n], pair_recv.at[xh * 2 + xl], target)

    keeps_pair = jnp.logical_and(inside, q == y)
    own_pair = jnp.where(keeps_pair, band, -1)
    start_all(4, pair_copy, own_pair)

    @pl.when(keeps_pair)
    def _():
        local(pair_part(band), pair_in.at[xh * 2 + xl], pair_recv.at[xh * 2 + xl]).start()

    def gf_copy():
        return remote(right_send, right_last, gf_send.at[0], gf_recv.at[0], partner)

    @pl.when(active)
    def _():
        repeat(8, lambda n: wait(right_in.at[n], right_in.at[n], gz_recv.at[n]))
        away = right_in[0, 1 - xl].astype(F32)
        for n in range(1, 8):
            away = away + right_in[n, 1 - xl].astype(F32)
        right_send[...] = away.astype(BF16)
        gf_copy().start()
        here = right_in[0, xl].astype(F32)
        for n in range(1, 8):
            here = here + right_in[n, xl].astype(F32)
        right_last[...] = here.astype(BF16)

    repeat(16, lambda n: wait(left_in.at[n], left_in.at[n], gl_recv.at[n]))
    left_total = total(left_in, 16).astype(BF16).astype(F32)

    @pl.when(jnp.logical_not(active))
    def _():
        wait(right_last, right_last, gf_recv.at[0])

    right_total = right_last[...].astype(F32)

    repeat(16, lambda n: wait(weight_in.at[n], weight_in.at[n], wa_recv.at[n]))
    weight_sum[...] = total(weight_in, 16).astype(BF16)
    start_all(8, wb_copy, z)
    local(weight_sum, weight_far.at[z], wb_recv.at[z]).start()

    sums = jnp.zeros((32, WIDE), F32)
    for h in range(2):
        picked = []
        for i in range(4):
            keep = turned[:, 16 + h * 4 + i : 17 + h * 4 + i]
            tile = left_total[:, h * 128 : (h + 1) * 128]
            picked.append(
                jnp.concatenate(
                    [
                        jnp.where(lax.div(lane, 32) == i, tile, 0.0) * keep,
                        jnp.where(lax.rem(wide_lane, 8) == h * 4 + i, right_total, 0.0) * keep,
                    ],
                    axis=1,
                )
            )
        picked = jnp.concatenate(picked, axis=0).astype(BF16)
        gained = dot(picked, maps[...]) * gain[...]
        whitened = white[h * 256 : (h + 1) * 256, :]
        stream_grad = spread[h * 256 : (h + 1) * 256, :1] * (
            gained
            - jnp.mean(gained, axis=-1, keepdims=True)
            - whitened * jnp.mean(gained * whitened, axis=-1, keepdims=True)
        )
        for piece in split(stream_grad, 2):
            sums = sums + dot(hot_turned[h], piece)
    for n in range(TILES):
        table_part[n] = sums[(n // 2) * 8 : (n // 2 + 1) * 8, (n % 2) * 128 : (n % 2 + 1) * 128]

    def t_copy():
        return remote(table_part.at[pl.ds((1 - c) * 3, 3)], table_core, t_send.at[0], t_recv.at[0], other_core)

    def tp_copy(n):
        return remote(table_p.at[plane], table_p.at[plane], tp_send.at[n], tp_recv.at[plane], plane_peer(n))

    def tz_copy(n):
        return remote(table_z.at[z], table_z.at[z], tz_send.at[n], tz_recv.at[z], device(y, n, xh, xl, c))

    def half(at_c):
        return table_all.at[pl.ds(at_c * 3, 3)]

    def t_last():
        return remote(table_half, half(c), t_send.at[1], t_recv.at[1], other_core)

    def arrive(count, ref, sem, own):
        def step(n):
            @pl.when(n != own)
            def _():
                wait(ref.at[n], ref.at[n], sem.at[n])

        repeat(count, step)

    t_copy().start()
    wait(table_core, table_core, t_recv.at[0])
    table_p[plane] = table_part[pl.ds(c * 3, 3)] + table_core[...]
    start_all(16, tp_copy, plane)

    repeat(8, lambda n: wait(weight_far.at[n], weight_far.at[n], wb_recv.at[n]))
    weight_total[...] = total(weight_far, 8).astype(BF16)
    start_all(16, wc_copy, plane)
    local(weight_total, wc_slot(plane), wc_recv.at[plane]).start()

    repeat(4, lambda n: wait(pair_part(n), pair_in.at[n], pair_recv.at[n]))
    for at_z in range(8):
        run = [
            pair_in[at_x * 2 + at_z % 2, :, (at_z // 2) * 8 : (at_z // 2 + 1) * 8, :].astype(F32) for at_x in range(2)
        ]
        pair_out[:, at_z * 16 : (at_z + 1) * 16, :] = jnp.concatenate(run, axis=1).astype(BF16)
    local(pair_out, pair_h, out_sem.at[0]).start()

    arrive(16, table_p, tp_recv, plane)
    table_z[z] = total(table_p, 16)
    start_all(8, tz_copy, z)

    def lay_out(at_c):
        for n in range(16):
            first = at_c * 16 + n % 4 * 4 + n // 4
            weight_out[pl.ds(first, 32, stride=32), :] = weight_all[at_c, n * 32 : (n + 1) * 32, :].astype(F32)

    repeat(16, lambda n: wait(weight_total, wc_slot(n), wc_recv.at[n]))
    wd_copy().start()

    sent_all(16, rm_copy, own_row)
    sent_all(16, cm_copy, own_column)
    sent_all(4, cot_copy, own_cot)
    sent_all(16, l_copy, own_row)
    sent_all(2, r3_copy, -1)
    sent_all(2, gx_copy, -1)
    sent_all(4, gz_copy, own_gz)
    sent_all(16, gl_copy, own_gl)
    sent_all(16, wa_copy, plane)
    sent_all(8, wb_copy, z)
    sent_all(4, pair_copy, own_pair)
    wh_copy().wait_send()
    t_copy().wait_send()

    @pl.when(active)
    def _():
        sent_all(8, r2_copy, z)
        sent_all(8, r2_forward, z)
        gf_copy().wait_send()

    @pl.when(jnp.logical_not(active))
    def _():
        r1_copy().wait_send()

    wait(weight_all.at[1 - c], weight_all.at[1 - c], wh_recv.at[1])
    for at_c in range(2):
        lay_out(at_c)
    local(weight_out, weight_grad_h, out_sem.at[1]).start()
    sent_all(16, wc_copy, plane)
    sent_all(16, tp_copy, plane)
    wd_copy().wait_send()

    arrive(8, table_z, tz_recv, z)
    summed = total(table_z, 8)
    table_half[...] = summed
    t_last().start()
    table_all[pl.ds(c * 3, 3)] = summed
    sent_all(8, tz_copy, z)
    wait(table_half, half(1 - c), t_recv.at[1])
    for n in range(TILES):
        high = min(8, table_out.shape[0] - (n // 2) * 8)
        table_out[(n // 2) * 8 : (n // 2) * 8 + high, (n % 2) * 128 : (n % 2 + 1) * 128] = table_all[n][:high]
    t_last().wait_send()
    wait(pair_out, pair_h, out_sem.at[0])
    wait(weight_out, weight_grad_h, out_sem.at[1])


def shape(dims, dtype=BF16):
    return jax.ShapeDtypeStruct(dims, dtype)


def body(
    alignment_token_classes, deletions, alignment_mask, homolog_stack_values,
    letter_lookup_coefficients, gap_lookup_coefficients, standardize_gain, standardize_offset,
    first_factor_map, left_bias_vector, second_factor_map, right_bias_vector,
    output_weight_matrix, cotangent,
):
    kinds = letter_lookup_coefficients.shape[0]
    grades = np.arange(32, dtype=np.float32)
    steps = jnp.asarray(
        np.stack([(grades > 0).astype(np.float32), (2.0 / math.pi * np.arctan(grades / 3.0)).astype(np.float32)], 1)
    )
    inputs = [
        alignment_token_classes.T, deletions.T, alignment_mask.T, homolog_stack_values,
        letter_lookup_coefficients, gap_lookup_coefficients, steps,
        standardize_gain.reshape(1, 256), standardize_offset.reshape(1, 256),
        first_factor_map.T, left_bias_vector.reshape(1, 32), second_factor_map.T, right_bias_vector.reshape(1, 32),
        output_weight_matrix,
    ]
    vmem = pltpu.VMEM
    scratch = [vmem(value.shape, value.dtype) for value in inputs] + [
        vmem((8, 16, 16, 128), BF16), vmem((4, 8, 32, 128), BF16),
        vmem((128, 128), F32), vmem((ROWS, 128), F32), vmem((8, 128), F32),
        vmem((2, 512, 128), F32),
        vmem((128, WIDE), F32), vmem((384, 256), BF16), vmem((8, 384), F32),
        vmem((1024, 128), F32), vmem((1024, 128), BF16), vmem((128, 1024), BF16),
        vmem((2, 32, 256), BF16),
        vmem((512, 256), F32), vmem((512, 128), F32),
        vmem((ROWS, WIDE), BF16), vmem((ROWS, WIDE), BF16),
        vmem((4, 4, 8, 128), F32), vmem((4, 4, 8, 128), F32),
        vmem((4, 8, 32, 128), BF16),
        vmem((4, ROWS, 1024), BF16), vmem((4, 4, ROWS, WIDE), BF16),
        vmem((256, 1024), BF16), vmem((1024, 256), F32), vmem((256, 1024), F32),
        vmem((1024, 256), BF16),
        vmem((1024, 128), F32), vmem((1024, 128), BF16),
        vmem((1024, 1024), BF16), vmem((1024, 1024), BF16),
        vmem((32, 32, 128), BF16), vmem((4, 8, 32, 128), BF16),
        vmem((4, 4, ROWS, WIDE), BF16), vmem((256, 512), F32), vmem((2, 4, ROWS, WIDE), BF16),
        vmem((4, 2, ROWS, WIDE), BF16), vmem((8, 2, ROWS, WIDE), BF16),
        vmem((ROWS, WIDE), BF16), vmem((ROWS, WIDE), BF16),
        vmem((4, ROWS, 1024), BF16), vmem((16, ROWS, WIDE), BF16),
        vmem((1024, 128), F32), vmem((512, 128), F32), vmem((512, 128), BF16),
        vmem((16, 32, 128), BF16), vmem((32, 128), BF16),
        vmem((8, 32, 128), BF16), vmem((32, 128), BF16), vmem((2, 512, 128), BF16),
        vmem((TILES, 8, 128), F32), vmem((3, 8, 128), F32),
        vmem((16, 3, 8, 128), F32), vmem((8, 3, 8, 128), F32),
        vmem((3, 8, 128), F32), vmem((TILES, 8, 128), F32),
        vmem((8, 128, 128), BF16), vmem((1024, 128), F32),
    ]
    sizes = [len(inputs) + 1, 2, 16, 16, 16, 16, 4, 4, 1, 1, 16, 8, 2, 2, 16, 16]
    sizes += [2, 2, 4, 8, 1, 1, 16, 16, 4, 4, 2, 2, 16, 16, 8, 8, 16, 16, 2, 2, 16, 16, 8, 8]
    results = pl.pallas_call(
        kernel,
        out_shape=[shape((8, 128, 128)), shape((1024, 128), F32), shape((kinds, 256), F32)],
        in_specs=[pl.BlockSpec(memory_space=pl.ANY)] * (len(inputs) + 1),
        out_specs=[pl.BlockSpec(memory_space=pl.ANY)] * 2 + [pl.BlockSpec(memory_space=pltpu.VMEM)],
        scratch_shapes=scratch + [pltpu.SemaphoreType.DMA((size,)) for size in sizes],
        compiler_params=pltpu.CompilerParams(
            collective_id=0, has_side_effects=True, vmem_limit_bytes=60 * 1024 * 1024
        ),
        name="outer_product_mean",
    )(*inputs, cotangent.reshape(8, 16, 2, 16, 128))
    return pl.pallas_call(
        hand_over,
        out_shape=[shape(value.shape, value.dtype) for value in results],
        in_specs=[pl.BlockSpec(memory_space=pl.ANY)] * 3,
        out_specs=[pl.BlockSpec(memory_space=pl.ANY)] * 3,
        scratch_shapes=[vmem(value.shape, value.dtype) for value in results] + [pltpu.SemaphoreType.DMA((3,))],
        name="hand_over",
    )(*results)


def hand_over(pair, weight, table, pair_out, weight_out, table_out, pair_here, weight_here, table_here, sem):
    here = [pair_here, weight_here, table_here]
    arrive = [local(src, dst, sem.at[n]) for n, (src, dst) in enumerate(zip([pair, weight, table], here))]
    leave = [local(src, dst, sem.at[n]) for n, (src, dst) in enumerate(zip(here, [pair_out, weight_out, table_out]))]
    for copy in arrive:
        copy.start()
    for first, second in zip(arrive, leave):
        first.wait()
        second.start()
    for copy in leave:
        copy.wait()


def solution(mesh):
    in_specs = (
        P("seq", "res"), P("seq", "res"), P("seq", "res"), P("seq", "res", None),
        P(), P(), P(), P(), P(), P(), P(), P(), P(),
        P("res", None, None),
    )
    out_specs = (P("res", "seq", None), P(), P())
    return jax.shard_map(body, mesh=mesh, in_specs=in_specs, out_specs=out_specs, check_vma=False)
```

```python
import math

import jax
import jax.numpy as jnp
import numpy as np
from jax import lax
from jax.experimental import pallas as pl
from jax.experimental.pallas import tpu as pltpu
from jax.sharding import PartitionSpec as P

EPSILON = 1e-05
MESH = pl.DeviceIdType.MESH
F32 = jnp.float32
BF16 = jnp.bfloat16

ROWS = 64
WIDE = 256
TILES = 6


def device(y, z, xh, xl, c):
    return (y * 16 + z * 2 + xh, xl * 2 + c)


def repeat(count, step):
    lax.fori_loop(0, count, lambda n, carried: (step(n), carried)[1], 0)


def remote(src, dst, send, recv, target):
    return pltpu.make_async_remote_copy(
        src_ref=src, dst_ref=dst, send_sem=send, recv_sem=recv, device_id=target, device_id_type=MESH
    )


def start_all(count, copy, own):
    def step(n):
        @pl.when(n != own)
        def _():
            copy(n).start()

    repeat(count, step)


def local(src, dst, sem):
    return pltpu.make_async_copy(src, dst, sem)


def drain(sem, gauge, count):
    part = gauge.at[pl.ds(0, count)]
    local(part, part, sem).wait()


def sent(sem, gauge, count, own, unit=1):
    @pl.when(own >= 0)
    def _():
        drain(sem, gauge, count - unit)

    @pl.when(own < 0)
    def _():
        drain(sem, gauge, count)


def lanes(dims):
    return lax.broadcasted_iota(jnp.int32, dims, len(dims) - 1)


def block(n, size):
    return pl.ds(pl.multiple_of(n * size, size), size)


def swap(parts, stride):
    lane = lanes(parts[0].shape)
    low = lax.rem(lax.div(lane, stride), 2) == 0
    high = lax.rem(lax.div(lane, 2 * stride), 2) == 0

    def pair(first, second, step, keep):
        return (
            jnp.where(keep, first, pltpu.roll(second, step, 1)),
            jnp.where(keep, pltpu.roll(first, 128 - step, 1), second),
        )

    a, b = pair(parts[0], parts[1], stride, low)
    c, d = pair(parts[2], parts[3], stride, low)
    a, c = pair(a, c, 2 * stride, high)
    b, d = pair(b, d, 2 * stride, high)
    return [a, b, c, d]


def dot(first, second):
    return jnp.dot(first, second, preferred_element_type=F32)


def dot_nt(first, second):
    return lax.dot_general(first, second, (((1,), (1,)), ((), ())), preferred_element_type=F32)


def split(value, count):
    pieces = []
    for _ in range(count):
        piece = value.astype(BF16)
        pieces.append(piece)
        value = value - piece.astype(F32)
    return pieces


def total(ref, count):
    value = ref[0].astype(F32)
    for n in range(1, count):
        value = value + ref[n].astype(F32)
    return value


def kernel(
    token_h, deletion_h, mask_h, stack_h, letters_h, gaps_h, steps_h, gain_h, offset_h,
    left_map_h, left_bias_h, right_map_h, right_bias_h, weight_h, cotangent,
    pair_h, weight_grad_h, table_out,
    token, deletion, mask, stack_raw, letters, gaps, steps, gain, offset,
    left_map, left_bias, right_map, right_bias, weight_raw, cot_raw, cot_stage,
    square, turned, mask_rows, stack, table, maps, bias, weight_wide, weight, weight_turned, hot_turned,
    white, spread, left_own, right_own, row_masks, column_masks, cot_all, left_all, right_all,
    right_mat, wide_grad, wide_outer, product, counts, scaled, folded, grad_outer, pair, pair_in,
    right_grad, right_part, right_core, right_sum, right_in, right_last, right_send, left_grad, left_in,
    weight_grad, weight_core, weight_half, weight_in, weight_sum, weight_far, weight_total, weight_all,
    table_part, table_core, table_p, table_z, table_half, table_all, pair_out, weight_out,
    gauge, gauge_m, gauge_w, gauge_t,
    in_sem, out_sem, rm_send, rm_recv, cm_send, cm_recv, cot_send, cot_recv,
    r1_send, r1_recv, r2_send, r2_recv, r3_send, r3_recv, l_send, l_recv,
    gx_send, gx_recv, gz_send, gz_recv, gf_send, gf_recv, gl_send, gl_recv, pair_send, pair_recv,
    wh_send, wh_recv, wa_send, wa_recv, wb_send, wb_recv, wc_send, wc_recv,
    t_send, t_recv, tp_send, tp_recv, tz_send, tz_recv,
):
    res = lax.axis_index("res")
    q = lax.axis_index("seq")
    y, z, xh = lax.div(res, 16), lax.rem(lax.div(res, 2), 8), lax.rem(res, 2)
    xl, c = lax.div(q, 2), lax.rem(q, 2)
    zi, parity = lax.div(z, 2), lax.rem(z, 2)
    active = parity == xl
    inside = lax.div(y, 2) == c
    other_q = (1 - xl) * 2 + c
    plane = y * 4 + xh * 2 + xl
    band = lax.rem(y, 2) * 2 + xh
    own_column = jnp.where(active, z * 2 + c, -1)
    own_row = jnp.where(inside, plane, -1)
    other_core = device(y, z, xh, xl, 1 - c)
    partner = device(y, z, xh, 1 - xl, c)

    def wait(src, dst, sem):
        local(src, dst, sem).wait()

    loads = [
        local(src, dst, in_sem.at[n])
        for n, (src, dst) in enumerate(
            [
                (token_h, token), (deletion_h, deletion), (mask_h, mask), (stack_h, stack_raw),
                (letters_h, letters), (gaps_h, gaps), (steps_h, steps), (gain_h, gain), (offset_h, offset),
                (left_map_h, left_map), (left_bias_h, left_bias), (right_map_h, right_map),
                (right_bias_h, right_bias), (weight_h, weight_raw), (cotangent.at[:, :, xl], cot_raw),
            ]
        )
    ]
    for load in loads:
        load.start()

    barrier = pltpu.get_barrier_semaphore()

    def signal(target):
        pl.semaphore_signal(barrier, inc=1, device_id=target, device_id_type=MESH)

    def greet(n):
        @pl.when(n != z * 4 + q)
        def _():
            signal((y * 16 + lax.div(n, 4) * 2 + xh, lax.rem(n, 4)))

        @pl.when(n != (y * 2 + xh) * 4 + q)
        def _():
            signal((lax.div(n, 8) * 16 + z * 2 + lax.rem(lax.div(n, 4), 2), lax.rem(n, 4)))

    repeat(32, greet)

    def line_user(n):
        return device(y, lax.div(n, 2), xh, parity, lax.rem(n, 2))

    def plane_user(n):
        return device(lax.div(n, 4), z, lax.div(lax.rem(n, 4), 2), lax.rem(n, 2), lax.div(y, 2))

    def rm_copy(n):
        return remote(mask_rows, row_masks.at[band, q], rm_send, rm_recv, plane_user(n))

    def cm_copy(n):
        return remote(mask_rows, column_masks.at[zi, q], cm_send, cm_recv, line_user(n))

    def cot_copy(n):
        return remote(cot_stage.at[n], cot_all.at[band], cot_send, cot_recv, device(n, z, c, xl, lax.div(y, 2)))

    own_cot = jnp.where(jnp.logical_and(inside, xh == c), y, -1)

    def left_slot(at_band, at_q):
        return left_all.at[at_q, :, block(at_band, WIDE)]

    def l_copy(n):
        return remote(left_own, left_slot(band, q), l_send, l_recv, plane_user(n))

    def r1_copy():
        return remote(right_own, right_all.at[zi, q], r1_send, r1_recv, partner)

    def r2_copy(n):
        return remote(
            right_own, right_all.at[zi, q], r2_send, r2_recv, device(y, n, xh, xl, c)
        )

    def r2_forward(n):
        return remote(
            right_all.at[zi, other_q], right_all.at[zi, other_q], r2_send, r2_recv,
            device(y, n, xh, xl, c),
        )

    def r3_copy(n):
        at_q = n * 2 + c
        return remote(right_all.at[:, at_q], right_all.at[:, at_q], r3_send, r3_recv, other_core)

    for load in loads[:13]:
        load.wait()
    mask_value = mask[...].astype(F32)
    empty = jnp.zeros((8, ROWS), F32)
    mask_rows[...] = jnp.where(
        c == 0, jnp.concatenate([mask_value, empty], axis=1), jnp.concatenate([empty, mask_value], axis=1)
    )
    square[...] = jnp.zeros((128, 128), F32)
    square[0:8, 0:ROWS] = token[...].astype(F32)
    square[8:16, 0:ROWS] = deletion[...].astype(F32)
    square[16:24, 0:ROWS] = mask_value
    turned[...] = square[...].T[:ROWS]
    for n in range(2):
        stack[n] = stack_raw[:, :, n * 128 : (n + 1) * 128].astype(F32).reshape(512, 128)
    table[...] = jnp.zeros((128, WIDE), F32)
    table[: letters.shape[0], :] = letters[...]
    table[32:64, :] = steps[:, 0:1] * gaps[0:1, :] + steps[:, 1:2] * gaps[1:2, :]
    spread_left = (
        lax.rem(lax.broadcasted_iota(jnp.int32, (128, 32), 0), 32) == lanes((128, 32))
    ).astype(F32).astype(BF16)
    spread_right = (
        lax.div(lax.broadcasted_iota(jnp.int32, (WIDE, 32), 0), 8) == lanes((WIDE, 32))
    ).astype(F32).astype(BF16)
    maps[:128, :] = dot(spread_left, left_map[...]).astype(BF16)
    maps[128:, :] = dot(spread_right, right_map[...]).astype(BF16)
    bias[...] = jnp.concatenate(
        [
            sum(dot_nt(piece, spread_left) for piece in split(jnp.broadcast_to(left_bias[...], (8, 32)), 3)),
            sum(dot_nt(piece, spread_right) for piece in split(jnp.broadcast_to(right_bias[...], (8, 32)), 3)),
        ],
        axis=1,
    )
    loads[14].wait()
    for n in range(4):
        strip = cot_raw[:, n * 4 : n * 4 + 4].astype(F32)
        strip = jnp.where(c == 0, strip[:, :, :8, :], strip[:, :, 8:, :])
        cot_stage[n] = strip.reshape(8, 32, 128).astype(BF16)
    lane = lanes((ROWS, 128))
    fine = lane.astype(F32)
    wide_lane = lanes((ROWS, WIDE))
    pieces = split(table[...], 3)
    right_value = jnp.zeros((ROWS, WIDE), F32)
    for h in range(2):
        hot = jnp.concatenate(
            [
                jnp.logical_or(fine == turned[:, i : i + 1], fine == turned[:, 8 + i : 9 + i] + 32.0).astype(F32)
                for i in range(h * 4, h * 4 + 4)
            ],
            axis=0,
        )
        hot_turned[h] = hot.T[:32].astype(BF16)
        hot = hot.astype(BF16)
        hidden = jnp.concatenate(
            [
                jnp.concatenate([stack[n, pl.ds(i, ROWS, stride=8), :] for i in range(h * 4, h * 4 + 4)], axis=0)
                for n in range(2)
            ],
            axis=1,
        ) + (dot(hot, pieces[0]) + dot(hot, pieces[1]) + dot(hot, pieces[2]))
        centered = hidden - jnp.mean(hidden, axis=-1, keepdims=True)
        variance = jnp.mean(centered * centered, axis=-1, keepdims=True)
        scale = lax.rsqrt(variance + EPSILON)
        whitened = centered * scale
        white[h * 256 : (h + 1) * 256, :] = whitened
        spread[h * 256 : (h + 1) * 256, :] = jnp.broadcast_to(scale, (256, 128))
        normed = (whitened * gain[...] + offset[...]).astype(BF16)
        rows = dot_nt(normed, maps[...]) + bias[:1, :]
        left_value = jnp.zeros((ROWS, 128), F32)
        for i in range(4):
            part = turned[:, 16 + h * 4 + i : 17 + h * 4 + i] * rows[i * ROWS : (i + 1) * ROWS, :]
            left_value = jnp.where(lax.div(lane, 32) == i, part[:, :128], left_value)
            right_value = jnp.where(lax.rem(wide_lane, 8) == h * 4 + i, part[:, 128:], right_value)
        left_own[:, h * 128 : (h + 1) * 128] = left_value.astype(BF16)
        if h == 0:
            pl.semaphore_wait(barrier, 62)
            start_all(4, cot_copy, own_cot)
            start_all(16, rm_copy, own_row)
            start_all(16, cm_copy, own_column)

            @pl.when(inside)
            def _():
                local(mask_rows, row_masks.at[band, q], rm_recv).start()

            @pl.when(jnp.logical_and(inside, xh == c))
            def _():
                local(cot_stage.at[y], cot_all.at[band], cot_recv).start()

            @pl.when(active)
            def _():
                local(mask_rows, column_masks.at[zi, q], cm_recv).start()

    right_own[...] = right_value.astype(BF16)

    @pl.when(jnp.logical_not(active))
    def _():
        r1_copy().start()

    @pl.when(active)
    def _():
        start_all(8, r2_copy, z)
        local(right_own, right_all.at[zi, q], r2_recv).start()

    start_all(16, l_copy, own_row)

    @pl.when(inside)
    def _():
        local(left_own, left_slot(band, q), l_recv).start()

    @pl.when(active)
    def _():
        wait(right_own, right_all.at[zi, other_q], r1_recv)
        start_all(8, r2_forward, z)

    loads[13].wait()
    weight_wide[...] = weight_raw[...].astype(F32)
    for t in range(2):
        for b in range(4):
            for a in range(4):
                at = ((t * 4 + b) * 4 + a) * 32
                weight[at : at + 32, :] = weight_wide[pl.ds(t * 16 + a * 4 + b, 32, stride=32), :].astype(BF16)
    for t in range(8):
        weight_turned[:, t * 128 : (t + 1) * 128] = weight[t * 128 : (t + 1) * 128, :].astype(F32).T.astype(BF16)

    wait(row_masks, row_masks, rm_recv)
    wait(column_masks, column_masks, cm_recv)
    column_mask = jnp.concatenate(
        [
            jnp.concatenate([column_masks[b, 2 * h] + column_masks[b, 2 * h + 1] for h in range(2)], axis=1)
            for b in range(4)
        ],
        axis=0,
    )
    for i in range(32):
        row = jnp.concatenate(
            [
                row_masks[i // 8, 2 * h, i % 8 : i % 8 + 1, :] + row_masks[i // 8, 2 * h + 1, i % 8 : i % 8 + 1, :]
                for h in range(2)
            ],
            axis=1,
        )
        product[i * 32 : (i + 1) * 32, :] = (row * column_mask).astype(BF16)
    counts[...] = dot(product[...], jnp.ones((256, 128), BF16))
    wait(cot_all, cot_all, cot_recv)
    for n in range(4):
        cot = cot_all[n].astype(F32).reshape(256, 128)
        scaled[n * 256 : (n + 1) * 256, :] = (cot / counts[n * 256 : (n + 1) * 256, :]).astype(BF16)

    def backward(g):
        span = block(g, 256)
        wide_grad[...] = dot_nt(weight[...], scaled[span, :])
        for t in range(8):
            for half in range(2):
                lane_part = wide_grad[t * 128 : (t + 1) * 128, half * 128 : (half + 1) * 128]
                parts = swap([lane_part[a * 32 : (a + 1) * 32, :] for a in range(4)], 32)
                for i, part in enumerate(parts):
                    at = pl.ds(pl.multiple_of(g * 256 + half * 128 + i * 32, 32), 32)
                    grad_outer[at, t * 128 : (t + 1) * 128] = part.astype(BF16)

    repeat(4, backward)

    def right_step(t):
        for b in range(2):
            right_part[:, b * 256 : (b + 1) * 256] = dot(
                left_all[...].reshape(256, 1024), grad_outer[:, t * 512 + b * 256 : t * 512 + (b + 1) * 256]
            )
        for at_q in range(4):
            rows = slice(at_q * ROWS, (at_q + 1) * ROWS)
            parts = swap([right_part[rows, b * 128 : (b + 1) * 128] for b in range(4)], 8)
            for b, part in enumerate(parts):
                right_grad[b, at_q, :, t * 128 : (t + 1) * 128] = part.astype(BF16)

    def gx_copy(n):
        return remote(right_grad.at[:, n * 2 + 1 - c], right_core.at[n], gx_send, gx_recv, other_core)

    wait(left_all, left_all, l_recv)
    right_step(0)
    right_step(1)
    start_all(2, gx_copy, -1)

    @pl.when(active)
    def _():
        drain(r2_recv, gauge, 7)

    @pl.when(jnp.logical_not(active))
    def _():
        drain(r2_recv, gauge, 8)

    start_all(2, r3_copy, -1)
    def gz_copy(n):
        return remote(
            right_sum.at[n], right_in.at[z], gz_send, gz_recv, device(y, n * 2 + xl, xh, xl, c)
        )

    own_gz = jnp.where(active, zi, -1)
    wait(right_core, right_core, gx_recv)
    for n in range(2):
        for b in range(4):
            right_sum[b, n] = (right_grad[b, n * 2 + c].astype(F32) + right_core[n, b].astype(F32)).astype(BF16)
    start_all(4, gz_copy, own_gz)

    @pl.when(active)
    def _():
        local(right_sum.at[zi], right_in.at[z], gz_recv).start()

    drain(r3_recv, gauge, 8)
    for at_q in range(4):
        rows = slice(at_q * ROWS, (at_q + 1) * ROWS)
        for t in range(2):
            parts = [right_all[b, at_q, :, t * 128 : (t + 1) * 128].astype(F32) for b in range(4)]
            for b, part in enumerate(swap(parts, 8)):
                right_mat[rows, (t * 4 + b) * 128 : (t * 4 + b + 1) * 128] = part.astype(BF16)


    def gl_part(n):
        return left_grad.at[lax.rem(n, 4), :, block(lax.div(n, 4), WIDE)]

    def gl_copy(n):
        target = device(c * 2 + lax.div(n, 8), z, lax.rem(lax.div(n, 4), 2), lax.div(lax.rem(n, 4), 2), lax.rem(n, 2))
        return remote(gl_part(n), left_in.at[plane], gl_send, gl_recv, target)

    own_gl = jnp.where(inside, band * 4 + q, -1)

    def left_step(g):
        span = block(g, 256)
        part = dot_nt(right_mat[...], grad_outer[span, :]).astype(BF16)
        for at_q in range(4):
            left_grad[at_q, :, span] = part[at_q * ROWS : (at_q + 1) * ROWS, :]

    for g in range(4):
        left_step(g)

        def start_left(n):
            @pl.when(n + g * 4 != own_gl)
            def _():
                gl_copy(n + g * 4).start()

        repeat(4, start_left)

    @pl.when(inside)
    def _():
        local(gl_part(band * 4 + q), left_in.at[plane], gl_recv).start()

    def forward(g):
        lead = left_all[:, :, block(g, 256)].reshape(256, 256).astype(F32).T.astype(BF16)
        wide_outer[...] = dot(lead, right_mat[...])
        for half in range(2):
            span = pl.ds(pl.multiple_of(g * 256 + half * 128, 128), 128)
            for t in range(8):
                tile = wide_outer[half * 128 : (half + 1) * 128, t * 128 : (t + 1) * 128]
                parts = swap([tile[i * 32 : (i + 1) * 32, :] for i in range(4)], 32)
                for a, part in enumerate(parts):
                    folded[(t * 4 + a) * 32 : (t * 4 + a + 1) * 32, span] = part.astype(BF16)

    def project(g):
        span = block(g, 256)
        value = dot(weight_turned[...], folded[:, span])
        update = (value.T / counts[span, :]).astype(BF16)
        pair[block(g, 8)] = update.reshape(8, 32, 128)

    repeat(4, forward)
    weight_grad[...] = dot(folded[...], scaled[...])

    def plane_peer(n):
        return device(lax.div(n, 4), z, lax.div(lax.rem(n, 4), 2), lax.rem(n, 2), c)

    def line_peer(n):
        return device(y, n, xh, xl, c)

    def wh_copy():
        return remote(weight_grad.at[block(1 - c, 512), :], weight_core, wh_send.at[0], wh_recv.at[0], other_core)

    def wa_part(n):
        return weight_half.at[block(n, 32), :]

    def wa_copy(n):
        return remote(wa_part(n), weight_in.at[plane], wa_send, wa_recv, plane_peer(n))

    def wb_copy(n):
        return remote(weight_sum, weight_far.at[z], wb_send, wb_recv, line_peer(n))

    def wc_slot(n):
        return weight_all.at[c, block(n, 32), :]

    def wc_copy(n):
        return remote(weight_total, wc_slot(plane), wc_send, wc_recv, plane_peer(n))

    def wd_copy():
        return remote(weight_all.at[c], weight_all.at[c], wh_send.at[1], wh_recv.at[1], other_core)

    wh_copy().start()
    repeat(4, project)
    wait(weight_core, weight_core, wh_recv.at[0])
    weight_half[...] = (weight_grad[block(c, 512), :] + weight_core[...]).astype(BF16)
    start_all(16, wa_copy, plane)
    local(wa_part(plane), weight_in.at[plane], wa_recv).start()

    def pair_part(n):
        return pair.at[block(n, 8)]

    def pair_copy(n):
        target = device(c * 2 + lax.div(n, 2), z, lax.rem(n, 2), lax.div(y, 2), lax.rem(y, 2))
        return remote(pair_part(n), pair_in.at[xh * 2 + xl], pair_send, pair_recv, target)

    keeps_pair = jnp.logical_and(inside, q == y)
    own_pair = jnp.where(keeps_pair, band, -1)
    start_all(4, pair_copy, own_pair)

    @pl.when(keeps_pair)
    def _():
        local(pair_part(band), pair_in.at[xh * 2 + xl], pair_recv).start()

    def gf_copy():
        return remote(right_send, right_last, gf_send, gf_recv, partner)

    @pl.when(active)
    def _():
        wait(right_in, right_in, gz_recv)
        away = right_in[0, 1 - xl].astype(F32)
        for n in range(1, 8):
            away = away + right_in[n, 1 - xl].astype(F32)
        right_send[...] = away.astype(BF16)
        gf_copy().start()
        here = right_in[0, xl].astype(F32)
        for n in range(1, 8):
            here = here + right_in[n, xl].astype(F32)
        right_last[...] = here.astype(BF16)

    wait(left_in, left_in, gl_recv)
    left_total = total(left_in, 16).astype(BF16).astype(F32)

    @pl.when(jnp.logical_not(active))
    def _():
        wait(right_last, right_last, gf_recv)

    right_total = right_last[...].astype(F32)

    wait(weight_in, weight_in, wa_recv)
    weight_sum[...] = total(weight_in, 16).astype(BF16)
    start_all(8, wb_copy, z)
    local(weight_sum, weight_far.at[z], wb_recv).start()

    sums = jnp.zeros((32, WIDE), F32)
    for h in range(2):
        picked = []
        for i in range(4):
            keep = turned[:, 16 + h * 4 + i : 17 + h * 4 + i]
            tile = left_total[:, h * 128 : (h + 1) * 128]
            picked.append(
                jnp.concatenate(
                    [
                        jnp.where(lax.div(lane, 32) == i, tile, 0.0) * keep,
                        jnp.where(lax.rem(wide_lane, 8) == h * 4 + i, right_total, 0.0) * keep,
                    ],
                    axis=1,
                )
            )
        picked = jnp.concatenate(picked, axis=0).astype(BF16)
        gained = dot(picked, maps[...]) * gain[...]
        whitened = white[h * 256 : (h + 1) * 256, :]
        stream_grad = spread[h * 256 : (h + 1) * 256, :1] * (
            gained
            - jnp.mean(gained, axis=-1, keepdims=True)
            - whitened * jnp.mean(gained * whitened, axis=-1, keepdims=True)
        )
        for piece in split(stream_grad, 2):
            sums = sums + dot(hot_turned[h], piece)
    for n in range(TILES):
        table_part[n] = sums[(n // 2) * 8 : (n // 2 + 1) * 8, (n % 2) * 128 : (n % 2 + 1) * 128]

    def t_copy():
        return remote(table_part.at[pl.ds((1 - c) * 3, 3)], table_core, t_send.at[0], t_recv.at[0], other_core)

    def tp_copy(n):
        return remote(table_p.at[plane], table_p.at[plane], tp_send, tp_recv, plane_peer(n))

    def tz_copy(n):
        return remote(table_z.at[z], table_z.at[z], tz_send, tz_recv, device(y, n, xh, xl, c))

    def half(at_c):
        return table_all.at[pl.ds(at_c * 3, 3)]

    def t_last():
        return remote(table_half, half(c), t_send.at[1], t_recv.at[1], other_core)

    t_copy().start()
    wait(table_core, table_core, t_recv.at[0])
    table_p[plane] = table_part[pl.ds(c * 3, 3)] + table_core[...]
    start_all(16, tp_copy, plane)

    wait(weight_far, weight_far, wb_recv)
    weight_total[...] = total(weight_far, 8).astype(BF16)
    start_all(16, wc_copy, plane)
    local(weight_total, wc_slot(plane), wc_recv).start()

    wait(pair_in, pair_in, pair_recv)
    for at_z in range(8):
        run = [
            pair_in[at_x * 2 + at_z % 2, :, (at_z // 2) * 8 : (at_z // 2 + 1) * 8, :].astype(F32) for at_x in range(2)
        ]
        pair_out[:, at_z * 16 : (at_z + 1) * 16, :] = jnp.concatenate(run, axis=1).astype(BF16)
    local(pair_out, pair_h, out_sem.at[0]).start()

    drain(tp_recv, gauge_t, 15)
    table_z[z] = total(table_p, 16)
    start_all(8, tz_copy, z)

    def lay_out(at_c):
        for n in range(16):
            first = at_c * 16 + n % 4 * 4 + n // 4
            weight_out[pl.ds(first, 32, stride=32), :] = weight_all[at_c, n * 32 : (n + 1) * 32, :].astype(F32)

    wait(weight_all.at[c], weight_all.at[c], wc_recv)
    wd_copy().start()

    sent(rm_send, gauge_m, 16, own_row)
    sent(cm_send, gauge_m, 16, own_column)
    sent(cot_send, gauge, 8, own_cot, 2)
    sent(l_send, gauge, 16, own_row)
    drain(r3_send, gauge, 8)
    drain(gx_send, gauge, 8)
    sent(gz_send, gauge, 8, own_gz, 2)
    sent(gl_send, gauge, 16, own_gl)
    drain(wa_send, gauge_w, 15)
    drain(wb_send, gauge_w, 7)
    sent(pair_send, gauge, 8, own_pair, 2)
    wh_copy().wait_send()
    t_copy().wait_send()

    @pl.when(active)
    def _():
        drain(r2_send, gauge, 14)
        gf_copy().wait_send()

    @pl.when(jnp.logical_not(active))
    def _():
        r1_copy().wait_send()

    wait(weight_all.at[1 - c], weight_all.at[1 - c], wh_recv.at[1])
    for at_c in range(2):
        lay_out(at_c)
    local(weight_out, weight_grad_h, out_sem.at[1]).start()
    drain(wc_send, gauge_w, 15)
    drain(tp_send, gauge_t, 15)
    wd_copy().wait_send()

    drain(tz_recv, gauge_t, 7)
    summed = total(table_z, 8)
    table_half[...] = summed
    t_last().start()
    table_all[pl.ds(c * 3, 3)] = summed
    drain(tz_send, gauge_t, 7)
    wait(table_half, half(1 - c), t_recv.at[1])
    for n in range(TILES):
        high = min(8, table_out.shape[0] - (n // 2) * 8)
        table_out[(n // 2) * 8 : (n // 2) * 8 + high, (n % 2) * 128 : (n % 2 + 1) * 128] = table_all[n][:high]
    t_last().wait_send()
    wait(pair_out, pair_h, out_sem.at[0])
    wait(weight_out, weight_grad_h, out_sem.at[1])


def shape(dims, dtype=BF16):
    return jax.ShapeDtypeStruct(dims, dtype)


def body(
    alignment_token_classes, deletions, alignment_mask, homolog_stack_values,
    letter_lookup_coefficients, gap_lookup_coefficients, standardize_gain, standardize_offset,
    first_factor_map, left_bias_vector, second_factor_map, right_bias_vector,
    output_weight_matrix, cotangent,
):
    kinds = letter_lookup_coefficients.shape[0]
    grades = np.arange(32, dtype=np.float32)
    steps = jnp.asarray(
        np.stack([(grades > 0).astype(np.float32), (2.0 / math.pi * np.arctan(grades / 3.0)).astype(np.float32)], 1)
    )
    inputs = [
        alignment_token_classes.T, deletions.T, alignment_mask.T, homolog_stack_values,
        letter_lookup_coefficients, gap_lookup_coefficients, steps,
        standardize_gain.reshape(1, 256), standardize_offset.reshape(1, 256),
        first_factor_map.T, left_bias_vector.reshape(1, 32), second_factor_map.T, right_bias_vector.reshape(1, 32),
        output_weight_matrix,
    ]
    vmem = pltpu.VMEM
    scratch = [vmem(value.shape, value.dtype) for value in inputs] + [
        vmem((8, 16, 16, 128), BF16), vmem((4, 8, 32, 128), BF16),
        vmem((128, 128), F32), vmem((ROWS, 128), F32), vmem((8, 128), F32),
        vmem((2, 512, 128), F32),
        vmem((128, WIDE), F32), vmem((384, 256), BF16), vmem((8, 384), F32),
        vmem((1024, 128), F32), vmem((1024, 128), BF16), vmem((128, 1024), BF16),
        vmem((2, 32, 256), BF16),
        vmem((512, 256), F32), vmem((512, 128), F32),
        vmem((ROWS, WIDE), BF16), vmem((ROWS, WIDE), BF16),
        vmem((4, 4, 8, 128), F32), vmem((4, 4, 8, 128), F32),
        vmem((4, 8, 32, 128), BF16),
        vmem((4, ROWS, 1024), BF16), vmem((4, 4, ROWS, WIDE), BF16),
        vmem((256, 1024), BF16), vmem((1024, 256), F32), vmem((256, 1024), F32),
        vmem((1024, 256), BF16),
        vmem((1024, 128), F32), vmem((1024, 128), BF16),
        vmem((1024, 1024), BF16), vmem((1024, 1024), BF16),
        vmem((32, 32, 128), BF16), vmem((4, 8, 32, 128), BF16),
        vmem((4, 4, ROWS, WIDE), BF16), vmem((256, 512), F32), vmem((2, 4, ROWS, WIDE), BF16),
        vmem((4, 2, ROWS, WIDE), BF16), vmem((8, 2, ROWS, WIDE), BF16),
        vmem((ROWS, WIDE), BF16), vmem((ROWS, WIDE), BF16),
        vmem((4, ROWS, 1024), BF16), vmem((16, ROWS, WIDE), BF16),
        vmem((1024, 128), F32), vmem((512, 128), F32), vmem((512, 128), BF16),
        vmem((16, 32, 128), BF16), vmem((32, 128), BF16),
        vmem((8, 32, 128), BF16), vmem((32, 128), BF16), vmem((2, 512, 128), BF16),
        vmem((TILES, 8, 128), F32), vmem((3, 8, 128), F32),
        vmem((16, 3, 8, 128), F32), vmem((8, 3, 8, 128), F32),
        vmem((3, 8, 128), F32), vmem((TILES, 8, 128), F32),
        vmem((8, 128, 128), BF16), vmem((1024, 128), F32),
        vmem((16, ROWS, WIDE), BF16), vmem((16, 8, 128), F32),
        vmem((16, 32, 128), BF16), vmem((16, 3, 8, 128), F32),
    ]
    sizes = [
        len(inputs) + 1, 2, 0, 0, 0, 0, 0, 0, 0, 0, 0, 0, 0, 0, 0, 0, 0, 0, 0, 0, 0, 0, 0, 0, 0, 0, 2, 2, 0,
        0, 0, 0, 0, 0, 2, 2, 0, 0, 0, 0,
    ]
    results = pl.pallas_call(
        kernel,
        out_shape=[shape((8, 128, 128)), shape((1024, 128), F32), shape((kinds, 256), F32)],
        in_specs=[pl.BlockSpec(memory_space=pl.ANY)] * (len(inputs) + 1),
        out_specs=[pl.BlockSpec(memory_space=pl.ANY)] * 2 + [pl.BlockSpec(memory_space=pltpu.VMEM)],
        scratch_shapes=scratch + [pltpu.SemaphoreType.DMA((size,)) if size else pltpu.SemaphoreType.DMA for size in sizes],
        compiler_params=pltpu.CompilerParams(
            collective_id=0, has_side_effects=True, vmem_limit_bytes=60 * 1024 * 1024
        ),
        name="outer_product_mean",
    )(*inputs, cotangent.reshape(8, 16, 2, 16, 128))
    return pl.pallas_call(
        hand_over,
        out_shape=[shape(value.shape, value.dtype) for value in results],
        in_specs=[pl.BlockSpec(memory_space=pl.ANY)] * 3,
        out_specs=[pl.BlockSpec(memory_space=pl.ANY)] * 3,
        scratch_shapes=[vmem(value.shape, value.dtype) for value in results] + [pltpu.SemaphoreType.DMA((3,))],
        name="hand_over",
    )(*results)


def hand_over(pair, weight, table, pair_out, weight_out, table_out, pair_here, weight_here, table_here, sem):
    here = [pair_here, weight_here, table_here]
    arrive = [local(src, dst, sem.at[n]) for n, (src, dst) in enumerate(zip([pair, weight, table], here))]
    leave = [local(src, dst, sem.at[n]) for n, (src, dst) in enumerate(zip(here, [pair_out, weight_out, table_out]))]
    for copy in arrive:
        copy.start()
    for first, second in zip(arrive, leave):
        first.wait()
        second.start()
    for copy in leave:
        copy.wait()


def solution(mesh):
    in_specs = (
        P("seq", "res"), P("seq", "res"), P("seq", "res"), P("seq", "res", None),
        P(), P(), P(), P(), P(), P(), P(), P(), P(),
        P("res", None, None),
    )
    out_specs = (P("res", "seq", None), P(), P())
    return jax.shard_map(body, mesh=mesh, in_specs=in_specs, out_specs=out_specs, check_vma=False)
```

```python
import math

import jax
import jax.numpy as jnp
import numpy as np
from jax import lax
from jax.experimental import pallas as pl
from jax.experimental.pallas import tpu as pltpu
from jax.sharding import PartitionSpec as P

EPSILON = 1e-05
MESH = pl.DeviceIdType.MESH
F32 = jnp.float32
BF16 = jnp.bfloat16

ROWS = 64
WIDE = 256
TILES = 6


def device(y, z, xh, xl, c):
    return (y * 16 + z * 2 + xh, xl * 2 + c)


def repeat(count, step):
    lax.fori_loop(0, count, lambda n, carried: (step(n), carried)[1], 0)


def remote(src, dst, send, recv, target):
    return pltpu.make_async_remote_copy(
        src_ref=src, dst_ref=dst, send_sem=send, recv_sem=recv, device_id=target, device_id_type=MESH
    )


def start_all(count, copy, own):
    for n in range(count):

        @pl.when(own != n)
        def _(n=n):
            copy(n).start()


def local(src, dst, sem):
    return pltpu.make_async_copy(src, dst, sem)


def drain(sem, gauge, count):
    part = gauge.at[pl.ds(0, count)]
    local(part, part, sem).wait()


def sent(sem, gauge, count, own, unit=1):
    @pl.when(own >= 0)
    def _():
        drain(sem, gauge, count - unit)

    @pl.when(own < 0)
    def _():
        drain(sem, gauge, count)


def lanes(dims):
    return lax.broadcasted_iota(jnp.int32, dims, len(dims) - 1)


def block(n, size):
    return pl.ds(pl.multiple_of(n * size, size), size)


def swap(parts, stride):
    lane = lanes(parts[0].shape)
    low = lax.rem(lax.div(lane, stride), 2) == 0
    high = lax.rem(lax.div(lane, 2 * stride), 2) == 0

    def pair(first, second, step, keep):
        return (
            jnp.where(keep, first, pltpu.roll(second, step, 1)),
            jnp.where(keep, pltpu.roll(first, 128 - step, 1), second),
        )

    a, b = pair(parts[0], parts[1], stride, low)
    c, d = pair(parts[2], parts[3], stride, low)
    a, c = pair(a, c, 2 * stride, high)
    b, d = pair(b, d, 2 * stride, high)
    return [a, b, c, d]


def dot(first, second):
    return jnp.dot(first, second, preferred_element_type=F32)


def dot_nt(first, second):
    return lax.dot_general(first, second, (((1,), (1,)), ((), ())), preferred_element_type=F32)


def split(value, count):
    pieces = []
    for _ in range(count):
        piece = value.astype(BF16)
        pieces.append(piece)
        value = value - piece.astype(F32)
    return pieces


def total(ref, count):
    value = ref[0].astype(F32)
    for n in range(1, count):
        value = value + ref[n].astype(F32)
    return value


def kernel(
    token_h, deletion_h, mask_h, stack_h, letters_h, gaps_h, steps_h, gain_h, offset_h,
    left_map_h, left_bias_h, right_map_h, right_bias_h, weight_h, cotangent,
    pair_h, weight_grad_h, table_out,
    token, deletion, mask, stack_raw, letters, gaps, steps, gain, offset,
    left_map, left_bias, right_map, right_bias, weight_raw, cot_raw, cot_stage,
    square, turned, mask_rows, stack, table, maps, bias, weight_wide, weight, weight_turned, hot_turned,
    white, spread, left_own, right_own, row_masks, column_masks, cot_all, left_all, right_all,
    right_mat, wide_grad, wide_outer, product, counts, scaled, folded, grad_outer, pair, pair_in,
    right_grad, right_part, right_core, right_sum, right_in, right_last, right_send, left_grad, left_in,
    weight_grad, weight_core, weight_half, weight_in, weight_sum, weight_far, weight_total, weight_all,
    table_part, table_core, table_p, table_z, table_half, table_all, pair_out, weight_out,
    gauge, gauge_m, gauge_w, gauge_t,
    in_sem, out_sem, rm_send, rm_recv, cm_send, cm_recv, cot_send, cot_recv,
    r1_send, r1_recv, r2_send, r2_recv, r3_send, r3_recv, l_send, l_recv,
    gx_send, gx_recv, gz_send, gz_recv, gf_send, gf_recv, gl_send, gl_recv, pair_send, pair_recv,
    wh_send, wh_recv, wa_send, wa_recv, wb_send, wb_recv, wc_send, wc_recv,
    t_send, t_recv, tp_send, tp_recv, tz_send, tz_recv,
):
    res = lax.axis_index("res")
    q = lax.axis_index("seq")
    y, z, xh = lax.div(res, 16), lax.rem(lax.div(res, 2), 8), lax.rem(res, 2)
    xl, c = lax.div(q, 2), lax.rem(q, 2)
    zi, parity = lax.div(z, 2), lax.rem(z, 2)
    active = parity == xl
    inside = lax.div(y, 2) == c
    other_q = (1 - xl) * 2 + c
    plane = y * 4 + xh * 2 + xl
    band = lax.rem(y, 2) * 2 + xh
    own_column = jnp.where(active, z * 2 + c, -1)
    own_row = jnp.where(inside, plane, -1)
    other_core = device(y, z, xh, xl, 1 - c)
    partner = device(y, z, xh, 1 - xl, c)

    def wait(src, dst, sem):
        local(src, dst, sem).wait()

    loads = [
        local(src, dst, in_sem.at[n])
        for n, (src, dst) in enumerate(
            [
                (token_h, token), (deletion_h, deletion), (mask_h, mask), (stack_h, stack_raw),
                (letters_h, letters), (gaps_h, gaps), (steps_h, steps), (gain_h, gain), (offset_h, offset),
                (left_map_h, left_map), (left_bias_h, left_bias), (right_map_h, right_map),
                (right_bias_h, right_bias), (weight_h, weight_raw), (cotangent.at[:, :, xl], cot_raw),
            ]
        )
    ]
    for load in loads:
        load.start()

    barrier = pltpu.get_barrier_semaphore()

    def signal(target):
        pl.semaphore_signal(barrier, inc=1, device_id=target, device_id_type=MESH)

    def greet(n):
        @pl.when(n != z * 4 + q)
        def _():
            signal((y * 16 + lax.div(n, 4) * 2 + xh, lax.rem(n, 4)))

        @pl.when(n != (y * 2 + xh) * 4 + q)
        def _():
            signal((lax.div(n, 8) * 16 + z * 2 + lax.rem(lax.div(n, 4), 2), lax.rem(n, 4)))

    for n in range(32):
        greet(n)

    def line_user(n):
        return device(y, lax.div(n, 2), xh, parity, lax.rem(n, 2))

    def plane_user(n):
        return device(lax.div(n, 4), z, lax.div(lax.rem(n, 4), 2), lax.rem(n, 2), lax.div(y, 2))

    def rm_copy(n):
        return remote(mask_rows, row_masks.at[band, q], rm_send, rm_recv, plane_user(n))

    def cm_copy(n):
        return remote(mask_rows, column_masks.at[zi, q], cm_send, cm_recv, line_user(n))

    def cot_copy(n):
        return remote(cot_stage.at[n], cot_all.at[band], cot_send, cot_recv, device(n, z, c, xl, lax.div(y, 2)))

    own_cot = jnp.where(jnp.logical_and(inside, xh == c), y, -1)

    def left_slot(at_band, at_q):
        return left_all.at[at_q, :, block(at_band, WIDE)]

    def l_copy(n):
        return remote(left_own, left_slot(band, q), l_send, l_recv, plane_user(n))

    def r1_copy():
        return remote(right_own, right_all.at[zi, q], r1_send, r1_recv, partner)

    def r2_copy(n):
        return remote(
            right_own, right_all.at[zi, q], r2_send, r2_recv, device(y, n, xh, xl, c)
        )

    def r2_forward(n):
        return remote(
            right_all.at[zi, other_q], right_all.at[zi, other_q], r2_send, r2_recv,
            device(y, n, xh, xl, c),
        )

    def r3_copy(n):
        at_q = n * 2 + c
        return remote(right_all.at[:, at_q], right_all.at[:, at_q], r3_send, r3_recv, other_core)

    for load in loads[:13]:
        load.wait()
    mask_value = mask[...].astype(F32)
    empty = jnp.zeros((8, ROWS), F32)
    mask_rows[...] = jnp.where(
        c == 0, jnp.concatenate([mask_value, empty], axis=1), jnp.concatenate([empty, mask_value], axis=1)
    )
    square[...] = jnp.zeros((128, 128), F32)
    square[0:8, 0:ROWS] = token[...].astype(F32)
    square[8:16, 0:ROWS] = deletion[...].astype(F32)
    square[16:24, 0:ROWS] = mask_value
    turned[...] = square[...].T[:ROWS]
    for n in range(2):
        stack[n] = stack_raw[:, :, n * 128 : (n + 1) * 128].astype(F32).reshape(512, 128)
    table[...] = jnp.zeros((128, WIDE), F32)
    table[: letters.shape[0], :] = letters[...]
    table[32:64, :] = steps[:, 0:1] * gaps[0:1, :] + steps[:, 1:2] * gaps[1:2, :]
    spread_left = (
        lax.rem(lax.broadcasted_iota(jnp.int32, (128, 32), 0), 32) == lanes((128, 32))
    ).astype(F32).astype(BF16)
    spread_right = (
        lax.div(lax.broadcasted_iota(jnp.int32, (WIDE, 32), 0), 8) == lanes((WIDE, 32))
    ).astype(F32).astype(BF16)
    maps[:128, :] = dot(spread_left, left_map[...]).astype(BF16)
    maps[128:, :] = dot(spread_right, right_map[...]).astype(BF16)
    bias[...] = jnp.concatenate(
        [
            sum(dot_nt(piece, spread_left) for piece in split(jnp.broadcast_to(left_bias[...], (8, 32)), 3)),
            sum(dot_nt(piece, spread_right) for piece in split(jnp.broadcast_to(right_bias[...], (8, 32)), 3)),
        ],
        axis=1,
    )
    loads[14].wait()
    for n in range(4):
        strip = cot_raw[:, n * 4 : n * 4 + 4].astype(F32)
        strip = jnp.where(c == 0, strip[:, :, :8, :], strip[:, :, 8:, :])
        cot_stage[n] = strip.reshape(8, 32, 128).astype(BF16)
    lane = lanes((ROWS, 128))
    fine = lane.astype(F32)
    wide_lane = lanes((ROWS, WIDE))
    pieces = split(table[...], 3)
    right_value = jnp.zeros((ROWS, WIDE), F32)
    for h in range(2):
        hot = jnp.concatenate(
            [
                jnp.logical_or(fine == turned[:, i : i + 1], fine == turned[:, 8 + i : 9 + i] + 32.0).astype(F32)
                for i in range(h * 4, h * 4 + 4)
            ],
            axis=0,
        )
        hot_turned[h] = hot.T[:32].astype(BF16)
        hot = hot.astype(BF16)
        hidden = jnp.concatenate(
            [
                jnp.concatenate([stack[n, pl.ds(i, ROWS, stride=8), :] for i in range(h * 4, h * 4 + 4)], axis=0)
                for n in range(2)
            ],
            axis=1,
        ) + (dot(hot, pieces[0]) + dot(hot, pieces[1]) + dot(hot, pieces[2]))
        centered = hidden - jnp.mean(hidden, axis=-1, keepdims=True)
        variance = jnp.mean(centered * centered, axis=-1, keepdims=True)
        scale = lax.rsqrt(variance + EPSILON)
        whitened = centered * scale
        white[h * 256 : (h + 1) * 256, :] = whitened
        spread[h * 256 : (h + 1) * 256, :] = jnp.broadcast_to(scale, (256, 128))
        normed = (whitened * gain[...] + offset[...]).astype(BF16)
        rows = dot_nt(normed, maps[...]) + bias[:1, :]
        left_value = jnp.zeros((ROWS, 128), F32)
        for i in range(4):
            part = turned[:, 16 + h * 4 + i : 17 + h * 4 + i] * rows[i * ROWS : (i + 1) * ROWS, :]
            left_value = jnp.where(lax.div(lane, 32) == i, part[:, :128], left_value)
            right_value = jnp.where(lax.rem(wide_lane, 8) == h * 4 + i, part[:, 128:], right_value)
        left_own[:, h * 128 : (h + 1) * 128] = left_value.astype(BF16)
    right_own[...] = right_value.astype(BF16)
    pl.semaphore_wait(barrier, 62)
    @pl.when(jnp.logical_not(active))
    def _():
        r1_copy().start()

    start_all(16, rm_copy, own_row)
    start_all(16, cm_copy, own_column)

    @pl.when(inside)
    def _():
        local(mask_rows, row_masks.at[band, q], rm_recv).start()

    @pl.when(active)
    def _():
        local(mask_rows, column_masks.at[zi, q], cm_recv).start()

    start_all(4, cot_copy, own_cot)

    @pl.when(jnp.logical_and(inside, xh == c))
    def _():
        local(cot_stage.at[y], cot_all.at[band], cot_recv).start()

    start_all(16, l_copy, own_row)

    @pl.when(inside)
    def _():
        local(left_own, left_slot(band, q), l_recv).start()

    @pl.when(active)
    def _():
        start_all(8, r2_copy, z)
        local(right_own, right_all.at[zi, q], r2_recv).start()

    @pl.when(active)
    def _():
        wait(right_own, right_all.at[zi, other_q], r1_recv)
        start_all(8, r2_forward, z)

    loads[13].wait()
    weight_wide[...] = weight_raw[...].astype(F32)
    for t in range(2):
        for b in range(4):
            for a in range(4):
                at = ((t * 4 + b) * 4 + a) * 32
                weight[at : at + 32, :] = weight_wide[pl.ds(t * 16 + a * 4 + b, 32, stride=32), :].astype(BF16)
    for t in range(8):
        weight_turned[:, t * 128 : (t + 1) * 128] = weight[t * 128 : (t + 1) * 128, :].astype(F32).T.astype(BF16)

    wait(row_masks, row_masks, rm_recv)
    wait(column_masks, column_masks, cm_recv)
    column_mask = jnp.concatenate(
        [
            jnp.concatenate([column_masks[b, 2 * h] + column_masks[b, 2 * h + 1] for h in range(2)], axis=1)
            for b in range(4)
        ],
        axis=0,
    )
    for i in range(32):
        row = jnp.concatenate(
            [
                row_masks[i // 8, 2 * h, i % 8 : i % 8 + 1, :] + row_masks[i // 8, 2 * h + 1, i % 8 : i % 8 + 1, :]
                for h in range(2)
            ],
            axis=1,
        )
        product[i * 32 : (i + 1) * 32, :] = (row * column_mask).astype(BF16)
    counts[...] = dot(product[...], jnp.ones((256, 128), BF16))
    wait(cot_all, cot_all, cot_recv)
    for n in range(4):
        cot = cot_all[n].astype(F32).reshape(256, 128)
        scaled[n * 256 : (n + 1) * 256, :] = (cot / counts[n * 256 : (n + 1) * 256, :]).astype(BF16)

    def backward(g):
        span = block(g, 256)
        wide_grad[...] = dot_nt(weight[...], scaled[span, :])
        for t in range(8):
            for half in range(2):
                lane_part = wide_grad[t * 128 : (t + 1) * 128, half * 128 : (half + 1) * 128]
                parts = swap([lane_part[a * 32 : (a + 1) * 32, :] for a in range(4)], 32)
                for i, part in enumerate(parts):
                    at = pl.ds(pl.multiple_of(g * 256 + half * 128 + i * 32, 32), 32)
                    grad_outer[at, t * 128 : (t + 1) * 128] = part.astype(BF16)

    repeat(4, backward)

    def right_step(t):
        for b in range(2):
            right_part[:, b * 256 : (b + 1) * 256] = dot(
                left_all[...].reshape(256, 1024), grad_outer[:, t * 512 + b * 256 : t * 512 + (b + 1) * 256]
            )
        for at_q in range(4):
            rows = slice(at_q * ROWS, (at_q + 1) * ROWS)
            parts = swap([right_part[rows, b * 128 : (b + 1) * 128] for b in range(4)], 8)
            for b, part in enumerate(parts):
                right_grad[b, at_q, :, t * 128 : (t + 1) * 128] = part.astype(BF16)

    def gx_copy(n):
        return remote(right_grad.at[:, n * 2 + 1 - c], right_core.at[n], gx_send, gx_recv, other_core)

    wait(left_all, left_all, l_recv)
    right_step(0)
    right_step(1)
    start_all(2, gx_copy, -1)

    @pl.when(active)
    def _():
        drain(r2_recv, gauge, 7)

    @pl.when(jnp.logical_not(active))
    def _():
        drain(r2_recv, gauge, 8)

    start_all(2, r3_copy, -1)
    def gz_copy(n):
        return remote(
            right_sum.at[n], right_in.at[z], gz_send, gz_recv, device(y, n * 2 + xl, xh, xl, c)
        )

    own_gz = jnp.where(active, zi, -1)
    wait(right_core, right_core, gx_recv)
    for n in range(2):
        for b in range(4):
            right_sum[b, n] = (right_grad[b, n * 2 + c].astype(F32) + right_core[n, b].astype(F32)).astype(BF16)
    start_all(4, gz_copy, own_gz)

    @pl.when(active)
    def _():
        local(right_sum.at[zi], right_in.at[z], gz_recv).start()

    drain(r3_recv, gauge, 8)
    for at_q in range(4):
        rows = slice(at_q * ROWS, (at_q + 1) * ROWS)
        for t in range(2):
            parts = [right_all[b, at_q, :, t * 128 : (t + 1) * 128].astype(F32) for b in range(4)]
            for b, part in enumerate(swap(parts, 8)):
                right_mat[rows, (t * 4 + b) * 128 : (t * 4 + b + 1) * 128] = part.astype(BF16)


    def gl_part(n):
        return left_grad.at[lax.rem(n, 4), :, block(lax.div(n, 4), WIDE)]

    def gl_copy(n):
        target = device(c * 2 + lax.div(n, 8), z, lax.rem(lax.div(n, 4), 2), lax.div(lax.rem(n, 4), 2), lax.rem(n, 2))
        return remote(gl_part(n), left_in.at[plane], gl_send, gl_recv, target)

    own_gl = jnp.where(inside, band * 4 + q, -1)

    def left_step(g):
        span = block(g, 256)
        part = dot_nt(right_mat[...], grad_outer[span, :]).astype(BF16)
        for at_q in range(4):
            left_grad[at_q, :, span] = part[at_q * ROWS : (at_q + 1) * ROWS, :]

    for g in range(4):
        left_step(g)

        def start_left(n):
            @pl.when(n + g * 4 != own_gl)
            def _():
                gl_copy(n + g * 4).start()

        repeat(4, start_left)

    @pl.when(inside)
    def _():
        local(gl_part(band * 4 + q), left_in.at[plane], gl_recv).start()

    def forward(g):
        lead = left_all[:, :, block(g, 256)].reshape(256, 256).astype(F32).T.astype(BF16)
        wide_outer[...] = dot(lead, right_mat[...])
        for half in range(2):
            span = pl.ds(pl.multiple_of(g * 256 + half * 128, 128), 128)
            for t in range(8):
                tile = wide_outer[half * 128 : (half + 1) * 128, t * 128 : (t + 1) * 128]
                parts = swap([tile[i * 32 : (i + 1) * 32, :] for i in range(4)], 32)
                for a, part in enumerate(parts):
                    folded[(t * 4 + a) * 32 : (t * 4 + a + 1) * 32, span] = part.astype(BF16)

    def project(g):
        span = block(g, 256)
        value = dot(weight_turned[...], folded[:, span])
        update = (value.T / counts[span, :]).astype(BF16)
        pair[block(g, 8)] = update.reshape(8, 32, 128)

    repeat(4, forward)
    weight_grad[...] = dot(folded[...], scaled[...])

    def plane_peer(n):
        return device(lax.div(n, 4), z, lax.div(lax.rem(n, 4), 2), lax.rem(n, 2), c)

    def line_peer(n):
        return device(y, n, xh, xl, c)

    def wh_copy():
        return remote(weight_grad.at[block(1 - c, 512), :], weight_core, wh_send.at[0], wh_recv.at[0], other_core)

    def wa_part(n):
        return weight_half.at[block(n, 32), :]

    def wa_copy(n):
        return remote(wa_part(n), weight_in.at[plane], wa_send, wa_recv, plane_peer(n))

    def wb_copy(n):
        return remote(weight_sum, weight_far.at[z], wb_send, wb_recv, line_peer(n))

    def wc_slot(n):
        return weight_all.at[c, block(n, 32), :]

    def wc_copy(n):
        return remote(weight_total, wc_slot(plane), wc_send, wc_recv, plane_peer(n))

    def wd_copy():
        return remote(weight_all.at[c], weight_all.at[c], wh_send.at[1], wh_recv.at[1], other_core)

    wh_copy().start()
    repeat(4, project)
    wait(weight_core, weight_core, wh_recv.at[0])
    weight_half[...] = (weight_grad[block(c, 512), :] + weight_core[...]).astype(BF16)
    start_all(16, wa_copy, plane)
    local(wa_part(plane), weight_in.at[plane], wa_recv).start()

    def pair_part(n):
        return pair.at[block(n, 8)]

    def pair_copy(n):
        target = device(c * 2 + lax.div(n, 2), z, lax.rem(n, 2), lax.div(y, 2), lax.rem(y, 2))
        return remote(pair_part(n), pair_in.at[xh * 2 + xl], pair_send, pair_recv, target)

    keeps_pair = jnp.logical_and(inside, q == y)
    own_pair = jnp.where(keeps_pair, band, -1)
    start_all(4, pair_copy, own_pair)

    @pl.when(keeps_pair)
    def _():
        local(pair_part(band), pair_in.at[xh * 2 + xl], pair_recv).start()

    def gf_copy():
        return remote(right_send, right_last, gf_send, gf_recv, partner)

    @pl.when(active)
    def _():
        wait(right_in, right_in, gz_recv)
        away = right_in[0, 1 - xl].astype(F32)
        for n in range(1, 8):
            away = away + right_in[n, 1 - xl].astype(F32)
        right_send[...] = away.astype(BF16)
        gf_copy().start()
        here = right_in[0, xl].astype(F32)
        for n in range(1, 8):
            here = here + right_in[n, xl].astype(F32)
        right_last[...] = here.astype(BF16)

    wait(left_in, left_in, gl_recv)
    left_total = total(left_in, 16).astype(BF16).astype(F32)

    @pl.when(jnp.logical_not(active))
    def _():
        wait(right_last, right_last, gf_recv)

    right_total = right_last[...].astype(F32)

    wait(weight_in, weight_in, wa_recv)
    weight_sum[...] = total(weight_in, 16).astype(BF16)
    start_all(8, wb_copy, z)
    local(weight_sum, weight_far.at[z], wb_recv).start()

    sums = jnp.zeros((32, WIDE), F32)
    for h in range(2):
        picked = []
        for i in range(4):
            keep = turned[:, 16 + h * 4 + i : 17 + h * 4 + i]
            tile = left_total[:, h * 128 : (h + 1) * 128]
            picked.append(
                jnp.concatenate(
                    [
                        jnp.where(lax.div(lane, 32) == i, tile, 0.0) * keep,
                        jnp.where(lax.rem(wide_lane, 8) == h * 4 + i, right_total, 0.0) * keep,
                    ],
                    axis=1,
                )
            )
        picked = jnp.concatenate(picked, axis=0).astype(BF16)
        gained = dot(picked, maps[...]) * gain[...]
        whitened = white[h * 256 : (h + 1) * 256, :]
        stream_grad = spread[h * 256 : (h + 1) * 256, :1] * (
            gained
            - jnp.mean(gained, axis=-1, keepdims=True)
            - whitened * jnp.mean(gained * whitened, axis=-1, keepdims=True)
        )
        for piece in split(stream_grad, 2):
            sums = sums + dot(hot_turned[h], piece)
    for n in range(TILES):
        table_part[n] = sums[(n // 2) * 8 : (n // 2 + 1) * 8, (n % 2) * 128 : (n % 2 + 1) * 128]

    def t_copy():
        return remote(table_part.at[pl.ds((1 - c) * 3, 3)], table_core, t_send.at[0], t_recv.at[0], other_core)

    def tp_copy(n):
        return remote(table_p.at[plane], table_p.at[plane], tp_send, tp_recv, plane_peer(n))

    def tz_copy(n):
        return remote(table_z.at[z], table_z.at[z], tz_send, tz_recv, device(y, n, xh, xl, c))

    def half(at_c):
        return table_all.at[pl.ds(at_c * 3, 3)]

    def t_last():
        return remote(table_half, half(c), t_send.at[1], t_recv.at[1], other_core)

    t_copy().start()
    wait(table_core, table_core, t_recv.at[0])
    table_p[plane] = table_part[pl.ds(c * 3, 3)] + table_core[...]
    start_all(16, tp_copy, plane)

    wait(weight_far, weight_far, wb_recv)
    weight_total[...] = total(weight_far, 8).astype(BF16)
    start_all(16, wc_copy, plane)
    local(weight_total, wc_slot(plane), wc_recv).start()

    wait(pair_in, pair_in, pair_recv)
    for at_z in range(8):
        run = [
            pair_in[at_x * 2 + at_z % 2, :, (at_z // 2) * 8 : (at_z // 2 + 1) * 8, :].astype(F32) for at_x in range(2)
        ]
        pair_out[:, at_z * 16 : (at_z + 1) * 16, :] = jnp.concatenate(run, axis=1).astype(BF16)
    local(pair_out, pair_h, out_sem.at[0]).start()

    drain(tp_recv, gauge_t, 15)
    table_z[z] = total(table_p, 16)
    start_all(8, tz_copy, z)

    def lay_out(at_c):
        for n in range(16):
            first = at_c * 16 + n % 4 * 4 + n // 4
            weight_out[pl.ds(first, 32, stride=32), :] = weight_all[at_c, n * 32 : (n + 1) * 32, :].astype(F32)

    wait(weight_all.at[c], weight_all.at[c], wc_recv)
    wd_copy().start()

    sent(rm_send, gauge_m, 16, own_row)
    sent(cm_send, gauge_m, 16, own_column)
    sent(cot_send, gauge, 8, own_cot, 2)
    sent(l_send, gauge, 16, own_row)
    drain(r3_send, gauge, 8)
    drain(gx_send, gauge, 8)
    sent(gz_send, gauge, 8, own_gz, 2)
    sent(gl_send, gauge, 16, own_gl)
    drain(wa_send, gauge_w, 15)
    drain(wb_send, gauge_w, 7)
    sent(pair_send, gauge, 8, own_pair, 2)
    wh_copy().wait_send()
    t_copy().wait_send()

    @pl.when(active)
    def _():
        drain(r2_send, gauge, 14)
        gf_copy().wait_send()

    @pl.when(jnp.logical_not(active))
    def _():
        r1_copy().wait_send()

    wait(weight_all.at[1 - c], weight_all.at[1 - c], wh_recv.at[1])
    for at_c in range(2):
        lay_out(at_c)
    local(weight_out, weight_grad_h, out_sem.at[1]).start()
    drain(wc_send, gauge_w, 15)
    drain(tp_send, gauge_t, 15)
    wd_copy().wait_send()

    drain(tz_recv, gauge_t, 7)
    summed = total(table_z, 8)
    table_half[...] = summed
    t_last().start()
    table_all[pl.ds(c * 3, 3)] = summed
    drain(tz_send, gauge_t, 7)
    wait(table_half, half(1 - c), t_recv.at[1])
    for n in range(TILES):
        high = min(8, table_out.shape[0] - (n // 2) * 8)
        table_out[(n // 2) * 8 : (n // 2) * 8 + high, (n % 2) * 128 : (n % 2 + 1) * 128] = table_all[n][:high]
    t_last().wait_send()
    wait(pair_out, pair_h, out_sem.at[0])
    wait(weight_out, weight_grad_h, out_sem.at[1])


def shape(dims, dtype=BF16):
    return jax.ShapeDtypeStruct(dims, dtype)


def body(
    alignment_token_classes, deletions, alignment_mask, homolog_stack_values,
    letter_lookup_coefficients, gap_lookup_coefficients, standardize_gain, standardize_offset,
    first_factor_map, left_bias_vector, second_factor_map, right_bias_vector,
    output_weight_matrix, cotangent,
):
    kinds = letter_lookup_coefficients.shape[0]
    grades = np.arange(32, dtype=np.float32)
    steps = jnp.asarray(
        np.stack([(grades > 0).astype(np.float32), (2.0 / math.pi * np.arctan(grades / 3.0)).astype(np.float32)], 1)
    )
    inputs = [
        alignment_token_classes.T, deletions.T, alignment_mask.T, homolog_stack_values,
        letter_lookup_coefficients, gap_lookup_coefficients, steps,
        standardize_gain.reshape(1, 256), standardize_offset.reshape(1, 256),
        first_factor_map.T, left_bias_vector.reshape(1, 32), second_factor_map.T, right_bias_vector.reshape(1, 32),
        output_weight_matrix,
    ]
    vmem = pltpu.VMEM
    scratch = [vmem(value.shape, value.dtype) for value in inputs] + [
        vmem((8, 16, 16, 128), BF16), vmem((4, 8, 32, 128), BF16),
        vmem((128, 128), F32), vmem((ROWS, 128), F32), vmem((8, 128), F32),
        vmem((2, 512, 128), F32),
        vmem((128, WIDE), F32), vmem((384, 256), BF16), vmem((8, 384), F32),
        vmem((1024, 128), F32), vmem((1024, 128), BF16), vmem((128, 1024), BF16),
        vmem((2, 32, 256), BF16),
        vmem((512, 256), F32), vmem((512, 128), F32),
        vmem((ROWS, WIDE), BF16), vmem((ROWS, WIDE), BF16),
        vmem((4, 4, 8, 128), F32), vmem((4, 4, 8, 128), F32),
        vmem((4, 8, 32, 128), BF16),
        vmem((4, ROWS, 1024), BF16), vmem((4, 4, ROWS, WIDE), BF16),
        vmem((256, 1024), BF16), vmem((1024, 256), F32), vmem((256, 1024), F32),
        vmem((1024, 256), BF16),
        vmem((1024, 128), F32), vmem((1024, 128), BF16),
        vmem((1024, 1024), BF16), vmem((1024, 1024), BF16),
        vmem((32, 32, 128), BF16), vmem((4, 8, 32, 128), BF16),
        vmem((4, 4, ROWS, WIDE), BF16), vmem((256, 512), F32), vmem((2, 4, ROWS, WIDE), BF16),
        vmem((4, 2, ROWS, WIDE), BF16), vmem((8, 2, ROWS, WIDE), BF16),
        vmem((ROWS, WIDE), BF16), vmem((ROWS, WIDE), BF16),
        vmem((4, ROWS, 1024), BF16), vmem((16, ROWS, WIDE), BF16),
        vmem((1024, 128), F32), vmem((512, 128), F32), vmem((512, 128), BF16),
        vmem((16, 32, 128), BF16), vmem((32, 128), BF16),
        vmem((8, 32, 128), BF16), vmem((32, 128), BF16), vmem((2, 512, 128), BF16),
        vmem((TILES, 8, 128), F32), vmem((3, 8, 128), F32),
        vmem((16, 3, 8, 128), F32), vmem((8, 3, 8, 128), F32),
        vmem((3, 8, 128), F32), vmem((TILES, 8, 128), F32),
        vmem((8, 128, 128), BF16), vmem((1024, 128), F32),
        vmem((16, ROWS, WIDE), BF16), vmem((16, 8, 128), F32),
        vmem((16, 32, 128), BF16), vmem((16, 3, 8, 128), F32),
    ]
    sizes = [
        len(inputs) + 1, 2, 0, 0, 0, 0, 0, 0, 0, 0, 0, 0, 0, 0, 0, 0, 0, 0, 0, 0, 0, 0, 0, 0, 0, 0, 2, 2, 0,
        0, 0, 0, 0, 0, 2, 2, 0, 0, 0, 0,
    ]
    results = pl.pallas_call(
        kernel,
        out_shape=[shape((8, 128, 128)), shape((1024, 128), F32), shape((kinds, 256), F32)],
        in_specs=[pl.BlockSpec(memory_space=pl.ANY)] * (len(inputs) + 1),
        out_specs=[pl.BlockSpec(memory_space=pl.ANY)] * 2 + [pl.BlockSpec(memory_space=pltpu.VMEM)],
        scratch_shapes=scratch + [pltpu.SemaphoreType.DMA((size,)) if size else pltpu.SemaphoreType.DMA for size in sizes],
        compiler_params=pltpu.CompilerParams(
            collective_id=0, has_side_effects=True, vmem_limit_bytes=60 * 1024 * 1024
        ),
        name="outer_product_mean",
    )(*inputs, cotangent.reshape(8, 16, 2, 16, 128))
    return pl.pallas_call(
        hand_over,
        out_shape=[shape(value.shape, value.dtype) for value in results],
        in_specs=[pl.BlockSpec(memory_space=pl.ANY)] * 3,
        out_specs=[pl.BlockSpec(memory_space=pl.ANY)] * 3,
        scratch_shapes=[vmem(value.shape, value.dtype) for value in results] + [pltpu.SemaphoreType.DMA((3,))],
        name="hand_over",
    )(*results)


def hand_over(pair, weight, table, pair_out, weight_out, table_out, pair_here, weight_here, table_here, sem):
    here = [pair_here, weight_here, table_here]
    arrive = [local(src, dst, sem.at[n]) for n, (src, dst) in enumerate(zip([pair, weight, table], here))]
    leave = [local(src, dst, sem.at[n]) for n, (src, dst) in enumerate(zip(here, [pair_out, weight_out, table_out]))]
    for copy in arrive:
        copy.start()
    for first, second in zip(arrive, leave):
        first.wait()
        second.start()
    for copy in leave:
        copy.wait()


def solution(mesh):
    in_specs = (
        P("seq", "res"), P("seq", "res"), P("seq", "res"), P("seq", "res", None),
        P(), P(), P(), P(), P(), P(), P(), P(), P(),
        P("res", None, None),
    )
    out_specs = (P("res", "seq", None), P(), P())
    return jax.shard_map(body, mesh=mesh, in_specs=in_specs, out_specs=out_specs, check_vma=False)
```

```python
import math

import jax
import jax.numpy as jnp
import numpy as np
from jax import lax
from jax.experimental import pallas as pl
from jax.experimental.pallas import tpu as pltpu
from jax.sharding import PartitionSpec as P

EPSILON = 1e-05
MESH = pl.DeviceIdType.MESH
F32 = jnp.float32
BF16 = jnp.bfloat16

ROWS = 64
WIDE = 256
TILES = 6


def device(y, z, xh, xl, c):
    return (y * 16 + z * 2 + xh, xl * 2 + c)


def repeat(count, step):
    lax.fori_loop(0, count, lambda n, carried: (step(n), carried)[1], 0)


def remote(src, dst, send, recv, target):
    return pltpu.make_async_remote_copy(
        src_ref=src, dst_ref=dst, send_sem=send, recv_sem=recv, device_id=target, device_id_type=MESH
    )


def start_all(count, copy, own):
    for n in range(count):

        @pl.when(own != n)
        def _(n=n):
            copy(n).start()


def local(src, dst, sem):
    return pltpu.make_async_copy(src, dst, sem)


def drain(sem, gauge, count):
    part = gauge.at[pl.ds(0, count)]
    local(part, part, sem).wait()


def sent(sem, gauge, count, own, unit=1):
    @pl.when(own >= 0)
    def _():
        drain(sem, gauge, count - unit)

    @pl.when(own < 0)
    def _():
        drain(sem, gauge, count)


def lanes(dims):
    return lax.broadcasted_iota(jnp.int32, dims, len(dims) - 1)


def block(n, size):
    return pl.ds(pl.multiple_of(n * size, size), size)


def swap(parts, stride):
    lane = lanes(parts[0].shape)
    low = lax.rem(lax.div(lane, stride), 2) == 0
    high = lax.rem(lax.div(lane, 2 * stride), 2) == 0

    def pair(first, second, step, keep):
        return (
            jnp.where(keep, first, pltpu.roll(second, step, 1)),
            jnp.where(keep, pltpu.roll(first, 128 - step, 1), second),
        )

    a, b = pair(parts[0], parts[1], stride, low)
    c, d = pair(parts[2], parts[3], stride, low)
    a, c = pair(a, c, 2 * stride, high)
    b, d = pair(b, d, 2 * stride, high)
    return [a, b, c, d]


def dot(first, second):
    return jnp.dot(first, second, preferred_element_type=F32)


def dot_nt(first, second):
    return lax.dot_general(first, second, (((1,), (1,)), ((), ())), preferred_element_type=F32)


def split(value, count):
    pieces = []
    for _ in range(count):
        piece = value.astype(BF16)
        pieces.append(piece)
        value = value - piece.astype(F32)
    return pieces


def total(ref, count):
    value = ref[0].astype(F32)
    for n in range(1, count):
        value = value + ref[n].astype(F32)
    return value


def kernel(
    token_h, deletion_h, mask_h, stack_h, letters_h, gaps_h, steps_h, gain_h, offset_h,
    left_map_h, left_bias_h, right_map_h, right_bias_h, weight_h, cotangent,
    pair_h, weight_grad_h, table_out,
    token, deletion, mask, stack_raw, letters, gaps, steps, gain, offset,
    left_map, left_bias, right_map, right_bias, weight_raw, cot_raw, cot_stage,
    square, turned, mask_rows, stack, table, maps, bias, weight_wide, weight, weight_turned, hot_turned,
    white, spread, left_own, right_own, row_masks, column_masks, cot_all, left_all, right_all,
    right_mat, wide_grad, wide_outer, product, counts, scaled, folded, grad_outer, pair, pair_in,
    right_grad, right_part, right_core, right_sum, right_in, right_last, right_send, left_grad, left_in,
    weight_grad, weight_core, weight_half, weight_in, weight_sum, weight_far, weight_total, weight_all,
    table_part, table_core, table_p, table_z, table_half, table_all, pair_out, weight_out,
    gauge, gauge_m, gauge_w, gauge_t,
    in_sem, out_sem, rm_send, rm_recv, cm_send, cm_recv, cot_send, cot_recv,
    r1_send, r1_recv, r2_send, r2_recv, r3_send, r3_recv, l_send, l_recv,
    gx_send, gx_recv, gz_send, gz_recv, gf_send, gf_recv, gl_send, gl_recv, pair_send, pair_recv,
    wh_send, wh_recv, wa_send, wa_recv, wb_send, wb_recv, wc_send, wc_recv,
    t_send, t_recv, tp_send, tp_recv, tz_send, tz_recv,
):
    res = lax.axis_index("res")
    q = lax.axis_index("seq")
    y, z, xh = lax.div(res, 16), lax.rem(lax.div(res, 2), 8), lax.rem(res, 2)
    xl, c = lax.div(q, 2), lax.rem(q, 2)
    zi, parity = lax.div(z, 2), lax.rem(z, 2)
    active = parity == xl
    inside = lax.div(y, 2) == c
    other_q = (1 - xl) * 2 + c
    plane = y * 4 + xh * 2 + xl
    band = lax.rem(y, 2) * 2 + xh
    own_column = jnp.where(active, z * 2 + c, -1)
    own_row = jnp.where(inside, plane, -1)
    other_core = device(y, z, xh, xl, 1 - c)
    partner = device(y, z, xh, 1 - xl, c)

    def wait(src, dst, sem):
        local(src, dst, sem).wait()

    loads = [
        local(src, dst, in_sem.at[n])
        for n, (src, dst) in enumerate(
            [
                (token_h, token), (deletion_h, deletion), (mask_h, mask), (stack_h, stack_raw),
                (letters_h, letters), (gaps_h, gaps), (steps_h, steps), (gain_h, gain), (offset_h, offset),
                (left_map_h, left_map), (left_bias_h, left_bias), (right_map_h, right_map),
                (right_bias_h, right_bias), (weight_h, weight_raw), (cotangent.at[:, :, xl], cot_raw),
            ]
        )
    ]
    for load in loads:
        load.start()

    barrier = pltpu.get_barrier_semaphore()

    def signal(target):
        pl.semaphore_signal(barrier, inc=1, device_id=target, device_id_type=MESH)

    def greet(n):
        @pl.when(n != z * 4 + q)
        def _():
            signal((y * 16 + lax.div(n, 4) * 2 + xh, lax.rem(n, 4)))

        @pl.when(n != (y * 2 + xh) * 4 + q)
        def _():
            signal((lax.div(n, 8) * 16 + z * 2 + lax.rem(lax.div(n, 4), 2), lax.rem(n, 4)))

    for n in range(32):
        greet(n)

    def line_user(n):
        return device(y, lax.div(n, 2), xh, parity, lax.rem(n, 2))

    def plane_user(n):
        return device(lax.div(n, 4), z, lax.div(lax.rem(n, 4), 2), lax.rem(n, 2), lax.div(y, 2))

    def rm_copy(n):
        return remote(mask_rows, row_masks.at[band, q], rm_send, rm_recv, plane_user(n))

    def cm_copy(n):
        return remote(mask_rows, column_masks.at[zi, q], cm_send, cm_recv, line_user(n))

    def cot_copy(n):
        return remote(cot_stage.at[n], cot_all.at[band], cot_send, cot_recv, device(n, z, c, xl, lax.div(y, 2)))

    own_cot = jnp.where(jnp.logical_and(inside, xh == c), y, -1)

    def left_slot(at_band, at_q):
        return left_all.at[at_q, :, block(at_band, WIDE)]

    def l_copy(n):
        return remote(left_own, left_slot(band, q), l_send, l_recv, plane_user(n))

    def r1_copy():
        return remote(right_own, right_all.at[zi, q], r1_send, r1_recv, partner)

    def r2_copy(n):
        return remote(
            right_own, right_all.at[zi, q], r2_send, r2_recv, device(y, n, xh, xl, c)
        )

    def r2_forward(n):
        return remote(
            right_all.at[zi, other_q], right_all.at[zi, other_q], r2_send, r2_recv,
            device(y, n, xh, xl, c),
        )

    def r3_copy(n):
        at_q = n * 2 + c
        return remote(right_all.at[:, at_q], right_all.at[:, at_q], r3_send, r3_recv, other_core)

    for load in loads[:13]:
        load.wait()
    mask_value = mask[...].astype(F32)
    empty = jnp.zeros((8, ROWS), F32)
    mask_rows[...] = jnp.where(
        c == 0, jnp.concatenate([mask_value, empty], axis=1), jnp.concatenate([empty, mask_value], axis=1)
    )
    square[...] = jnp.zeros((128, 128), F32)
    square[0:8, 0:ROWS] = token[...].astype(F32)
    square[8:16, 0:ROWS] = deletion[...].astype(F32)
    square[16:24, 0:ROWS] = mask_value
    turned[...] = square[...].T[:ROWS]
    for n in range(2):
        stack[n] = stack_raw[:, n * 128 : (n + 1) * 128].astype(F32)
    table[...] = jnp.zeros((128, WIDE), F32)
    table[: letters.shape[0], :] = letters[...]
    table[32:64, :] = steps[:, 0:1] * gaps[0:1, :] + steps[:, 1:2] * gaps[1:2, :]
    spread_left = (
        lax.rem(lax.broadcasted_iota(jnp.int32, (128, 32), 0), 32) == lanes((128, 32))
    ).astype(F32).astype(BF16)
    spread_right = (
        lax.div(lax.broadcasted_iota(jnp.int32, (WIDE, 32), 0), 8) == lanes((WIDE, 32))
    ).astype(F32).astype(BF16)
    maps[:128, :] = dot(spread_left, left_map[...]).astype(BF16)
    maps[128:, :] = dot(spread_right, right_map[...]).astype(BF16)
    bias[...] = jnp.concatenate(
        [
            sum(dot_nt(piece, spread_left) for piece in split(jnp.broadcast_to(left_bias[...], (8, 32)), 3)),
            sum(dot_nt(piece, spread_right) for piece in split(jnp.broadcast_to(right_bias[...], (8, 32)), 3)),
        ],
        axis=1,
    )
    loads[14].wait()
    for n in range(4):
        strip = cot_raw[:, n * 4 : n * 4 + 4].astype(F32)
        strip = jnp.where(c == 0, strip[:, :, :8, :], strip[:, :, 8:, :])
        cot_stage[n] = strip.reshape(8, 32, 128).astype(BF16)
    lane = lanes((ROWS, 128))
    fine = lane.astype(F32)
    wide_lane = lanes((ROWS, WIDE))
    pieces = split(table[...], 3)
    right_value = jnp.zeros((ROWS, WIDE), F32)
    for h in range(2):
        hot = jnp.concatenate(
            [
                jnp.logical_or(fine == turned[:, i : i + 1], fine == turned[:, 8 + i : 9 + i] + 32.0).astype(F32)
                for i in range(h * 4, h * 4 + 4)
            ],
            axis=0,
        )
        hot_turned[h] = hot.T[:32].astype(BF16)
        hot = hot.astype(BF16)
        hidden = jnp.concatenate(
            [
                jnp.concatenate([stack[n, pl.ds(i, ROWS, stride=8), :] for i in range(h * 4, h * 4 + 4)], axis=0)
                for n in range(2)
            ],
            axis=1,
        ) + (dot(hot, pieces[0]) + dot(hot, pieces[1]) + dot(hot, pieces[2]))
        centered = hidden - jnp.mean(hidden, axis=-1, keepdims=True)
        variance = jnp.mean(centered * centered, axis=-1, keepdims=True)
        scale = lax.rsqrt(variance + EPSILON)
        whitened = centered * scale
        white[h * 256 : (h + 1) * 256, :] = whitened
        spread[h * 256 : (h + 1) * 256, :] = jnp.broadcast_to(scale, (256, 128))
        normed = (whitened * gain[...] + offset[...]).astype(BF16)
        rows = dot_nt(normed, maps[...]) + bias[:1, :]
        left_value = jnp.zeros((ROWS, 128), F32)
        for i in range(4):
            part = turned[:, 16 + h * 4 + i : 17 + h * 4 + i] * rows[i * ROWS : (i + 1) * ROWS, :]
            left_value = jnp.where(lax.div(lane, 32) == i, part[:, :128], left_value)
            right_value = jnp.where(lax.rem(wide_lane, 8) == h * 4 + i, part[:, 128:], right_value)
        left_own[:, h * 128 : (h + 1) * 128] = left_value.astype(BF16)
    right_own[...] = right_value.astype(BF16)
    pl.semaphore_wait(barrier, 62)
    @pl.when(jnp.logical_not(active))
    def _():
        r1_copy().start()

    start_all(16, rm_copy, own_row)
    start_all(16, cm_copy, own_column)

    @pl.when(inside)
    def _():
        local(mask_rows, row_masks.at[band, q], rm_recv).start()

    @pl.when(active)
    def _():
        local(mask_rows, column_masks.at[zi, q], cm_recv).start()

    start_all(4, cot_copy, own_cot)

    @pl.when(jnp.logical_and(inside, xh == c))
    def _():
        local(cot_stage.at[y], cot_all.at[band], cot_recv).start()

    start_all(16, l_copy, own_row)

    @pl.when(inside)
    def _():
        local(left_own, left_slot(band, q), l_recv).start()

    @pl.when(active)
    def _():
        start_all(8, r2_copy, z)
        local(right_own, right_all.at[zi, q], r2_recv).start()

    @pl.when(active)
    def _():
        wait(right_own, right_all.at[zi, other_q], r1_recv)
        start_all(8, r2_forward, z)

    loads[13].wait()
    weight_wide[...] = weight_raw[...].astype(F32)
    for t in range(2):
        for b in range(4):
            for a in range(4):
                at = ((t * 4 + b) * 4 + a) * 32
                weight[at : at + 32, :] = weight_wide[pl.ds(t * 16 + a * 4 + b, 32, stride=32), :].astype(BF16)
    for t in range(8):
        weight_turned[:, t * 128 : (t + 1) * 128] = weight[t * 128 : (t + 1) * 128, :].astype(F32).T.astype(BF16)

    wait(row_masks, row_masks, rm_recv)
    wait(column_masks, column_masks, cm_recv)
    column_mask = jnp.concatenate(
        [
            jnp.concatenate([column_masks[b, 2 * h] + column_masks[b, 2 * h + 1] for h in range(2)], axis=1)
            for b in range(4)
        ],
        axis=0,
    )
    for i in range(32):
        row = jnp.concatenate(
            [
                row_masks[i // 8, 2 * h, i % 8 : i % 8 + 1, :] + row_masks[i // 8, 2 * h + 1, i % 8 : i % 8 + 1, :]
                for h in range(2)
            ],
            axis=1,
        )
        product[i * 32 : (i + 1) * 32, :] = (row * column_mask).astype(BF16)
    counts[...] = dot(product[...], jnp.ones((256, 128), BF16))
    wait(cot_all, cot_all, cot_recv)
    for n in range(4):
        cot = cot_all[n].astype(F32).reshape(256, 128)
        scaled[n * 256 : (n + 1) * 256, :] = (cot / counts[n * 256 : (n + 1) * 256, :]).astype(BF16)

    def backward(g):
        span = block(g, 256)
        wide_grad[...] = dot_nt(weight[...], scaled[span, :])
        for t in range(8):
            for half in range(2):
                lane_part = wide_grad[t * 128 : (t + 1) * 128, half * 128 : (half + 1) * 128]
                parts = swap([lane_part[a * 32 : (a + 1) * 32, :] for a in range(4)], 32)
                for i, part in enumerate(parts):
                    at = pl.ds(pl.multiple_of(g * 256 + half * 128 + i * 32, 32), 32)
                    grad_outer[at, t * 128 : (t + 1) * 128] = part.astype(BF16)

    repeat(4, backward)

    def right_step(t):
        for b in range(2):
            right_part[:, b * 256 : (b + 1) * 256] = dot(
                left_all[...].reshape(256, 1024), grad_outer[:, t * 512 + b * 256 : t * 512 + (b + 1) * 256]
            )
        for at_q in range(4):
            rows = slice(at_q * ROWS, (at_q + 1) * ROWS)
            parts = swap([right_part[rows, b * 128 : (b + 1) * 128] for b in range(4)], 8)
            for b, part in enumerate(parts):
                right_grad[b, at_q, :, t * 128 : (t + 1) * 128] = part.astype(BF16)

    def gx_copy(n):
        return remote(right_grad.at[:, n * 2 + 1 - c], right_core.at[n], gx_send, gx_recv, other_core)

    wait(left_all, left_all, l_recv)
    right_step(0)
    right_step(1)
    start_all(2, gx_copy, -1)

    @pl.when(active)
    def _():
        drain(r2_recv, gauge, 7)

    @pl.when(jnp.logical_not(active))
    def _():
        drain(r2_recv, gauge, 8)

    start_all(2, r3_copy, -1)
    def gz_copy(n):
        return remote(
            right_sum.at[n], right_in.at[z], gz_send, gz_recv, device(y, n * 2 + xl, xh, xl, c)
        )

    own_gz = jnp.where(active, zi, -1)
    wait(right_core, right_core, gx_recv)
    for n in range(2):
        for b in range(4):
            right_sum[b, n] = (right_grad[b, n * 2 + c].astype(F32) + right_core[n, b].astype(F32)).astype(BF16)
    start_all(4, gz_copy, own_gz)

    @pl.when(active)
    def _():
        local(right_sum.at[zi], right_in.at[z], gz_recv).start()

    drain(r3_recv, gauge, 8)
    for at_q in range(4):
        rows = slice(at_q * ROWS, (at_q + 1) * ROWS)
        for t in range(2):
            parts = [right_all[b, at_q, :, t * 128 : (t + 1) * 128].astype(F32) for b in range(4)]
            for b, part in enumerate(swap(parts, 8)):
                right_mat[rows, (t * 4 + b) * 128 : (t * 4 + b + 1) * 128] = part.astype(BF16)


    def gl_part(n):
        return left_grad.at[lax.rem(n, 4), :, block(lax.div(n, 4), WIDE)]

    def gl_copy(n):
        target = device(c * 2 + lax.div(n, 8), z, lax.rem(lax.div(n, 4), 2), lax.div(lax.rem(n, 4), 2), lax.rem(n, 2))
        return remote(gl_part(n), left_in.at[plane], gl_send, gl_recv, target)

    own_gl = jnp.where(inside, band * 4 + q, -1)

    def left_step(g):
        span = block(g, 256)
        part = dot_nt(right_mat[...], grad_outer[span, :]).astype(BF16)
        for at_q in range(4):
            left_grad[at_q, :, span] = part[at_q * ROWS : (at_q + 1) * ROWS, :]

    for g in range(4):
        left_step(g)

        def start_left(n):
            @pl.when(n + g * 4 != own_gl)
            def _():
                gl_copy(n + g * 4).start()

        repeat(4, start_left)

    @pl.when(inside)
    def _():
        local(gl_part(band * 4 + q), left_in.at[plane], gl_recv).start()

    def forward(g):
        lead = left_all[:, :, block(g, 256)].reshape(256, 256).astype(F32).T.astype(BF16)
        wide_outer[...] = dot(lead, right_mat[...])
        for half in range(2):
            span = pl.ds(pl.multiple_of(g * 256 + half * 128, 128), 128)
            for t in range(8):
                tile = wide_outer[half * 128 : (half + 1) * 128, t * 128 : (t + 1) * 128]
                parts = swap([tile[i * 32 : (i + 1) * 32, :] for i in range(4)], 32)
                for a, part in enumerate(parts):
                    folded[(t * 4 + a) * 32 : (t * 4 + a + 1) * 32, span] = part.astype(BF16)

    def project(g):
        span = block(g, 256)
        value = dot(weight_turned[...], folded[:, span])
        update = (value.T / counts[span, :]).astype(BF16)
        pair[block(g, 8)] = update.reshape(8, 32, 128)

    repeat(4, forward)
    weight_grad[...] = dot(folded[...], scaled[...])

    def plane_peer(n):
        return device(lax.div(n, 4), z, lax.div(lax.rem(n, 4), 2), lax.rem(n, 2), c)

    def line_peer(n):
        return device(y, n, xh, xl, c)

    def wh_copy():
        return remote(weight_grad.at[block(1 - c, 512), :], weight_core, wh_send.at[0], wh_recv.at[0], other_core)

    def wa_part(n):
        return weight_half.at[block(n, 32), :]

    def wa_copy(n):
        return remote(wa_part(n), weight_in.at[plane], wa_send, wa_recv, plane_peer(n))

    def wb_copy(n):
        return remote(weight_sum, weight_far.at[z], wb_send, wb_recv, line_peer(n))

    def wc_slot(n):
        return weight_all.at[c, block(n, 32), :]

    def wc_copy(n):
        return remote(weight_total, wc_slot(plane), wc_send, wc_recv, plane_peer(n))

    def wd_copy():
        return remote(weight_all.at[c], weight_all.at[c], wh_send.at[1], wh_recv.at[1], other_core)

    wh_copy().start()
    repeat(4, project)
    wait(weight_core, weight_core, wh_recv.at[0])
    weight_half[...] = (weight_grad[block(c, 512), :] + weight_core[...]).astype(BF16)
    start_all(16, wa_copy, plane)
    local(wa_part(plane), weight_in.at[plane], wa_recv).start()

    def pair_part(n):
        return pair.at[block(n, 8)]

    def pair_copy(n):
        target = device(c * 2 + lax.div(n, 2), z, lax.rem(n, 2), lax.div(y, 2), lax.rem(y, 2))
        return remote(pair_part(n), pair_in.at[xh * 2 + xl], pair_send, pair_recv, target)

    keeps_pair = jnp.logical_and(inside, q == y)
    own_pair = jnp.where(keeps_pair, band, -1)
    start_all(4, pair_copy, own_pair)

    @pl.when(keeps_pair)
    def _():
        local(pair_part(band), pair_in.at[xh * 2 + xl], pair_recv).start()

    def gf_copy():
        return remote(right_send, right_last, gf_send, gf_recv, partner)

    @pl.when(active)
    def _():
        wait(right_in, right_in, gz_recv)
        away = right_in[0, 1 - xl].astype(F32)
        for n in range(1, 8):
            away = away + right_in[n, 1 - xl].astype(F32)
        right_send[...] = away.astype(BF16)
        gf_copy().start()
        here = right_in[0, xl].astype(F32)
        for n in range(1, 8):
            here = here + right_in[n, xl].astype(F32)
        right_last[...] = here.astype(BF16)

    wait(left_in, left_in, gl_recv)
    left_total = total(left_in, 16).astype(BF16).astype(F32)

    @pl.when(jnp.logical_not(active))
    def _():
        wait(right_last, right_last, gf_recv)

    right_total = right_last[...].astype(F32)

    wait(weight_in, weight_in, wa_recv)
    weight_sum[...] = total(weight_in, 16).astype(BF16)
    start_all(8, wb_copy, z)
    local(weight_sum, weight_far.at[z], wb_recv).start()

    sums = jnp.zeros((32, WIDE), F32)
    for h in range(2):
        picked = []
        for i in range(4):
            keep = turned[:, 16 + h * 4 + i : 17 + h * 4 + i]
            tile = left_total[:, h * 128 : (h + 1) * 128]
            picked.append(
                jnp.concatenate(
                    [
                        jnp.where(lax.div(lane, 32) == i, tile, 0.0) * keep,
                        jnp.where(lax.rem(wide_lane, 8) == h * 4 + i, right_total, 0.0) * keep,
                    ],
                    axis=1,
                )
            )
        picked = jnp.concatenate(picked, axis=0).astype(BF16)
        gained = dot(picked, maps[...]) * gain[...]
        whitened = white[h * 256 : (h + 1) * 256, :]
        stream_grad = spread[h * 256 : (h + 1) * 256, :1] * (
            gained
            - jnp.mean(gained, axis=-1, keepdims=True)
            - whitened * jnp.mean(gained * whitened, axis=-1, keepdims=True)
        )
        for piece in split(stream_grad, 2):
            sums = sums + dot(hot_turned[h], piece)
    for n in range(TILES):
        table_part[n] = sums[(n // 2) * 8 : (n // 2 + 1) * 8, (n % 2) * 128 : (n % 2 + 1) * 128]

    def t_copy():
        return remote(table_part.at[pl.ds((1 - c) * 3, 3)], table_core, t_send.at[0], t_recv.at[0], other_core)

    def tp_copy(n):
        return remote(table_p.at[plane], table_p.at[plane], tp_send, tp_recv, plane_peer(n))

    def tz_copy(n):
        return remote(table_z.at[z], table_z.at[z], tz_send, tz_recv, device(y, n, xh, xl, c))

    def half(at_c):
        return table_all.at[pl.ds(at_c * 3, 3)]

    def t_last():
        return remote(table_half, half(c), t_send.at[1], t_recv.at[1], other_core)

    t_copy().start()
    wait(table_core, table_core, t_recv.at[0])
    table_p[plane] = table_part[pl.ds(c * 3, 3)] + table_core[...]
    start_all(16, tp_copy, plane)

    wait(weight_far, weight_far, wb_recv)
    weight_total[...] = total(weight_far, 8).astype(BF16)
    start_all(16, wc_copy, plane)
    local(weight_total, wc_slot(plane), wc_recv).start()

    wait(pair_in, pair_in, pair_recv)
    for at_z in range(8):
        run = [
            pair_in[at_x * 2 + at_z % 2].astype(F32)[:, (at_z // 2) * 8 : (at_z // 2 + 1) * 8, :] for at_x in range(2)
        ]
        pair_out[:, at_z * 16 : (at_z + 1) * 16, :] = jnp.concatenate(run, axis=1).astype(BF16)
    local(pair_out, pair_h, out_sem.at[0]).start()

    drain(tp_recv, gauge_t, 15)
    table_z[z] = total(table_p, 16)
    start_all(8, tz_copy, z)

    def lay_out(at_c):
        for n in range(16):
            first = at_c * 16 + n % 4 * 4 + n // 4
            weight_out[pl.ds(first, 32, stride=32), :] = weight_all[at_c, n * 32 : (n + 1) * 32, :].astype(F32)

    wait(weight_all.at[c], weight_all.at[c], wc_recv)
    wd_copy().start()

    sent(rm_send, gauge_m, 16, own_row)
    sent(cm_send, gauge_m, 16, own_column)
    sent(cot_send, gauge, 8, own_cot, 2)
    sent(l_send, gauge, 16, own_row)
    drain(r3_send, gauge, 8)
    drain(gx_send, gauge, 8)
    sent(gz_send, gauge, 8, own_gz, 2)
    sent(gl_send, gauge, 16, own_gl)
    drain(wa_send, gauge_w, 15)
    drain(wb_send, gauge_w, 7)
    sent(pair_send, gauge, 8, own_pair, 2)
    wh_copy().wait_send()
    t_copy().wait_send()

    @pl.when(active)
    def _():
        drain(r2_send, gauge, 14)
        gf_copy().wait_send()

    @pl.when(jnp.logical_not(active))
    def _():
        r1_copy().wait_send()

    wait(weight_all.at[1 - c], weight_all.at[1 - c], wh_recv.at[1])
    for at_c in range(2):
        lay_out(at_c)
    local(weight_out, weight_grad_h, out_sem.at[1]).start()
    drain(wc_send, gauge_w, 15)
    drain(tp_send, gauge_t, 15)
    wd_copy().wait_send()

    drain(tz_recv, gauge_t, 7)
    summed = total(table_z, 8)
    table_half[...] = summed
    t_last().start()
    table_all[pl.ds(c * 3, 3)] = summed
    drain(tz_send, gauge_t, 7)
    wait(table_half, half(1 - c), t_recv.at[1])
    for n in range(TILES):
        high = min(8, table_out.shape[0] - (n // 2) * 8)
        table_out[(n // 2) * 8 : (n // 2) * 8 + high, (n % 2) * 128 : (n % 2 + 1) * 128] = table_all[n][:high]
    t_last().wait_send()
    wait(pair_out, pair_h, out_sem.at[0])
    wait(weight_out, weight_grad_h, out_sem.at[1])


def shape(dims, dtype=BF16):
    return jax.ShapeDtypeStruct(dims, dtype)


def body(
    alignment_token_classes, deletions, alignment_mask, homolog_stack_values,
    letter_lookup_coefficients, gap_lookup_coefficients, standardize_gain, standardize_offset,
    first_factor_map, left_bias_vector, second_factor_map, right_bias_vector,
    output_weight_matrix, cotangent,
):
    kinds = letter_lookup_coefficients.shape[0]
    grades = np.arange(32, dtype=np.float32)
    steps = jnp.asarray(
        np.stack([(grades > 0).astype(np.float32), (2.0 / math.pi * np.arctan(grades / 3.0)).astype(np.float32)], 1)
    )
    inputs = [
        alignment_token_classes.T, deletions.T, alignment_mask.T, homolog_stack_values.reshape(512, 256),
        letter_lookup_coefficients, gap_lookup_coefficients, steps,
        standardize_gain.reshape(1, 256), standardize_offset.reshape(1, 256),
        first_factor_map.T, left_bias_vector.reshape(1, 32), second_factor_map.T, right_bias_vector.reshape(1, 32),
        output_weight_matrix,
    ]
    vmem = pltpu.VMEM
    scratch = [vmem(value.shape, value.dtype) for value in inputs] + [
        vmem((8, 16, 16, 128), BF16), vmem((4, 8, 32, 128), BF16),
        vmem((128, 128), F32), vmem((ROWS, 128), F32), vmem((8, 128), F32),
        vmem((2, 512, 128), F32),
        vmem((128, WIDE), F32), vmem((384, 256), BF16), vmem((8, 384), F32),
        vmem((1024, 128), F32), vmem((1024, 128), BF16), vmem((128, 1024), BF16),
        vmem((2, 32, 256), BF16),
        vmem((512, 256), F32), vmem((512, 128), F32),
        vmem((ROWS, WIDE), BF16), vmem((ROWS, WIDE), BF16),
        vmem((4, 4, 8, 128), F32), vmem((4, 4, 8, 128), F32),
        vmem((4, 8, 32, 128), BF16),
        vmem((4, ROWS, 1024), BF16), vmem((4, 4, ROWS, WIDE), BF16),
        vmem((256, 1024), BF16), vmem((1024, 256), F32), vmem((256, 1024), F32),
        vmem((1024, 256), BF16),
        vmem((1024, 128), F32), vmem((1024, 128), BF16),
        vmem((1024, 1024), BF16), vmem((1024, 1024), BF16),
        vmem((32, 32, 128), BF16), vmem((4, 8, 32, 128), BF16),
        vmem((4, 4, ROWS, WIDE), BF16), vmem((256, 512), F32), vmem((2, 4, ROWS, WIDE), BF16),
        vmem((4, 2, ROWS, WIDE), BF16), vmem((8, 2, ROWS, WIDE), BF16),
        vmem((ROWS, WIDE), BF16), vmem((ROWS, WIDE), BF16),
        vmem((4, ROWS, 1024), BF16), vmem((16, ROWS, WIDE), BF16),
        vmem((1024, 128), F32), vmem((512, 128), F32), vmem((512, 128), BF16),
        vmem((16, 32, 128), BF16), vmem((32, 128), BF16),
        vmem((8, 32, 128), BF16), vmem((32, 128), BF16), vmem((2, 512, 128), BF16),
        vmem((TILES, 8, 128), F32), vmem((3, 8, 128), F32),
        vmem((16, 3, 8, 128), F32), vmem((8, 3, 8, 128), F32),
        vmem((3, 8, 128), F32), vmem((TILES, 8, 128), F32),
        vmem((8, 128, 128), BF16), vmem((1024, 128), F32),
        vmem((16, ROWS, WIDE), BF16), vmem((16, 8, 128), F32),
        vmem((16, 32, 128), BF16), vmem((16, 3, 8, 128), F32),
    ]
    sizes = [
        len(inputs) + 1, 2, 0, 0, 0, 0, 0, 0, 0, 0, 0, 0, 0, 0, 0, 0, 0, 0, 0, 0, 0, 0, 0, 0, 0, 0, 2, 2, 0,
        0, 0, 0, 0, 0, 2, 2, 0, 0, 0, 0,
    ]
    results = pl.pallas_call(
        kernel,
        out_shape=[shape((8, 128, 128)), shape((1024, 128), F32), shape((kinds, 256), F32)],
        in_specs=[pl.BlockSpec(memory_space=pl.ANY)] * (len(inputs) + 1),
        out_specs=[pl.BlockSpec(memory_space=pl.ANY)] * 2 + [pl.BlockSpec(memory_space=pltpu.VMEM)],
        scratch_shapes=scratch + [pltpu.SemaphoreType.DMA((size,)) if size else pltpu.SemaphoreType.DMA for size in sizes],
        compiler_params=pltpu.CompilerParams(
            collective_id=0, has_side_effects=True, vmem_limit_bytes=60 * 1024 * 1024
        ),
        name="outer_product_mean",
    )(*inputs, cotangent.reshape(8, 16, 2, 16, 128))
    return pl.pallas_call(
        hand_over,
        out_shape=[shape(value.shape, value.dtype) for value in results],
        in_specs=[pl.BlockSpec(memory_space=pl.ANY)] * 3,
        out_specs=[pl.BlockSpec(memory_space=pl.ANY)] * 3,
        scratch_shapes=[vmem(value.shape, value.dtype) for value in results] + [pltpu.SemaphoreType.DMA((3,))],
        name="hand_over",
    )(*results)


def hand_over(pair, weight, table, pair_out, weight_out, table_out, pair_here, weight_here, table_here, sem):
    here = [pair_here, weight_here, table_here]
    arrive = [local(src, dst, sem.at[n]) for n, (src, dst) in enumerate(zip([pair, weight, table], here))]
    leave = [local(src, dst, sem.at[n]) for n, (src, dst) in enumerate(zip(here, [pair_out, weight_out, table_out]))]
    for copy in arrive:
        copy.start()
    for first, second in zip(arrive, leave):
        first.wait()
        second.start()
    for copy in leave:
        copy.wait()


def solution(mesh):
    in_specs = (
        P("seq", "res"), P("seq", "res"), P("seq", "res"), P("seq", "res", None),
        P(), P(), P(), P(), P(), P(), P(), P(), P(),
        P("res", None, None),
    )
    out_specs = (P("res", "seq", None), P(), P())
    return jax.shard_map(body, mesh=mesh, in_specs=in_specs, out_specs=out_specs, check_vma=False)
```

```python
import math

import jax
import jax.numpy as jnp
import numpy as np
from jax import lax
from jax.experimental import pallas as pl
from jax.experimental.pallas import tpu as pltpu
from jax.sharding import PartitionSpec as P

EPSILON = 1e-05
MESH = pl.DeviceIdType.MESH
F32 = jnp.float32
BF16 = jnp.bfloat16

ROWS = 64
WIDE = 256
TILES = 6


def device(y, z, xh, xl, c):
    return (y * 16 + z * 2 + xh, xl * 2 + c)


def repeat(count, step):
    lax.fori_loop(0, count, lambda n, carried: (step(n), carried)[1], 0)


def remote(src, dst, send, recv, target):
    return pltpu.make_async_remote_copy(
        src_ref=src, dst_ref=dst, send_sem=send, recv_sem=recv, device_id=target, device_id_type=MESH
    )


def start_all(count, copy, own):
    for n in range(count):

        @pl.when(own != n)
        def _(n=n):
            copy(n).start()


def local(src, dst, sem):
    return pltpu.make_async_copy(src, dst, sem)


def drain(sem, gauge, count):
    part = gauge.at[pl.ds(0, count)]
    local(part, part, sem).wait()


def sent(sem, gauge, count, own, unit=1):
    @pl.when(own >= 0)
    def _():
        drain(sem, gauge, count - unit)

    @pl.when(own < 0)
    def _():
        drain(sem, gauge, count)


def lanes(dims):
    return lax.broadcasted_iota(jnp.int32, dims, len(dims) - 1)


def block(n, size):
    return pl.ds(pl.multiple_of(n * size, size), size)


def swap(parts, stride):
    lane = lanes(parts[0].shape)
    low = lax.rem(lax.div(lane, stride), 2) == 0
    high = lax.rem(lax.div(lane, 2 * stride), 2) == 0

    def pair(first, second, step, keep):
        return (
            jnp.where(keep, first, pltpu.roll(second, step, 1)),
            jnp.where(keep, pltpu.roll(first, 128 - step, 1), second),
        )

    a, b = pair(parts[0], parts[1], stride, low)
    c, d = pair(parts[2], parts[3], stride, low)
    a, c = pair(a, c, 2 * stride, high)
    b, d = pair(b, d, 2 * stride, high)
    return [a, b, c, d]


def dot(first, second):
    return jnp.dot(first, second, preferred_element_type=F32)


def dot_nt(first, second):
    return lax.dot_general(first, second, (((1,), (1,)), ((), ())), preferred_element_type=F32)


def split(value, count):
    pieces = []
    for _ in range(count):
        piece = value.astype(BF16)
        pieces.append(piece)
        value = value - piece.astype(F32)
    return pieces


def total(ref, count):
    value = ref[0].astype(F32)
    for n in range(1, count):
        value = value + ref[n].astype(F32)
    return value


def kernel(
    token_h, deletion_h, mask_h, stack_h, letters_h, gaps_h, steps_h, gain_h, offset_h,
    left_map_h, left_bias_h, right_map_h, right_bias_h, weight_h, cotangent,
    pair_h, weight_grad_h, table_out,
    token, deletion, mask, stack_raw, letters, gaps, steps, gain, offset,
    left_map, left_bias, right_map, right_bias, weight_raw, cot_raw, cot_stage,
    square, turned, mask_rows, stack, table, maps, bias, weight_wide, weight, weight_turned, hot_turned,
    white, spread, left_own, right_own, row_masks, column_masks, cot_all, left_all, right_all,
    right_mat, wide_grad, wide_outer, product, counts, scaled, folded, grad_outer, pair, pair_in,
    right_grad, right_part, right_core, right_sum, right_in, right_last, right_send, left_grad, left_in,
    weight_grad, weight_core, weight_half, weight_in, weight_sum, weight_far, weight_total, weight_all,
    table_part, table_core, table_p, table_z, table_half, table_all, pair_out, weight_out,
    gauge, gauge_m, gauge_w, gauge_t,
    in_sem, out_sem, rm_send, rm_recv, cm_send, cm_recv, cot_send, cot_recv,
    r1_send, r1_recv, r2_send, r2_recv, r3_send, r3_recv, l_send, l_recv,
    gx_send, gx_recv, gz_send, gz_recv, gf_send, gf_recv, gl_send, gl_recv, pair_send, pair_recv,
    wh_send, wh_recv, wa_send, wa_recv, wb_send, wb_recv, wc_send, wc_recv,
    t_send, t_recv, tp_send, tp_recv, tz_send, tz_recv,
):
    res = lax.axis_index("res")
    q = lax.axis_index("seq")
    y, z, xh = lax.div(res, 16), lax.rem(lax.div(res, 2), 8), lax.rem(res, 2)
    xl, c = lax.div(q, 2), lax.rem(q, 2)
    zi, parity = lax.div(z, 2), lax.rem(z, 2)
    active = parity == xl
    inside = lax.div(y, 2) == c
    other_q = (1 - xl) * 2 + c
    plane = y * 4 + xh * 2 + xl
    band = lax.rem(y, 2) * 2 + xh
    own_column = jnp.where(active, z * 2 + c, -1)
    own_row = jnp.where(inside, plane, -1)
    other_core = device(y, z, xh, xl, 1 - c)
    partner = device(y, z, xh, 1 - xl, c)

    def wait(src, dst, sem):
        local(src, dst, sem).wait()

    loads = [
        local(src, dst, in_sem.at[n])
        for n, (src, dst) in enumerate(
            [
                (token_h, token), (deletion_h, deletion), (mask_h, mask), (stack_h, stack_raw),
                (letters_h, letters), (gaps_h, gaps), (steps_h, steps), (gain_h, gain), (offset_h, offset),
                (left_map_h, left_map), (left_bias_h, left_bias), (right_map_h, right_map),
                (right_bias_h, right_bias), (weight_h, weight_raw), (cotangent.at[:, :, xl], cot_raw),
            ]
        )
    ]
    for load in loads:
        load.start()

    barrier = pltpu.get_barrier_semaphore()

    def signal(target):
        pl.semaphore_signal(barrier, inc=1, device_id=target, device_id_type=MESH)

    def greet(n):
        @pl.when(n != z * 4 + q)
        def _():
            signal((y * 16 + lax.div(n, 4) * 2 + xh, lax.rem(n, 4)))

        @pl.when(n != (y * 2 + xh) * 4 + q)
        def _():
            signal((lax.div(n, 8) * 16 + z * 2 + lax.rem(lax.div(n, 4), 2), lax.rem(n, 4)))

    for n in range(32):
        greet(n)

    def line_user(n):
        return device(y, lax.div(n, 2), xh, parity, lax.rem(n, 2))

    def plane_user(n):
        return device(lax.div(n, 4), z, lax.div(lax.rem(n, 4), 2), lax.rem(n, 2), lax.div(y, 2))

    def rm_copy(n):
        return remote(mask_rows, row_masks.at[band, q], rm_send, rm_recv, plane_user(n))

    def cm_copy(n):
        return remote(mask_rows, column_masks.at[zi, q], cm_send, cm_recv, line_user(n))

    def cot_copy(n):
        return remote(cot_stage.at[n], cot_all.at[band], cot_send, cot_recv, device(n, z, c, xl, lax.div(y, 2)))

    own_cot = jnp.where(jnp.logical_and(inside, xh == c), y, -1)

    def left_slot(at_band, at_q):
        return left_all.at[at_q, :, block(at_band, WIDE)]

    def l_copy(n):
        return remote(left_own, left_slot(band, q), l_send, l_recv, plane_user(n))

    def r1_copy():
        return remote(right_own, right_all.at[zi, q], r1_send, r1_recv, partner)

    def r2_copy(n):
        return remote(
            right_own, right_all.at[zi, q], r2_send, r2_recv, device(y, n, xh, xl, c)
        )

    def r2_forward(n):
        return remote(
            right_all.at[zi, other_q], right_all.at[zi, other_q], r2_send, r2_recv,
            device(y, n, xh, xl, c),
        )

    def r3_copy(n):
        at_q = n * 2 + c
        return remote(right_all.at[:, at_q], right_all.at[:, at_q], r3_send, r3_recv, other_core)

    for load in loads[:13]:
        load.wait()
    mask_value = mask[...].astype(F32)
    empty = jnp.zeros((8, ROWS), F32)
    mask_rows[...] = jnp.where(
        c == 0, jnp.concatenate([mask_value, empty], axis=1), jnp.concatenate([empty, mask_value], axis=1)
    )
    square[...] = jnp.zeros((128, 128), F32)
    square[0:8, 0:ROWS] = token[...].astype(F32)
    square[8:16, 0:ROWS] = deletion[...].astype(F32)
    square[16:24, 0:ROWS] = mask_value
    turned[...] = square[...].T[:ROWS]
    for n in range(2):
        stack[n] = stack_raw[:, n * 128 : (n + 1) * 128].astype(F32)
    table[...] = jnp.zeros((128, WIDE), F32)
    table[: letters.shape[0], :] = letters[...]
    table[32:64, :] = steps[:, 0:1] * gaps[0:1, :] + steps[:, 1:2] * gaps[1:2, :]
    spread_left = (
        lax.rem(lax.broadcasted_iota(jnp.int32, (128, 32), 0), 32) == lanes((128, 32))
    ).astype(F32).astype(BF16)
    spread_right = (
        lax.div(lax.broadcasted_iota(jnp.int32, (WIDE, 32), 0), 8) == lanes((WIDE, 32))
    ).astype(F32).astype(BF16)
    maps[:128, :] = dot(spread_left, left_map[...]).astype(BF16)
    maps[128:, :] = dot(spread_right, right_map[...]).astype(BF16)
    bias[...] = jnp.concatenate(
        [
            sum(dot_nt(piece, spread_left) for piece in split(jnp.broadcast_to(left_bias[...], (8, 32)), 3)),
            sum(dot_nt(piece, spread_right) for piece in split(jnp.broadcast_to(right_bias[...], (8, 32)), 3)),
        ],
        axis=1,
    )
    loads[14].wait()
    for n in range(4):
        strip = cot_raw[:, n * 4 : n * 4 + 4].astype(F32)
        strip = jnp.where(c == 0, strip[:, :, :8, :], strip[:, :, 8:, :])
        cot_stage[n] = strip.reshape(8, 32, 128).astype(BF16)
    lane = lanes((ROWS, 128))
    fine = lane.astype(F32)
    wide_lane = lanes((ROWS, WIDE))
    pieces = split(table[...], 3)
    right_value = jnp.zeros((ROWS, WIDE), F32)
    for h in range(2):
        hot = jnp.concatenate(
            [
                jnp.logical_or(fine == turned[:, i : i + 1], fine == turned[:, 8 + i : 9 + i] + 32.0).astype(F32)
                for i in range(h * 4, h * 4 + 4)
            ],
            axis=0,
        )
        hot_turned[h] = hot.T[:32].astype(BF16)
        hot = hot.astype(BF16)
        hidden = jnp.concatenate(
            [
                jnp.concatenate([stack[n, pl.ds(i, ROWS, stride=8), :] for i in range(h * 4, h * 4 + 4)], axis=0)
                for n in range(2)
            ],
            axis=1,
        ) + (dot(hot, pieces[0]) + dot(hot, pieces[1]) + dot(hot, pieces[2]))
        centered = hidden - jnp.mean(hidden, axis=-1, keepdims=True)
        variance = jnp.mean(centered * centered, axis=-1, keepdims=True)
        scale = lax.rsqrt(variance + EPSILON)
        whitened = centered * scale
        white[h * 256 : (h + 1) * 256, :] = whitened
        spread[h * 256 : (h + 1) * 256, :] = jnp.broadcast_to(scale, (256, 128))
        normed = (whitened * gain[...] + offset[...]).astype(BF16)
        rows = dot_nt(normed, maps[...]) + bias[:1, :]
        left_value = jnp.zeros((ROWS, 128), F32)
        for i in range(4):
            part = turned[:, 16 + h * 4 + i : 17 + h * 4 + i] * rows[i * ROWS : (i + 1) * ROWS, :]
            left_value = jnp.where(lax.div(lane, 32) == i, part[:, :128], left_value)
            right_value = jnp.where(lax.rem(wide_lane, 8) == h * 4 + i, part[:, 128:], right_value)
        left_own[:, h * 128 : (h + 1) * 128] = left_value.astype(BF16)
    right_own[...] = right_value.astype(BF16)
    pl.semaphore_wait(barrier, 62)
    @pl.when(jnp.logical_not(active))
    def _():
        r1_copy().start()

    start_all(16, rm_copy, own_row)
    start_all(16, cm_copy, own_column)

    @pl.when(inside)
    def _():
        local(mask_rows, row_masks.at[band, q], rm_recv).start()

    @pl.when(active)
    def _():
        local(mask_rows, column_masks.at[zi, q], cm_recv).start()

    start_all(4, cot_copy, own_cot)

    @pl.when(jnp.logical_and(inside, xh == c))
    def _():
        local(cot_stage.at[y], cot_all.at[band], cot_recv).start()

    start_all(16, l_copy, own_row)

    @pl.when(inside)
    def _():
        local(left_own, left_slot(band, q), l_recv).start()

    @pl.when(active)
    def _():
        start_all(8, r2_copy, z)
        local(right_own, right_all.at[zi, q], r2_recv).start()

    @pl.when(active)
    def _():
        wait(right_own, right_all.at[zi, other_q], r1_recv)
        start_all(8, r2_forward, z)

    loads[13].wait()
    weight_wide[...] = weight_raw[...].astype(F32)
    for t in range(2):
        for b in range(4):
            for a in range(4):
                at = ((t * 4 + b) * 4 + a) * 32
                weight[at : at + 32, :] = weight_wide[pl.ds(t * 16 + a * 4 + b, 32, stride=32), :].astype(BF16)
    for t in range(8):
        weight_turned[:, t * 128 : (t + 1) * 128] = weight[t * 128 : (t + 1) * 128, :].astype(F32).T.astype(BF16)

    wait(row_masks, row_masks, rm_recv)
    wait(column_masks, column_masks, cm_recv)
    column_mask = jnp.concatenate(
        [
            jnp.concatenate([column_masks[b, 2 * h] + column_masks[b, 2 * h + 1] for h in range(2)], axis=1)
            for b in range(4)
        ],
        axis=0,
    )
    for i in range(32):
        row = jnp.concatenate(
            [
                row_masks[i // 8, 2 * h, i % 8 : i % 8 + 1, :] + row_masks[i // 8, 2 * h + 1, i % 8 : i % 8 + 1, :]
                for h in range(2)
            ],
            axis=1,
        )
        product[i * 32 : (i + 1) * 32, :] = (row * column_mask).astype(BF16)
    counts[...] = dot(product[...], jnp.ones((256, 128), BF16))
    wait(cot_all, cot_all, cot_recv)
    for n in range(4):
        cot = cot_all[n].astype(F32).reshape(256, 128)
        scaled[n * 256 : (n + 1) * 256, :] = (cot / counts[n * 256 : (n + 1) * 256, :]).astype(BF16)

    def backward(g):
        span = block(g, 256)
        wide_grad[...] = dot_nt(weight[...], scaled[span, :])
        for t in range(8):
            for half in range(2):
                lane_part = wide_grad[t * 128 : (t + 1) * 128, half * 128 : (half + 1) * 128].astype(BF16)
                parts = swap([lane_part[a * 32 : (a + 1) * 32, :] for a in range(4)], 32)
                for i, part in enumerate(parts):
                    at = pl.ds(pl.multiple_of(g * 256 + half * 128 + i * 32, 32), 32)
                    grad_outer[at, t * 128 : (t + 1) * 128] = part.astype(BF16)

    repeat(4, backward)

    def right_step(t):
        for at_q in range(4):
            rows = slice(at_q * ROWS, (at_q + 1) * ROWS)
            parts = swap([right_part[rows, (t * 4 + b) * 128 : (t * 4 + b + 1) * 128] for b in range(4)], 8)
            for b, part in enumerate(parts):
                right_grad[b, at_q, :, t * 128 : (t + 1) * 128] = part.astype(BF16)

    def gx_copy(n):
        return remote(right_grad.at[:, n * 2 + 1 - c], right_core.at[n], gx_send, gx_recv, other_core)

    wait(left_all, left_all, l_recv)
    right_part[...] = dot(left_all[...].reshape(256, 1024), grad_outer[...])
    right_step(0)
    right_step(1)
    start_all(2, gx_copy, -1)

    @pl.when(active)
    def _():
        drain(r2_recv, gauge, 7)

    @pl.when(jnp.logical_not(active))
    def _():
        drain(r2_recv, gauge, 8)

    start_all(2, r3_copy, -1)
    def gz_copy(n):
        return remote(
            right_sum.at[n], right_in.at[z], gz_send, gz_recv, device(y, n * 2 + xl, xh, xl, c)
        )

    own_gz = jnp.where(active, zi, -1)
    wait(right_core, right_core, gx_recv)
    for n in range(2):
        for b in range(4):
            right_sum[b, n] = (right_grad[b, n * 2 + c].astype(F32) + right_core[n, b].astype(F32)).astype(BF16)
    start_all(4, gz_copy, own_gz)

    @pl.when(active)
    def _():
        local(right_sum.at[zi], right_in.at[z], gz_recv).start()

    drain(r3_recv, gauge, 8)
    for at_q in range(4):
        rows = slice(at_q * ROWS, (at_q + 1) * ROWS)
        for t in range(2):
            parts = [right_all[b, at_q, :, t * 128 : (t + 1) * 128].astype(F32) for b in range(4)]
            for b, part in enumerate(swap(parts, 8)):
                right_mat[rows, (t * 4 + b) * 128 : (t * 4 + b + 1) * 128] = part.astype(BF16)


    def gl_part(n):
        return left_grad.at[lax.rem(n, 4), :, block(lax.div(n, 4), WIDE)]

    def gl_copy(n):
        target = device(c * 2 + lax.div(n, 8), z, lax.rem(lax.div(n, 4), 2), lax.div(lax.rem(n, 4), 2), lax.rem(n, 2))
        return remote(gl_part(n), left_in.at[plane], gl_send, gl_recv, target)

    own_gl = jnp.where(inside, band * 4 + q, -1)

    def left_step(g):
        span = block(g, 256)
        part = dot_nt(right_mat[...], grad_outer[span, :]).astype(BF16)
        for at_q in range(4):
            left_grad[at_q, :, span] = part[at_q * ROWS : (at_q + 1) * ROWS, :]

    for g in range(4):
        left_step(g)

        def start_left(n):
            @pl.when(n + g * 4 != own_gl)
            def _():
                gl_copy(n + g * 4).start()

        repeat(4, start_left)

    @pl.when(inside)
    def _():
        local(gl_part(band * 4 + q), left_in.at[plane], gl_recv).start()

    def forward(g):
        lead = left_all[:, :, block(g, 256)].reshape(256, 256).astype(F32).T.astype(BF16)
        wide_outer[...] = dot(lead, right_mat[...])
        for half in range(2):
            span = pl.ds(pl.multiple_of(g * 256 + half * 128, 128), 128)
            for t in range(8):
                tile = wide_outer[half * 128 : (half + 1) * 128, t * 128 : (t + 1) * 128].astype(BF16)
                parts = swap([tile[i * 32 : (i + 1) * 32, :] for i in range(4)], 32)
                for a, part in enumerate(parts):
                    folded[(t * 4 + a) * 32 : (t * 4 + a + 1) * 32, span] = part.astype(BF16)

    def project(g):
        span = block(g, 256)
        value = dot(weight_turned[...], folded[:, span])
        update = (value.T / counts[span, :]).astype(BF16)
        pair[block(g, 8)] = update.reshape(8, 32, 128)

    repeat(4, forward)
    weight_grad[...] = dot(folded[...], scaled[...])

    def plane_peer(n):
        return device(lax.div(n, 4), z, lax.div(lax.rem(n, 4), 2), lax.rem(n, 2), c)

    def line_peer(n):
        return device(y, n, xh, xl, c)

    def wh_copy():
        return remote(weight_grad.at[block(1 - c, 512), :], weight_core, wh_send.at[0], wh_recv.at[0], other_core)

    def wa_part(n):
        return weight_half.at[block(n, 32), :]

    def wa_copy(n):
        return remote(wa_part(n), weight_in.at[plane], wa_send, wa_recv, plane_peer(n))

    def wb_copy(n):
        return remote(weight_sum, weight_far.at[z], wb_send, wb_recv, line_peer(n))

    def wc_slot(n):
        return weight_all.at[c, block(n, 32), :]

    def wc_copy(n):
        return remote(weight_total, wc_slot(plane), wc_send, wc_recv, plane_peer(n))

    def wd_copy():
        return remote(weight_all.at[c], weight_all.at[c], wh_send.at[1], wh_recv.at[1], other_core)

    wh_copy().start()
    repeat(4, project)
    wait(weight_core, weight_core, wh_recv.at[0])
    weight_half[...] = (weight_grad[block(c, 512), :] + weight_core[...]).astype(BF16)
    start_all(16, wa_copy, plane)
    local(wa_part(plane), weight_in.at[plane], wa_recv).start()

    def pair_part(n):
        return pair.at[block(n, 8)]

    def pair_copy(n):
        target = device(c * 2 + lax.div(n, 2), z, lax.rem(n, 2), lax.div(y, 2), lax.rem(y, 2))
        return remote(pair_part(n), pair_in.at[xh * 2 + xl], pair_send, pair_recv, target)

    keeps_pair = jnp.logical_and(inside, q == y)
    own_pair = jnp.where(keeps_pair, band, -1)
    start_all(4, pair_copy, own_pair)

    @pl.when(keeps_pair)
    def _():
        local(pair_part(band), pair_in.at[xh * 2 + xl], pair_recv).start()

    def gf_copy():
        return remote(right_send, right_last, gf_send, gf_recv, partner)

    @pl.when(active)
    def _():
        wait(right_in, right_in, gz_recv)
        away = right_in[0, 1 - xl].astype(F32)
        for n in range(1, 8):
            away = away + right_in[n, 1 - xl].astype(F32)
        right_send[...] = away.astype(BF16)
        gf_copy().start()
        here = right_in[0, xl].astype(F32)
        for n in range(1, 8):
            here = here + right_in[n, xl].astype(F32)
        right_last[...] = here.astype(BF16)

    wait(left_in, left_in, gl_recv)
    left_total = total(left_in, 16).astype(BF16).astype(F32)

    @pl.when(jnp.logical_not(active))
    def _():
        wait(right_last, right_last, gf_recv)

    right_total = right_last[...].astype(F32)

    wait(weight_in, weight_in, wa_recv)
    weight_sum[...] = total(weight_in, 16).astype(BF16)
    start_all(8, wb_copy, z)
    local(weight_sum, weight_far.at[z], wb_recv).start()

    sums = jnp.zeros((32, WIDE), F32)
    for h in range(2):
        picked = []
        for i in range(4):
            keep = turned[:, 16 + h * 4 + i : 17 + h * 4 + i]
            tile = left_total[:, h * 128 : (h + 1) * 128]
            picked.append(
                jnp.concatenate(
                    [
                        jnp.where(lax.div(lane, 32) == i, tile, 0.0) * keep,
                        jnp.where(lax.rem(wide_lane, 8) == h * 4 + i, right_total, 0.0) * keep,
                    ],
                    axis=1,
                )
            )
        picked = jnp.concatenate(picked, axis=0).astype(BF16)
        gained = dot(picked, maps[...]) * gain[...]
        whitened = white[h * 256 : (h + 1) * 256, :]
        stream_grad = spread[h * 256 : (h + 1) * 256, :1] * (
            gained
            - jnp.mean(gained, axis=-1, keepdims=True)
            - whitened * jnp.mean(gained * whitened, axis=-1, keepdims=True)
        )
        for piece in split(stream_grad, 2):
            sums = sums + dot(hot_turned[h], piece)
    for n in range(TILES):
        table_part[n] = sums[(n // 2) * 8 : (n // 2 + 1) * 8, (n % 2) * 128 : (n % 2 + 1) * 128]

    def t_copy():
        return remote(table_part.at[pl.ds((1 - c) * 3, 3)], table_core, t_send.at[0], t_recv.at[0], other_core)

    def tp_copy(n):
        return remote(table_p.at[plane], table_p.at[plane], tp_send, tp_recv, plane_peer(n))

    def tz_copy(n):
        return remote(table_z.at[z], table_z.at[z], tz_send, tz_recv, device(y, n, xh, xl, c))

    def half(at_c):
        return table_all.at[pl.ds(at_c * 3, 3)]

    def t_last():
        return remote(table_half, half(c), t_send.at[1], t_recv.at[1], other_core)

    t_copy().start()
    wait(table_core, table_core, t_recv.at[0])
    table_p[plane] = table_part[pl.ds(c * 3, 3)] + table_core[...]
    start_all(16, tp_copy, plane)

    wait(weight_far, weight_far, wb_recv)
    weight_total[...] = total(weight_far, 8).astype(BF16)
    start_all(16, wc_copy, plane)
    local(weight_total, wc_slot(plane), wc_recv).start()

    wait(pair_in, pair_in, pair_recv)
    for at_z in range(8):
        run = [
            pair_in[at_x * 2 + at_z % 2].astype(F32)[:, (at_z // 2) * 8 : (at_z // 2 + 1) * 8, :] for at_x in range(2)
        ]
        pair_out[:, at_z * 16 : (at_z + 1) * 16, :] = jnp.concatenate(run, axis=1).astype(BF16)
    local(pair_out, pair_h, out_sem.at[0]).start()

    drain(tp_recv, gauge_t, 15)
    table_z[z] = total(table_p, 16)
    start_all(8, tz_copy, z)

    def lay_out(at_c):
        for n in range(16):
            first = at_c * 16 + n % 4 * 4 + n // 4
            weight_out[pl.ds(first, 32, stride=32), :] = weight_all[at_c, n * 32 : (n + 1) * 32, :].astype(F32)

    wait(weight_all.at[c], weight_all.at[c], wc_recv)
    wd_copy().start()

    sent(rm_send, gauge_m, 16, own_row)
    sent(cm_send, gauge_m, 16, own_column)
    sent(cot_send, gauge, 8, own_cot, 2)
    sent(l_send, gauge, 16, own_row)
    drain(r3_send, gauge, 8)
    drain(gx_send, gauge, 8)
    sent(gz_send, gauge, 8, own_gz, 2)
    sent(gl_send, gauge, 16, own_gl)
    drain(wa_send, gauge_w, 15)
    drain(wb_send, gauge_w, 7)
    sent(pair_send, gauge, 8, own_pair, 2)
    wh_copy().wait_send()
    t_copy().wait_send()

    @pl.when(active)
    def _():
        drain(r2_send, gauge, 14)
        gf_copy().wait_send()

    @pl.when(jnp.logical_not(active))
    def _():
        r1_copy().wait_send()

    wait(weight_all.at[1 - c], weight_all.at[1 - c], wh_recv.at[1])
    for at_c in range(2):
        lay_out(at_c)
    local(weight_out, weight_grad_h, out_sem.at[1]).start()
    drain(wc_send, gauge_w, 15)
    drain(tp_send, gauge_t, 15)
    wd_copy().wait_send()

    drain(tz_recv, gauge_t, 7)
    summed = total(table_z, 8)
    table_half[...] = summed
    t_last().start()
    table_all[pl.ds(c * 3, 3)] = summed
    drain(tz_send, gauge_t, 7)
    wait(table_half, half(1 - c), t_recv.at[1])
    for n in range(TILES):
        high = min(8, table_out.shape[0] - (n // 2) * 8)
        table_out[(n // 2) * 8 : (n // 2) * 8 + high, (n % 2) * 128 : (n % 2 + 1) * 128] = table_all[n][:high]
    t_last().wait_send()
    wait(pair_out, pair_h, out_sem.at[0])
    wait(weight_out, weight_grad_h, out_sem.at[1])


def shape(dims, dtype=BF16):
    return jax.ShapeDtypeStruct(dims, dtype)


def body(
    alignment_token_classes, deletions, alignment_mask, homolog_stack_values,
    letter_lookup_coefficients, gap_lookup_coefficients, standardize_gain, standardize_offset,
    first_factor_map, left_bias_vector, second_factor_map, right_bias_vector,
    output_weight_matrix, cotangent,
):
    kinds = letter_lookup_coefficients.shape[0]
    grades = np.arange(32, dtype=np.float32)
    steps = jnp.asarray(
        np.stack([(grades > 0).astype(np.float32), (2.0 / math.pi * np.arctan(grades / 3.0)).astype(np.float32)], 1)
    )
    inputs = [
        alignment_token_classes.T, deletions.T, alignment_mask.T, homolog_stack_values.reshape(512, 256),
        letter_lookup_coefficients, gap_lookup_coefficients, steps,
        standardize_gain.reshape(1, 256), standardize_offset.reshape(1, 256),
        first_factor_map.T, left_bias_vector.reshape(1, 32), second_factor_map.T, right_bias_vector.reshape(1, 32),
        output_weight_matrix,
    ]
    vmem = pltpu.VMEM
    scratch = [vmem(value.shape, value.dtype) for value in inputs] + [
        vmem((8, 16, 16, 128), BF16), vmem((4, 8, 32, 128), BF16),
        vmem((128, 128), F32), vmem((ROWS, 128), F32), vmem((8, 128), F32),
        vmem((2, 512, 128), F32),
        vmem((128, WIDE), F32), vmem((384, 256), BF16), vmem((8, 384), F32),
        vmem((1024, 128), F32), vmem((1024, 128), BF16), vmem((128, 1024), BF16),
        vmem((2, 32, 256), BF16),
        vmem((512, 256), F32), vmem((512, 128), F32),
        vmem((ROWS, WIDE), BF16), vmem((ROWS, WIDE), BF16),
        vmem((4, 4, 8, 128), F32), vmem((4, 4, 8, 128), F32),
        vmem((4, 8, 32, 128), BF16),
        vmem((4, ROWS, 1024), BF16), vmem((4, 4, ROWS, WIDE), BF16),
        vmem((256, 1024), BF16), vmem((1024, 256), F32), vmem((256, 1024), F32),
        vmem((1024, 256), BF16),
        vmem((1024, 128), F32), vmem((1024, 128), BF16),
        vmem((1024, 1024), BF16), vmem((1024, 1024), BF16),
        vmem((32, 32, 128), BF16), vmem((4, 8, 32, 128), BF16),
        vmem((4, 4, ROWS, WIDE), BF16), vmem((256, 1024), F32), vmem((2, 4, ROWS, WIDE), BF16),
        vmem((4, 2, ROWS, WIDE), BF16), vmem((8, 2, ROWS, WIDE), BF16),
        vmem((ROWS, WIDE), BF16), vmem((ROWS, WIDE), BF16),
        vmem((4, ROWS, 1024), BF16), vmem((16, ROWS, WIDE), BF16),
        vmem((1024, 128), F32), vmem((512, 128), F32), vmem((512, 128), BF16),
        vmem((16, 32, 128), BF16), vmem((32, 128), BF16),
        vmem((8, 32, 128), BF16), vmem((32, 128), BF16), vmem((2, 512, 128), BF16),
        vmem((TILES, 8, 128), F32), vmem((3, 8, 128), F32),
        vmem((16, 3, 8, 128), F32), vmem((8, 3, 8, 128), F32),
        vmem((3, 8, 128), F32), vmem((TILES, 8, 128), F32),
        vmem((8, 128, 128), BF16), vmem((1024, 128), F32),
        vmem((16, ROWS, WIDE), BF16), vmem((16, 8, 128), F32),
        vmem((16, 32, 128), BF16), vmem((16, 3, 8, 128), F32),
    ]
    sizes = [
        len(inputs) + 1, 2, 0, 0, 0, 0, 0, 0, 0, 0, 0, 0, 0, 0, 0, 0, 0, 0, 0, 0, 0, 0, 0, 0, 0, 0, 2, 2, 0,
        0, 0, 0, 0, 0, 2, 2, 0, 0, 0, 0,
    ]
    results = pl.pallas_call(
        kernel,
        out_shape=[shape((8, 128, 128)), shape((1024, 128), F32), shape((kinds, 256), F32)],
        in_specs=[pl.BlockSpec(memory_space=pl.ANY)] * (len(inputs) + 1),
        out_specs=[pl.BlockSpec(memory_space=pl.ANY)] * 2 + [pl.BlockSpec(memory_space=pltpu.VMEM)],
        scratch_shapes=scratch + [pltpu.SemaphoreType.DMA((size,)) if size else pltpu.SemaphoreType.DMA for size in sizes],
        compiler_params=pltpu.CompilerParams(
            collective_id=0, has_side_effects=True, vmem_limit_bytes=60 * 1024 * 1024
        ),
        name="outer_product_mean",
    )(*inputs, cotangent.reshape(8, 16, 2, 16, 128))
    return pl.pallas_call(
        hand_over,
        out_shape=[shape(value.shape, value.dtype) for value in results],
        in_specs=[pl.BlockSpec(memory_space=pl.ANY)] * 3,
        out_specs=[pl.BlockSpec(memory_space=pl.ANY)] * 3,
        scratch_shapes=[vmem(value.shape, value.dtype) for value in results] + [pltpu.SemaphoreType.DMA((3,))],
        name="hand_over",
    )(*results)


def hand_over(pair, weight, table, pair_out, weight_out, table_out, pair_here, weight_here, table_here, sem):
    here = [pair_here, weight_here, table_here]
    arrive = [local(src, dst, sem.at[n]) for n, (src, dst) in enumerate(zip([pair, weight, table], here))]
    leave = [local(src, dst, sem.at[n]) for n, (src, dst) in enumerate(zip(here, [pair_out, weight_out, table_out]))]
    for copy in arrive:
        copy.start()
    for first, second in zip(arrive, leave):
        first.wait()
        second.start()
    for copy in leave:
        copy.wait()


def solution(mesh):
    in_specs = (
        P("seq", "res"), P("seq", "res"), P("seq", "res"), P("seq", "res", None),
        P(), P(), P(), P(), P(), P(), P(), P(), P(),
        P("res", None, None),
    )
    out_specs = (P("res", "seq", None), P(), P())
    return jax.shard_map(body, mesh=mesh, in_specs=in_specs, out_specs=out_specs, check_vma=False)
```
